32 devices in a mesh: dp: 8 (over z, y), mp: 4 (over x, core).
Axes of the slice: x: 2, y: 2, z: 4, core: 2. Of those that a mesh axis runs over, the one named last changes fastest.
Arguments:
- hidden: bfloat16 [128, 5120], P('dp', 'mp'), may hold values from -6 to 6
- w_query: bfloat16 [5120, 8192], P(None, 'mp'), may hold values from -0.078125 to 0.078125
- w_key: bfloat16 [5120, 1024], P(None, 'mp'), may hold values from -0.078125 to 0.078125
- w_value: bfloat16 [5120, 1024], P(None, 'mp'), may hold values from -0.078125 to 0.078125
- query_gain: float32 [128], replicated, may hold values from 0.5 to 3
- key_gain: float32 [128], replicated, may hold values from 0.5 to 3
- kv_pool: bfloat16 [6144, 16, 8, 256], P('dp', None, 'mp')
- page_table: int32 [128, 48], replicated, may hold values from 0 to 767, as said below
- parent: int32 [128], replicated, may hold values from 0 to 127, as said below
- surviving: int32 [128], replicated, may hold values from 0 to 1, as said below
Outputs:
- refilled_pool: bfloat16 [6144, 16, 8, 256], P('dp', None, 'mp')
- attention: bfloat16 [128, 8192], P('dp', 'mp')
The draws below stay inside these ranges and needn't reach their ends.
Inputs may be any that keep to these rules, and one draw needn't show every extreme that they name: `page_table`: for each group, its 16 rows together name each page 0 to 767 once. A pruned branch's parent survives. For every group, at most 2 of its pruned branches have parents in any one group, and this is reached in every draw; those branches have different parents. For a surviving branch the entry names some surviving branch and is not used. `surviving`: each group keeps 2 to 4 of its branches.
All inputs are finite; a program needn't handle non-finite values.
Results may differ from the reference program's by a relative error of at most 0.015.
The reference program's roundings to bfloat16 on the way (of `query_rows`) count: a program that leaves them out, or rounds other values in their place, can miss the bound.
Values may be sent and summed in bfloat16 or wider, within the bound.
No kernel may reach another device: no remote copies, remote signals or barrier semaphores. Data moves between devices by JAX's collectives and lax.ppermute only.
A program may use at most 192 MiB of HBM per device.

```python
import math
import jax
import jax.numpy as jnp
from jax import lax

D = 5120
H = 64
KVH = 8
HD = 128
PAGE = 16
NPAGE = 48
BR_DEV = 16
CAP = 2
BRANCHES = 128
POOL_DEV = 768
POOL = 6144


def routing(key):
    groups = BRANCHES // BR_DEV
    key_count, key_order, key_shift, key_pick, key_group, key_other = jax.random.split(key, 6)
    counts = jax.random.randint(key_count, (groups,), 2, 5)
    order_perm = jax.vmap(lambda subkey: jax.random.permutation(subkey, BR_DEV))(jax.random.split(key_order, groups))
    position = jnp.argsort(order_perm, axis=1)
    alive_mask = position < counts[:, None]
    child_mask = jnp.logical_not(alive_mask)
    child_rank = jnp.maximum(jnp.cumsum(child_mask.astype(jnp.int32), axis=1) - 1, 0)
    group_shift = jax.random.randint(key_shift, (groups,), 0, groups)
    group_ids = jnp.arange(groups, dtype=jnp.int32)
    src_group = (group_ids[:, None] + group_shift[:, None] + child_rank // CAP) % groups
    pair_base = jax.random.randint(key_pick, (groups, BR_DEV), 0, 12)
    base_pick = jnp.take_along_axis(pair_base, child_rank // CAP, axis=1)
    pick_index = (base_pick + child_rank % CAP) % counts[src_group]
    chosen = order_perm[src_group, pick_index]
    other_group = jax.random.randint(key_group, (groups, BR_DEV), 0, groups)
    other_pick = jax.random.randint(key_other, (groups, BR_DEV), 0, 12)
    other_chosen = order_perm[other_group, other_pick % counts[other_group]]
    parent_ids = jnp.where(alive_mask, other_group * BR_DEV + other_chosen, src_group * BR_DEV + chosen)
    return (alive_mask.reshape(-1).astype(jnp.int32), parent_ids.reshape(-1).astype(jnp.int32))


def draw_parent(key, part):
    return routing(key)[1]


def draw_surviving(key, part):
    return routing(key)[0]


def draw_page_table(key, part):
    key = jax.random.fold_in(key, 7)
    groups = BRANCHES // BR_DEV
    perms = jax.vmap(lambda subkey: jax.random.permutation(subkey, BR_DEV * NPAGE))(jax.random.split(key, groups))
    return perms.reshape(BRANCHES, NPAGE).astype(jnp.int32)


def draw_kv_pool(key, part):
    key = jax.random.fold_in(key, 11)
    key_first, key_second = jax.random.split(key, 2)
    shape = (POOL, PAGE, KVH, HD)
    keys_part = 2.5 * jax.random.normal(key_first, shape)
    values_part = jax.random.normal(key_second, shape)
    return jnp.concatenate([keys_part, values_part], axis=-1).astype(jnp.bfloat16)


def shard_levels(stream_key, extent, cuts, low, top_value):
    level, own = 1.0, jax.random.fold_in(stream_key, 6)
    for axis_at, blocks in cuts:
        draws = jnp.exp(jax.random.uniform(jax.random.fold_in(own, axis_at), (blocks,), jnp.float32, low / len(cuts), top_value / len(cuts)))
        level = level * jnp.repeat(draws, extent[axis_at] // blocks).reshape([-1 if axis == axis_at else 1 for axis in range(len(extent))])
    return level


def noise(key, shape, spread, reach, shards=(), held_as=jnp.bfloat16):
    level = shard_levels(key, shape, shards, -0.22, 0.18) if shards else 1.0
    array = jax.random.normal(key, shape, jnp.float32) * spread * level
    return jnp.minimum(jnp.maximum(array, -reach), reach).astype(held_as)


def setup_inputs(seed: int = 0) -> dict:
    keys = jax.random.split(jax.random.key(seed), 11)
    return {
        "hidden": noise(keys[0], (BRANCHES, D), 1.0, 6.0, ((0, 8), (1, 4))),
        "w_query": noise(keys[1], (D, H * HD), D ** -0.5, 0.078125, ((1, 4),)),
        "w_key": noise(keys[2], (D, KVH * HD), D ** -0.5, 0.078125, ((1, 4),)),
        "w_value": noise(keys[3], (D, KVH * HD), D ** -0.5, 0.078125, ((1, 4),)),
        "query_gain": jnp.clip(jnp.exp(jax.random.uniform(keys[4], (HD,), jnp.float32, math.log(0.5), math.log(3.0))), 0.5, 3.0),
        "key_gain": jnp.clip(jnp.exp(jax.random.uniform(keys[5], (HD,), jnp.float32, math.log(0.5), math.log(3.0))), 0.5, 3.0),
        "kv_pool": draw_kv_pool(jax.random.fold_in(keys[10], 71), 0),
        "page_table": draw_page_table(jax.random.fold_in(keys[10], 71), 0),
        "parent": draw_parent(jax.random.fold_in(keys[10], 71), 0),
        "surviving": draw_surviving(jax.random.fold_in(keys[10], 71), 0),
    }


def normalize(values, gain):
    return values * lax.rsqrt(lax.optimization_barrier(jnp.mean(values * values, -1, keepdims=True)) + 1e-06) * gain

def attend(query_one, key_one, value_one, window):
    keys_part = window[..., :HD].astype(jnp.float32)
    values_part = window[..., HD:].astype(jnp.float32)
    scores = jnp.einsum('kgd,tkd->kgt', query_one.astype(jnp.float32), keys_part)
    own_score = jnp.einsum('kgd,kd->kg', query_one.astype(jnp.float32), key_one.astype(jnp.float32))
    peak_score = jnp.maximum(lax.optimization_barrier(jnp.max(scores, -1)), own_score)
    expo_terms = jnp.exp(scores - peak_score[..., None])
    own_term = jnp.exp(own_score - peak_score)
    total_mass = lax.optimization_barrier(jnp.sum(expo_terms, -1)) + own_term
    weights = (expo_terms / total_mass[..., None]).astype(jnp.bfloat16)
    own_weight = (own_term / total_mass).astype(jnp.bfloat16)
    mixed_out = jnp.einsum('kgt,tkd->kgd', weights.astype(jnp.float32), values_part)
    mixed_out = mixed_out + own_weight.astype(jnp.float32)[..., None] * value_one.astype(jnp.float32)[:, None, :]
    return mixed_out.astype(jnp.bfloat16)

def reference(hidden, w_query, w_key, w_value, query_gain, key_gain, kv_pool, page_table, parent, surviving):
    head_group = H // KVH
    query_full = jnp.dot(hidden, w_query, preferred_element_type=jnp.float32).reshape(BRANCHES, KVH, head_group, HD)
    query_rows = (normalize(query_full, query_gain) / math.sqrt(HD)).astype(jnp.bfloat16)
    key_full = jnp.dot(hidden, w_key, preferred_element_type=jnp.float32).reshape(BRANCHES, KVH, HD)
    key_rows = normalize(key_full, key_gain).astype(jnp.bfloat16)
    value_rows = jnp.dot(hidden, w_value, preferred_element_type=jnp.float32).reshape(BRANCHES, KVH, HD).astype(jnp.bfloat16)
    slot_ids = jnp.arange(BRANCHES, dtype=jnp.int32)
    source = jnp.where(surviving > 0, slot_ids, parent).astype(jnp.int32)
    src_pages = (source // BR_DEV * POOL_DEV)[:, None] + page_table[source]
    dst_pages = (slot_ids // BR_DEV * POOL_DEV)[:, None] + page_table
    refilled = kv_pool.at[dst_pages.reshape(-1)].set(kv_pool[src_pages.reshape(-1)])

    def one_branch(inputs):
        query_one, key_one, value_one, pages_one = inputs
        window = refilled[pages_one].reshape(NPAGE * PAGE, KVH, 2 * HD)
        return attend(query_one, key_one, value_one, window)
    outputs = lax.map(one_branch, (query_rows, key_rows, value_rows, dst_pages))
    return (refilled, outputs.reshape(BRANCHES, H * HD))
```

```python
import functools
import math

import jax
import jax.numpy as jnp
from jax import lax
from jax.experimental import pallas as pl
from jax.experimental.pallas import tpu as pltpu
from jax.sharding import PartitionSpec as P

H = 64
KVH = 8
HD = 128
PAGE = 16
NPAGE = 48
CAP = 2
KEEP = 4
NZ = 4
ROUNDS = 24
PREFIX = 8
PIECES = 2
NEVER = 1 << 20


def normalize(values, gain):
    return values * lax.rsqrt(jnp.mean(values * values, -1, keepdims=True) + 1e-06) * gain


def line_times(need):
    ny = need.shape[1]
    at_z = jnp.any(need, axis=1)
    steps = jnp.arange(NZ)[:, None] - jnp.arange(NZ)[None, :]
    hops = jnp.max(
        jnp.where(at_z & (steps > 0)[:, :, None, None], steps[:, :, None, None], 0), axis=0
    )
    across = need & (jnp.arange(ny)[:, None] != jnp.arange(ny)[None, :])[None, :, None, :, None]
    across = jnp.any(across, axis=1)
    far_across = jnp.any(across & (steps[:, :, None, None] == hops[None]), axis=0)
    rank_key = (hops * 2 + far_across) * KEEP - jnp.arange(KEEP)
    pos = jnp.sum((rank_key[..., None, :] > rank_key[..., :, None]).astype(jnp.int32), axis=-1)
    count = [jnp.sum((hops >= h + 1).astype(jnp.int32), axis=-1) for h in range(NZ - 1)]
    never = jnp.full((ny, KEEP), NEVER, jnp.int32)
    times = []
    starts = {}
    for lz in range(NZ):
        row = []
        begin = None
        for sz in range(lz, -1, -1):
            away = lz - sz
            if away == 0:
                begin = jnp.zeros((ny,), jnp.int32)
            else:
                begin = jnp.maximum(
                    begin + count[away - 1][sz + 1] if lz < NZ - 1 else begin,
                    starts[(lz - 1, sz)] + 1,
                )
            starts[(lz, sz)] = begin
            if lz == NZ - 1:
                row.append(never)
            else:
                row.append(jnp.where(hops[sz] > away, begin[:, None] + pos[sz], NEVER))
        row = row[::-1] + [never] * (NZ - 1 - lz)
        times.append(jnp.stack(row))
    return jnp.stack(times)


def plan(parent, surviving, groups, branch_count):
    ny = groups // NZ
    alive = (surviving > 0).reshape(groups, branch_count)
    local = jnp.arange(branch_count)
    rank = jnp.sum((alive[:, None, :] & (local[None, :] < local[:, None])[None]).astype(jnp.int32), axis=-1)
    item = (jnp.arange(groups)[:, None] * KEEP + rank).reshape(-1)
    ids = jnp.arange(groups * branch_count)
    item_of_parent = jnp.sum(jnp.where(parent[:, None] == ids[None, :], item[None, :], 0), axis=1)
    wanted = jnp.where(surviving > 0, -1, item_of_parent).reshape(groups, branch_count)
    items = jnp.arange(groups * KEEP)
    child = jnp.max(
        jnp.where(wanted[:, :, None] == items[None, None, :], local[None, :, None], -1), axis=1
    ).reshape(NZ, ny, NZ, ny, KEEP)
    branch = jnp.sum(
        jnp.where(
            alive[:, :, None] & (rank[:, :, None] == jnp.arange(KEEP)[None, None, :]),
            local[None, :, None],
            0,
        ),
        axis=1,
    ).reshape(NZ, ny, KEEP)
    need = child >= 0
    up = line_times(need)
    down = line_times(need[::-1, :, ::-1])[::-1, ::-1]
    here = jnp.arange(NZ)
    from_below = jnp.concatenate([jnp.full_like(up[:1], NEVER), up[:-1]])
    from_above = jnp.concatenate([down[1:], jnp.full_like(down[:1], NEVER)])
    side = (here[:, None] - here[None, :])[:, :, None, None]
    ready = jnp.where(side == 0, 0, jnp.where(side > 0, from_below, from_above) + 1)
    ready = ready.transpose(0, 2, 1, 3).reshape(NZ, ny, 1, NZ * KEEP)
    crossing = need.transpose(0, 3, 1, 2, 4)
    crossing = crossing & (jnp.arange(ny)[:, None] != jnp.arange(ny)[None, :])[None, :, :, None, None]
    crossing = crossing.reshape(NZ, ny, ny, NZ * KEEP)
    slots = NZ * KEEP
    order = jnp.where(crossing, ready * slots + jnp.arange(slots), NEVER * slots)
    order = jnp.minimum(order, NEVER)
    before = jnp.sum((order[..., None, :] < order[..., :, None]).astype(jnp.int32), axis=-1)
    lead = jnp.where(crossing, ready - before, -NEVER)
    run = jnp.max(
        jnp.where(order[..., None, :] <= order[..., :, None], lead[..., None, :], -NEVER), axis=-1
    )
    cross = jnp.where(crossing, run + before, NEVER).reshape(NZ, ny, ny, NZ, KEEP)
    return child, branch, up, down, cross


def last_round(*times):
    ends = [jnp.max(jnp.where(t < NEVER, t, -1)) for t in times]
    return functools.reduce(jnp.maximum, ends) + 1


def my_tables(parent, surviving, groups, branch_count, me):
    ny = groups // NZ
    child, branch, up, down, cross = plan(parent, surviving, groups, branch_count)
    rounds = last_round(up, down, cross)
    z, y = me // ny, me % ny

    def pick(array, *index):
        for i in index:
            array = lax.dynamic_index_in_dim(array, i, 0, keepdims=False)
        return array

    def line(times, lz):
        padded = jnp.concatenate(
            [jnp.full_like(times[:1], NEVER), times, jnp.full_like(times[:1], NEVER)]
        )
        mine = pick(padded, lz + 1)
        return lax.dynamic_index_in_dim(mine, y, 1, keepdims=False).reshape(-1)

    round_ids = jnp.arange(ROUNDS)

    def table(times, values):
        hit = times[None, :] == round_ids[:, None]
        return jnp.sum(jnp.where(hit, values[None, :] + 1, 0), axis=1) - 1

    slots = NZ * KEEP
    slot_ids = jnp.arange(slots)
    own = (slot_ids // KEEP) == z
    own_branch = pick(branch, z, y)
    source = jnp.where(own, slots + own_branch[slot_ids % KEEP], slot_ids)
    takers_of = pick(child, z, y)

    def takers_on(line_y):
        return lax.dynamic_index_in_dim(takers_of, line_y, 1, keepdims=False).reshape(-1)

    def taker_table(times, line_y):
        return table(times, takers_on(line_y))

    sends = [table(line(up, z), source), table(line(down, z), source)]
    in_up, in_down = line(up, z - 1), line(down, z + 1)
    saves = [table(in_up, slot_ids), table(in_down, slot_ids)]
    takers = [taker_table(in_up, y), taker_table(in_down, y)]
    for shift in range(1, ny):
        y_to, y_from = (y + shift) % ny, (y + ny - shift) % ny
        sends.append(table(pick(cross, z, y, y_to).reshape(-1), source))
        takers.append(taker_table(pick(cross, z, y_from, y).reshape(-1), y_from))
    own_takers = lax.dynamic_index_in_dim(takers_on(y).reshape(NZ, KEEP), z, 0, keepdims=False)
    alive = lax.dynamic_index_in_dim(
        (surviving > 0).reshape(groups, branch_count), me, 0, keepdims=False
    )
    kept = jnp.where(jnp.arange(KEEP) < jnp.sum(alive.astype(jnp.int32)), own_branch, -1)
    return (
        rounds,
        jnp.stack(sends, 1).reshape(-1),
        jnp.stack(saves, 1).reshape(-1),
        jnp.stack(takers, 1).reshape(-1),
        kept,
        own_takers,
    )


SMEM = pl.BlockSpec(memory_space=pltpu.SMEM)
VMEM = pl.BlockSpec(memory_space=pltpu.VMEM)
ANY = pl.BlockSpec(memory_space=pl.ANY)


def step_kernel(links, piece, sending, arrived_count, *refs):
    pages = NPAGE // PIECES
    first = piece * pages
    at, sends, saves, takers, table = refs[:5]
    arrived = refs[5 : 5 + arrived_count]
    rest = refs[5 + arrived_count :]
    pool, _, _, _ = rest[:4]
    store, refilled = rest[4:6]
    packed = rest[6 : 6 + (links if sending else 0)]
    inbox, outbox, in_sem, file_sem, save_sem, pack_sem, out_sem = rest[-7:]
    slots = NZ * KEEP
    now = at[0]
    past = at[1]
    source = [sends[now * links + l] if sending else -1 for l in range(links)]
    save = [saves[past * 2 + l] if arrived_count else -1 for l in range(2)]
    taker = [takers[past * links + l] if arrived_count else -1 for l in range(links)]
    comes = [(taker[l] >= 0) | (save[l] >= 0) if l < 2 else taker[l] >= 0 for l in range(links)]

    if arrived_count:
        for l in range(links):

            @pl.when(comes[l])
            def _():
                pltpu.make_async_copy(arrived[l], inbox.at[l], in_sem.at[l]).start()

    if sending:
        for l in range(links):
            fresh = False
            if arrived_count:
                fresh = (source[l] == save[0]) | (source[l] == save[1])

            @pl.when(source[l] >= slots)
            def _():
                @pl.loop(0, pages, unroll=8)
                def _(p):
                    page = table[(source[l] - slots) * NPAGE + first + p]
                    pltpu.make_async_copy(
                        pool.at[page], outbox.at[l, p], pack_sem.at[l]
                    ).start()

            @pl.when((source[l] >= 0) & (source[l] < slots) & jnp.logical_not(fresh))
            def _():
                pltpu.make_async_copy(
                    store.at[jnp.clip(source[l], 0, slots - 1), pl.ds(first, pages)],
                    outbox.at[l],
                    pack_sem.at[l],
                ).start()

    if arrived_count:
        for l in range(links):

            @pl.when(comes[l])
            def _():
                pltpu.make_async_copy(arrived[l], inbox.at[l], in_sem.at[l]).wait()

            if l < 2 and sending:
                for to in range(links):

                    @pl.when((source[to] >= 0) & (source[to] == save[l]))
                    def _():
                        pltpu.make_async_copy(inbox.at[l], packed[to], out_sem.at[to]).start()

    if sending:
        for l in range(links):
            fresh = False
            if arrived_count:
                fresh = (source[l] == save[0]) | (source[l] == save[1])

            @pl.when((source[l] >= 0) & jnp.logical_not(fresh))
            def _():
                pltpu.make_async_copy(outbox.at[l], outbox.at[l], pack_sem.at[l]).wait()
                pltpu.make_async_copy(outbox.at[l], packed[l], out_sem.at[l]).start()

    if arrived_count:
        for l in range(links):
            if l < 2:

                @pl.when(save[l] >= 0)
                def _():
                    pltpu.make_async_copy(
                        inbox.at[l],
                        store.at[jnp.maximum(save[l], 0), pl.ds(first, pages)],
                        save_sem.at[l],
                    ).start()

            @pl.when(taker[l] >= 0)
            def _():
                @pl.loop(0, pages, unroll=8)
                def _(p):
                    page = table[taker[l] * NPAGE + first + p]
                    pltpu.make_async_copy(
                        inbox.at[l, p], refilled.at[page], file_sem.at[l]
                    ).start()

    if sending:
        for l in range(links):

            @pl.when(source[l] >= 0)
            def _():
                pltpu.make_async_copy(outbox.at[l], packed[l], out_sem.at[l]).wait()

    if arrived_count:
        for l in range(links):
            if l < 2:

                @pl.when(save[l] >= 0)
                def _():
                    pltpu.make_async_copy(inbox.at[l], inbox.at[l], save_sem.at[l]).wait()

            @pl.when(taker[l] >= 0)
            def _():
                pltpu.make_async_copy(inbox.at[l], inbox.at[l], file_sem.at[l]).wait()


def step(links, piece, sending, now, past, tables, arrived, pool, token, store, refilled):
    sends, saves, takers, table = tables
    at = jnp.stack([jnp.asarray(now, jnp.int32), jnp.asarray(past, jnp.int32)])
    window = jax.ShapeDtypeStruct((NPAGE // PIECES,) + pool.shape[1:], pool.dtype)
    count = len(arrived)
    out = pl.pallas_call(
        functools.partial(step_kernel, links, piece, sending, count),
        out_shape=[
            jax.ShapeDtypeStruct(store.shape, store.dtype),
            jax.ShapeDtypeStruct(refilled.shape, refilled.dtype),
        ]
        + ([window] * links if sending else []),
        in_specs=[SMEM] * 5 + [ANY] * (count + 4),
        out_specs=[ANY] * (2 + (links if sending else 0)),
        scratch_shapes=[
            pltpu.VMEM((links,) + window.shape, window.dtype),
            pltpu.VMEM((links,) + window.shape, window.dtype),
            pltpu.SemaphoreType.DMA((links,)),
            pltpu.SemaphoreType.DMA((links,)),
            pltpu.SemaphoreType.DMA((2,)),
            pltpu.SemaphoreType.DMA((links,)),
            pltpu.SemaphoreType.DMA((links,)),
        ],
        compiler_params=pltpu.CompilerParams(vmem_limit_bytes=32 * 1024 * 1024),
        input_output_aliases={5 + count + 2: 0, 5 + count + 3: 1},
        cost_estimate=pl.CostEstimate(flops=0, bytes_accessed=6_000_000, transcendentals=0),
        name="step",
    )(at, sends, saves, takers, table, *arrived, pool, token, store, refilled)
    return out[0], out[1], list(out[2:])


def first_kernel(links, sends, table, pool, *refs):
    pages = NPAGE // PIECES
    slots = NZ * KEEP
    packed = refs[: links * PIECES]
    outbox, in_sem, out_sem = refs[links * PIECES :]
    for piece in range(PIECES):
        for l in range(links):
            source = sends[l]

            @pl.when(source >= slots)
            def _():
                @pl.loop(0, pages, unroll=8)
                def _(p):
                    page = table[(source - slots) * NPAGE + piece * pages + p]
                    pltpu.make_async_copy(
                        pool.at[page], outbox.at[piece, l, p], in_sem.at[piece, l]
                    ).start()

    for piece in range(PIECES):
        for l in range(links):
            box, target = outbox.at[piece, l], packed[piece * links + l]

            @pl.when(sends[l] >= slots)
            def _():
                pltpu.make_async_copy(box, box, in_sem.at[piece, l]).wait()
                pltpu.make_async_copy(box, target, out_sem.at[piece, l]).start()

    for piece in range(PIECES):
        for l in range(links):
            box, target = outbox.at[piece, l], packed[piece * links + l]

            @pl.when(sends[l] >= slots)
            def _():
                pltpu.make_async_copy(box, target, out_sem.at[piece, l]).wait()


def first_windows(links, sends, table, pool):
    window = jax.ShapeDtypeStruct((NPAGE // PIECES,) + pool.shape[1:], pool.dtype)
    return pl.pallas_call(
        functools.partial(first_kernel, links),
        out_shape=[window] * (links * PIECES),
        in_specs=[SMEM] * 2 + [ANY],
        out_specs=[ANY] * (links * PIECES),
        scratch_shapes=[
            pltpu.VMEM((PIECES, links) + window.shape, window.dtype),
            pltpu.SemaphoreType.DMA((PIECES, links)),
            pltpu.SemaphoreType.DMA((PIECES, links)),
        ],
        compiler_params=pltpu.CompilerParams(vmem_limit_bytes=32 * 1024 * 1024),
        cost_estimate=pl.CostEstimate(flops=0, bytes_accessed=6_000_000, transcendentals=0),
        name="first_windows",
    )(sends, table, pool)


def own_kernel(kept, own_takers, table, pool, token, refilled, store, window, in_sem, out_sem):
    for k in range(KEEP):
        source = kept[k]

        @pl.when(source >= 0)
        def _():
            @pl.loop(0, NPAGE, unroll=8)
            def _(p):
                pltpu.make_async_copy(
                    pool.at[table[source * NPAGE + p]], window.at[k, p], in_sem.at[k]
                ).start()

    for k in range(KEEP):
        source = kept[k]

        @pl.when(source >= 0)
        def _():
            pltpu.make_async_copy(window.at[k], window.at[k], in_sem.at[k]).wait()

        for to, lane in ((source, 0), (own_takers[k], 1)):

            @pl.when((source >= 0) & (to >= 0))
            def _():
                @pl.loop(0, NPAGE, unroll=8)
                def _(p):
                    pltpu.make_async_copy(
                        window.at[k, p], refilled.at[table[to * NPAGE + p]], out_sem.at[k, lane]
                    ).start()

    for k in range(KEEP):
        source = kept[k]

        for to, lane in ((source, 0), (own_takers[k], 1)):

            @pl.when((source >= 0) & (to >= 0))
            def _():
                pltpu.make_async_copy(window.at[k], window.at[k], out_sem.at[k, lane]).wait()


def own_windows(kept, own_takers, table, pool, token):
    return pl.pallas_call(
        own_kernel,
        out_shape=[
            jax.ShapeDtypeStruct(pool.shape, pool.dtype),
            jax.ShapeDtypeStruct((NZ * KEEP, NPAGE) + pool.shape[1:], pool.dtype),
        ],
        in_specs=[SMEM] * 3 + [ANY] * 2,
        out_specs=[ANY] * 2,
        scratch_shapes=[
            pltpu.VMEM((KEEP, NPAGE) + pool.shape[1:], pool.dtype),
            pltpu.SemaphoreType.DMA((KEEP,)),
            pltpu.SemaphoreType.DMA((KEEP, 2)),
        ],
        compiler_params=pltpu.CompilerParams(vmem_limit_bytes=32 * 1024 * 1024),
        cost_estimate=pl.CostEstimate(flops=0, bytes_accessed=9_000_000, transcendentals=0),
        name="own_windows",
    )(kept, own_takers, table, pool, token)


def attend_kernel(count, who, table, query, own_key, own_value, refilled, before, out, window, sem):
    out[...] = before[...]
    kv = refilled.shape[2]
    tokens = NPAGE * PAGE * kv
    for i in range(count):
        branch = who[i]

        @pl.when(branch >= 0)
        def _():
            @pl.loop(0, NPAGE, unroll=8)
            def _(p):
                pltpu.make_async_copy(
                    refilled.at[table[branch * NPAGE + p]], window.at[i, p], sem.at[i]
                ).start()

    for i in range(count):
        branch = who[i]

        @pl.when(branch >= 0)
        def _():
            pltpu.make_async_copy(window.at[i], window.at[i], sem.at[i]).wait()
            rows = query[branch]
            if kv == 1:
                flat = window[i, :, :, 0, :].reshape(tokens, 2 * HD)
            else:
                flat = window.at[i].reshape(tokens, 2 * HD)
            scores = lax.dot_general(
                rows, flat[:, :HD], (((1,), (1,)), ((), ())), preferred_element_type=jnp.float32
            )
            token = lax.broadcasted_iota(jnp.int32, scores.shape, 1)
            head = lax.broadcasted_iota(jnp.int32, scores.shape, 0)
            scores = jnp.where(token % kv == head // (H // KVH), scores, -jnp.inf)
            own = jnp.sum(
                rows.astype(jnp.float32) * own_key[branch].astype(jnp.float32), -1, keepdims=True
            )
            peak = jnp.maximum(jnp.max(scores, -1, keepdims=True), own)
            terms = jnp.exp(scores - peak)
            own_term = jnp.exp(own - peak)
            total = jnp.sum(terms, -1, keepdims=True) + own_term
            weights = (terms / total).astype(jnp.bfloat16)
            own_weight = (own_term / total).astype(jnp.bfloat16).astype(jnp.float32)
            mixed = jnp.dot(weights, flat[:, HD:], preferred_element_type=jnp.float32)
            mixed = mixed + own_weight * own_value[branch].astype(jnp.float32)
            out[branch] = mixed.astype(out.dtype)


def attend(who, table, rows, refilled, before):
    count = who.shape[0]
    query, own_key, own_value = rows
    return pl.pallas_call(
        functools.partial(attend_kernel, count),
        out_shape=jax.ShapeDtypeStruct(before.shape, before.dtype),
        in_specs=[SMEM] * 2 + [VMEM] * 3 + [ANY, VMEM],
        out_specs=VMEM,
        scratch_shapes=[
            pltpu.VMEM((count, NPAGE) + refilled.shape[1:], refilled.dtype),
            pltpu.SemaphoreType.DMA((count,)),
        ],
        input_output_aliases={6: 0},
        compiler_params=pltpu.CompilerParams(vmem_limit_bytes=32 * 1024 * 1024),
        cost_estimate=pl.CostEstimate(
            flops=count * 2 * 2 * 16 * 1536 * 128, bytes_accessed=count * 800_000, transcendentals=0
        ),
        name="attend",
    )(who, table, query, own_key, own_value, refilled, before)


def token_rows(hidden, w_query, w_key, w_value, query_gain, key_gain):
    features = lax.all_gather(hidden, "mp", axis=1, tiled=True)
    branch_count = features.shape[0]
    head_group = H // KVH
    heads = w_query.shape[1] // HD
    kv_local = w_key.shape[1] // HD
    query_full = jnp.dot(features, w_query, preferred_element_type=jnp.float32)
    query_full = query_full.reshape(branch_count, heads, HD)
    query_rows = (normalize(query_full, query_gain) / math.sqrt(HD)).astype(jnp.bfloat16)
    key_full = jnp.dot(features, w_key, preferred_element_type=jnp.float32)
    key_rows = normalize(key_full.reshape(branch_count, kv_local, HD), key_gain).astype(jnp.bfloat16)
    value_rows = jnp.dot(features, w_value, preferred_element_type=jnp.float32)
    value_rows = value_rows.reshape(branch_count, kv_local, HD).astype(jnp.bfloat16)
    return (
        query_rows,
        jnp.repeat(key_rows, head_group, axis=1),
        jnp.repeat(value_rows, head_group, axis=1),
    )


def shards(
    hidden, w_query, w_key, w_value, query_gain, key_gain, kv_pool, page_table, parent, surviving
):
    groups = lax.axis_size("dp")
    me = lax.axis_index("dp")
    ny = groups // NZ
    branch_count = hidden.shape[0]
    links = 2 + ny - 1
    rounds, sends, saves, takers, kept, own_takers = my_tables(
        parent, surviving, groups, branch_count, me
    )
    my_table = lax.dynamic_slice_in_dim(
        page_table, me * branch_count, branch_count, 0
    ).reshape(-1)
    tables = (sends, saves, takers, my_table)
    pairs = [
        [(g, g + ny) for g in range(groups - ny)],
        [(g, g - ny) for g in range(ny, groups)],
    ] + [
        [(g, g // ny * ny + (g % ny + shift) % ny) for g in range(groups)] for shift in range(1, ny)
    ]

    def travel(packed):
        return [lax.ppermute(window, "dp", pair) for window, pair in zip(packed, pairs)]

    def took(r):
        return lax.dynamic_slice_in_dim(takers, r * links, links, 0)

    packed = first_windows(links, sends, my_table, kv_pool)
    moving = [travel(packed[piece * links : (piece + 1) * links]) for piece in range(PIECES)]
    refilled, store = own_windows(kept, own_takers, my_table, kv_pool, packed[0])
    rows = token_rows(hidden, w_query, w_key, w_value, query_gain, key_gain)
    attention = jnp.zeros((branch_count, rows[0].shape[1], HD), jnp.bfloat16)
    for r in range(1, PREFIX):
        for piece in range(PIECES):
            store, refilled, packed = step(
                links, piece, True, r, r - 1, tables, moving.pop(0), kv_pool, attention, store, refilled
            )
            moving.append(travel(packed))
        if r == 1:
            attention = attend(
                jnp.concatenate([kept, own_takers]), my_table, rows, refilled, attention
            )
        attention = attend(took(r - 1), my_table, rows, refilled, attention)
    for piece in range(PIECES):
        store, refilled, _ = step(
            links, piece, False, PREFIX, PREFIX - 1, tables, moving.pop(0), kv_pool, attention, store, refilled
        )

    def more(state):
        return state[0] < rounds

    def one_round(state):
        r, store, refilled, attention = state
        moving = []
        for piece in range(PIECES):
            store, refilled, packed = step(
                links, piece, True, r, r, tables, [], kv_pool, attention, store, refilled
            )
            moving.append(travel(packed))
        attention = attend(took(r - 1), my_table, rows, refilled, attention)
        for piece in range(PIECES):
            store, refilled, _ = step(
                links, piece, False, r, r, tables, moving.pop(0), kv_pool, attention, store, refilled
            )
        return r + 1, store, refilled, attention

    r, store, refilled, attention = lax.while_loop(
        more, one_round, (jnp.int32(PREFIX), store, refilled, attention)
    )
    attention = attend(took(r - 1), my_table, rows, refilled, attention)
    return (refilled, attention.reshape(branch_count, -1))


def solution(mesh):
    return jax.shard_map(
        shards,
        mesh=mesh,
        in_specs=(
            P("dp", "mp"),
            P(None, "mp"),
            P(None, "mp"),
            P(None, "mp"),
            P(),
            P(),
            P("dp", None, "mp", None),
            P(),
            P(),
            P(),
        ),
        out_specs=(P("dp", None, "mp", None), P("dp", "mp")),
        check_vma=False,
    )
```

```python
import functools
import math

import jax
import jax.numpy as jnp
from jax import lax
from jax.experimental import pallas as pl
from jax.experimental.pallas import tpu as pltpu
from jax.sharding import PartitionSpec as P

H = 64
KVH = 8
HD = 128
PAGE = 16
NPAGE = 48
CAP = 2
KEEP = 4
NZ = 4
ROUNDS = 24
PREFIX = 8
PIECES = 2
NEVER = 1 << 20


def normalize(values, gain):
    return values * lax.rsqrt(jnp.mean(values * values, -1, keepdims=True) + 1e-06) * gain


def line_times(need):
    ny = need.shape[1]
    at_z = jnp.any(need, axis=1)
    steps = jnp.arange(NZ)[:, None] - jnp.arange(NZ)[None, :]
    hops = jnp.max(
        jnp.where(at_z & (steps > 0)[:, :, None, None], steps[:, :, None, None], 0), axis=0
    )
    across = need & (jnp.arange(ny)[:, None] != jnp.arange(ny)[None, :])[None, :, None, :, None]
    across = jnp.any(across, axis=1)
    far_across = jnp.any(across & (steps[:, :, None, None] == hops[None]), axis=0)
    rank_key = (hops * 2 + far_across) * KEEP - jnp.arange(KEEP)
    pos = jnp.sum((rank_key[..., None, :] > rank_key[..., :, None]).astype(jnp.int32), axis=-1)
    count = [jnp.sum((hops >= h + 1).astype(jnp.int32), axis=-1) for h in range(NZ - 1)]
    never = jnp.full((ny, KEEP), NEVER, jnp.int32)
    times = []
    starts = {}
    for lz in range(NZ):
        row = []
        begin = None
        for sz in range(lz, -1, -1):
            away = lz - sz
            if away == 0:
                begin = jnp.zeros((ny,), jnp.int32)
            else:
                begin = jnp.maximum(
                    begin + count[away - 1][sz + 1] if lz < NZ - 1 else begin,
                    starts[(lz - 1, sz)] + 1,
                )
            starts[(lz, sz)] = begin
            if lz == NZ - 1:
                row.append(never)
            else:
                row.append(jnp.where(hops[sz] > away, begin[:, None] + pos[sz], NEVER))
        row = row[::-1] + [never] * (NZ - 1 - lz)
        times.append(jnp.stack(row))
    return jnp.stack(times)


def plan(parent, surviving, groups, branch_count):
    ny = groups // NZ
    alive = (surviving > 0).reshape(groups, branch_count)
    local = jnp.arange(branch_count)
    rank = jnp.sum((alive[:, None, :] & (local[None, :] < local[:, None])[None]).astype(jnp.int32), axis=-1)
    item = (jnp.arange(groups)[:, None] * KEEP + rank).reshape(-1)
    ids = jnp.arange(groups * branch_count)
    item_of_parent = jnp.sum(jnp.where(parent[:, None] == ids[None, :], item[None, :], 0), axis=1)
    wanted = jnp.where(surviving > 0, -1, item_of_parent).reshape(groups, branch_count)
    items = jnp.arange(groups * KEEP)
    child = jnp.max(
        jnp.where(wanted[:, :, None] == items[None, None, :], local[None, :, None], -1), axis=1
    ).reshape(NZ, ny, NZ, ny, KEEP)
    branch = jnp.sum(
        jnp.where(
            alive[:, :, None] & (rank[:, :, None] == jnp.arange(KEEP)[None, None, :]),
            local[None, :, None],
            0,
        ),
        axis=1,
    ).reshape(NZ, ny, KEEP)
    need = child >= 0
    up = line_times(need)
    down = line_times(need[::-1, :, ::-1])[::-1, ::-1]
    here = jnp.arange(NZ)
    from_below = jnp.concatenate([jnp.full_like(up[:1], NEVER), up[:-1]])
    from_above = jnp.concatenate([down[1:], jnp.full_like(down[:1], NEVER)])
    side = (here[:, None] - here[None, :])[:, :, None, None]
    ready = jnp.where(side == 0, 0, jnp.where(side > 0, from_below, from_above) + 1)
    ready = ready.transpose(0, 2, 1, 3).reshape(NZ, ny, 1, NZ * KEEP)
    crossing = need.transpose(0, 3, 1, 2, 4)
    crossing = crossing & (jnp.arange(ny)[:, None] != jnp.arange(ny)[None, :])[None, :, :, None, None]
    crossing = crossing.reshape(NZ, ny, ny, NZ * KEEP)
    slots = NZ * KEEP
    order = jnp.where(crossing, ready * slots + jnp.arange(slots), NEVER * slots)
    order = jnp.minimum(order, NEVER)
    before = jnp.sum((order[..., None, :] < order[..., :, None]).astype(jnp.int32), axis=-1)
    lead = jnp.where(crossing, ready - before, -NEVER)
    run = jnp.max(
        jnp.where(order[..., None, :] <= order[..., :, None], lead[..., None, :], -NEVER), axis=-1
    )
    cross = jnp.where(crossing, run + before, NEVER).reshape(NZ, ny, ny, NZ, KEEP)
    return child, branch, up, down, cross


def last_round(*times):
    ends = [jnp.max(jnp.where(t < NEVER, t, -1)) for t in times]
    return functools.reduce(jnp.maximum, ends) + 1


def my_tables(parent, surviving, groups, branch_count, me):
    ny = groups // NZ
    child, branch, up, down, cross = plan(parent, surviving, groups, branch_count)
    rounds = last_round(up, down, cross)
    z, y = me // ny, me % ny

    def pick(array, *index):
        for i in index:
            array = lax.dynamic_index_in_dim(array, i, 0, keepdims=False)
        return array

    def line(times, lz):
        padded = jnp.concatenate(
            [jnp.full_like(times[:1], NEVER), times, jnp.full_like(times[:1], NEVER)]
        )
        mine = pick(padded, lz + 1)
        return lax.dynamic_index_in_dim(mine, y, 1, keepdims=False).reshape(-1)

    round_ids = jnp.arange(ROUNDS)

    def table(times, values):
        hit = times[None, :] == round_ids[:, None]
        return jnp.sum(jnp.where(hit, values[None, :] + 1, 0), axis=1) - 1

    slots = NZ * KEEP
    slot_ids = jnp.arange(slots)
    own = (slot_ids // KEEP) == z
    own_branch = pick(branch, z, y)
    source = jnp.where(own, slots + own_branch[slot_ids % KEEP], slot_ids)
    takers_of = pick(child, z, y)

    def takers_on(line_y):
        return lax.dynamic_index_in_dim(takers_of, line_y, 1, keepdims=False).reshape(-1)

    def taker_table(times, line_y):
        return table(times, takers_on(line_y))

    even = z % 2 == 0
    out_up, out_down = line(up, z), line(down, z)
    in_up, in_down = line(up, z - 1), line(down, z + 1)
    outs = [jnp.where(even, out_up, out_down), jnp.where(even, out_down, out_up)]
    ins = [jnp.where(even, in_down, in_up), jnp.where(even, in_up, in_down)]
    sends = [table(times, source) for times in outs]
    saves = [table(times, slot_ids) for times in ins]
    takers = [taker_table(times, y) for times in ins]
    for shift in range(1, ny):
        y_to, y_from = (y + shift) % ny, (y + ny - shift) % ny
        sends.append(table(pick(cross, z, y, y_to).reshape(-1), source))
        takers.append(taker_table(pick(cross, z, y_from, y).reshape(-1), y_from))
    own_takers = lax.dynamic_index_in_dim(takers_on(y).reshape(NZ, KEEP), z, 0, keepdims=False)
    alive = lax.dynamic_index_in_dim(
        (surviving > 0).reshape(groups, branch_count), me, 0, keepdims=False
    )
    kept = jnp.where(jnp.arange(KEEP) < jnp.sum(alive.astype(jnp.int32)), own_branch, -1)
    return (
        rounds,
        jnp.stack(sends, 1).reshape(-1),
        jnp.stack(saves, 1).reshape(-1),
        jnp.stack(takers, 1).reshape(-1),
        kept,
        own_takers,
    )


def first_sends(parent, surviving, groups, branch_count, me):
    ny = groups // NZ
    z, y = me // ny, me % ny
    target = jnp.arange(groups * branch_count) // branch_count
    target_z, target_y = target // ny, target % ny
    local = jnp.arange(branch_count)
    mine = (surviving == 0) & (parent // branch_count == me)
    mine = mine[None, :] & (parent % branch_count == local[:, None])
    best = []
    for steps in (target_z - z, z - target_z):
        hops = jnp.max(jnp.where(mine, steps[None, :], 0), axis=1)
        far_across = jnp.any(
            mine & (steps[None, :] == hops[:, None]) & (target_y != y)[None, :], axis=1
        )
        key = (hops * 2 + far_across) * branch_count + branch_count - 1 - local
        key = jnp.max(jnp.where(hops > 0, key, -1))
        best.append(jnp.where(key >= 0, branch_count - 1 - key % branch_count, -1))
    even = z % 2 == 0
    sends = [jnp.where(even, best[0], best[1]), jnp.where(even, best[1], best[0])]
    for shift in range(1, ny):
        crossing = mine & ((target_z == z) & (target_y == (y + shift) % ny))[None, :]
        first = jnp.min(jnp.where(jnp.any(crossing, axis=1), local, branch_count))
        sends.append(jnp.where(first < branch_count, first, -1))
    return jnp.stack(sends)


SMEM = pl.BlockSpec(memory_space=pltpu.SMEM)
VMEM = pl.BlockSpec(memory_space=pltpu.VMEM)
HBM = pl.BlockSpec(memory_space=pltpu.HBM)
ANY = pl.BlockSpec(memory_space=pl.ANY)


def step_kernel(links, piece, now, past, arrived_count, *refs):
    pages = NPAGE // PIECES
    first = piece * pages
    if now is None and past is None:
        at, refs = refs[0], refs[1:]
        now = past = at[0]
        sending = arrived_count == 0
    else:
        sending = now is not None
    table = refs[0]
    arrived = refs[1 : 1 + arrived_count]
    pool = refs[1 + arrived_count]
    store, refilled = refs[5 + arrived_count : 7 + arrived_count]
    packed = refs[7 + arrived_count : -4]
    file_sem, save_sem, pack_sem, fresh_sem = refs[-4:]
    slots = NZ * KEEP
    saves_at = ROUNDS * links
    takers_at = saves_at + ROUNDS * 2
    pages_at = takers_at + ROUNDS * links
    if sending:
        source = [table[now * links + l] for l in range(links)]
    if arrived_count:
        save = [table[saves_at + past * 2 + l] for l in range(2)]
        taker = [table[takers_at + past * links + l] for l in range(links)]

    def is_fresh(l):
        if not arrived_count:
            return False
        return (source[l] >= 0) & ((source[l] == save[0]) | (source[l] == save[1]))

    if sending:
        for l in range(links):

            @pl.when(source[l] >= slots)
            def _():
                @pl.loop(0, pages, unroll=8)
                def _(p):
                    page = table[pages_at + (source[l] - slots) * NPAGE + first + p]
                    pltpu.make_async_copy(
                        pool.at[page], packed[l].at[p], pack_sem.at[l]
                    ).start()

            @pl.when((source[l] >= 0) & (source[l] < slots) & jnp.logical_not(is_fresh(l)))
            def _():
                pltpu.make_async_copy(
                    store.at[jnp.clip(source[l], 0, slots - 1), pl.ds(first, pages)],
                    packed[l],
                    pack_sem.at[l],
                ).start()

            if arrived_count:
                for come in range(2):

                    @pl.when((source[l] >= 0) & (source[l] == save[come]))
                    def _():
                        pltpu.make_async_copy(arrived[come], packed[l], fresh_sem.at[l]).start()

    if arrived_count:
        for l in range(links):
            if l < 2:

                @pl.when(save[l] >= 0)
                def _():
                    pltpu.make_async_copy(
                        arrived[l],
                        store.at[jnp.maximum(save[l], 0), pl.ds(first, pages)],
                        save_sem.at[l],
                    ).start()

            @pl.when(taker[l] >= 0)
            def _():
                @pl.loop(0, pages, unroll=8)
                def _(p):
                    page = table[pages_at + taker[l] * NPAGE + first + p]
                    pltpu.make_async_copy(
                        arrived[l].at[p], refilled.at[page], file_sem.at[l]
                    ).start()

    if sending:
        for l in range(links):

            @pl.when((source[l] >= 0) & jnp.logical_not(is_fresh(l)))
            def _():
                pltpu.make_async_copy(packed[l], packed[l], pack_sem.at[l]).wait()

            if arrived_count:

                @pl.when(is_fresh(l))
                def _():
                    pltpu.make_async_copy(packed[l], packed[l], fresh_sem.at[l]).wait()

    if arrived_count:
        for l in range(links):
            if l < 2:

                @pl.when(save[l] >= 0)
                def _():
                    pltpu.make_async_copy(arrived[l], arrived[l], save_sem.at[l]).wait()

            @pl.when(taker[l] >= 0)
            def _():
                pltpu.make_async_copy(arrived[l], arrived[l], file_sem.at[l]).wait()


def step(links, piece, now, past, table, arrived, pool, token, store, refilled, sending=None):
    window = jax.ShapeDtypeStruct((NPAGE // PIECES,) + pool.shape[1:], pool.dtype)
    count = len(arrived)
    at = []
    if sending is None:
        sending = now is not None
    else:
        at = [jnp.stack([now if sending else past])]
        now = past = None
    lead = len(at) + 1 + count
    out = pl.pallas_call(
        functools.partial(step_kernel, links, piece, now, past, count),
        out_shape=[
            jax.ShapeDtypeStruct(store.shape, store.dtype),
            jax.ShapeDtypeStruct(refilled.shape, refilled.dtype),
        ]
        + ([window] * links if sending else []),
        in_specs=[SMEM] * (len(at) + 1) + [VMEM] * count + [HBM, ANY, HBM, HBM],
        out_specs=[HBM] * 2 + [VMEM] * (links if sending else 0),
        scratch_shapes=[
            pltpu.SemaphoreType.DMA((links,)),
            pltpu.SemaphoreType.DMA((2,)),
            pltpu.SemaphoreType.DMA((links,)),
            pltpu.SemaphoreType.DMA((links,)),
        ],
        input_output_aliases={lead + 2: 0, lead + 3: 1},
        compiler_params=pltpu.CompilerParams(vmem_limit_bytes=32 * 1024 * 1024),
        cost_estimate=pl.CostEstimate(flops=0, bytes_accessed=6_000_000, transcendentals=0),
        name="step",
    )(*at, table, *arrived, pool, token, store, refilled)
    return out[0], out[1], list(out[2:])


def first_kernel(links, sends, table, pool, *refs):
    pages = NPAGE // PIECES
    packed, sem = refs[:-1], refs[-1]
    for piece in range(PIECES):
        for l in range(links):

            @pl.when(sends[l] >= 0)
            def _():
                @pl.loop(0, pages, unroll=8)
                def _(p):
                    page = table[sends[l] * NPAGE + piece * pages + p]
                    pltpu.make_async_copy(
                        pool.at[page], packed[piece * links + l].at[p], sem.at[piece, l]
                    ).start()

    for piece in range(PIECES):
        for l in range(links):
            box = packed[piece * links + l]

            @pl.when(sends[l] >= 0)
            def _():
                pltpu.make_async_copy(box, box, sem.at[piece, l]).wait()


def first_windows(links, sends, table, pool):
    window = jax.ShapeDtypeStruct((NPAGE // PIECES,) + pool.shape[1:], pool.dtype)
    return pl.pallas_call(
        functools.partial(first_kernel, links),
        out_shape=[window] * (links * PIECES),
        in_specs=[SMEM] * 2 + [HBM],
        out_specs=[VMEM] * (links * PIECES),
        scratch_shapes=[pltpu.SemaphoreType.DMA((PIECES, links))],
        compiler_params=pltpu.CompilerParams(vmem_limit_bytes=32 * 1024 * 1024),
        cost_estimate=pl.CostEstimate(flops=0, bytes_accessed=6_000_000, transcendentals=0),
        name="first_windows",
    )(sends, table, pool)


def own_kernel(kept, own_takers, table, pool, token, refilled, store, window, in_sem, out_sem):
    for k in range(KEEP):
        source = kept[k]

        @pl.when(source >= 0)
        def _():
            @pl.loop(0, NPAGE, unroll=8)
            def _(p):
                pltpu.make_async_copy(
                    pool.at[table[source * NPAGE + p]], window.at[k, p], in_sem.at[k]
                ).start()

    for k in range(KEEP):
        source = kept[k]

        @pl.when(source >= 0)
        def _():
            pltpu.make_async_copy(window.at[k], window.at[k], in_sem.at[k]).wait()

        for to, lane in ((source, 0), (own_takers[k], 1)):

            @pl.when((source >= 0) & (to >= 0))
            def _():
                @pl.loop(0, NPAGE, unroll=8)
                def _(p):
                    pltpu.make_async_copy(
                        window.at[k, p], refilled.at[table[to * NPAGE + p]], out_sem.at[k, lane]
                    ).start()

    for k in range(KEEP):
        source = kept[k]

        for to, lane in ((source, 0), (own_takers[k], 1)):

            @pl.when((source >= 0) & (to >= 0))
            def _():
                pltpu.make_async_copy(window.at[k], window.at[k], out_sem.at[k, lane]).wait()


def own_windows(kept, own_takers, table, pool, token):
    return pl.pallas_call(
        own_kernel,
        out_shape=[
            jax.ShapeDtypeStruct(pool.shape, pool.dtype),
            jax.ShapeDtypeStruct((NZ * KEEP, NPAGE) + pool.shape[1:], pool.dtype),
        ],
        in_specs=[SMEM] * 3 + [HBM, ANY],
        out_specs=[HBM] * 2,
        scratch_shapes=[
            pltpu.VMEM((KEEP, NPAGE) + pool.shape[1:], pool.dtype),
            pltpu.SemaphoreType.DMA((KEEP,)),
            pltpu.SemaphoreType.DMA((KEEP, 2)),
        ],
        compiler_params=pltpu.CompilerParams(vmem_limit_bytes=32 * 1024 * 1024),
        cost_estimate=pl.CostEstimate(flops=0, bytes_accessed=9_000_000, transcendentals=0),
        name="own_windows",
    )(kept, own_takers, table, pool, token)


def attend_kernel(count, who, table, query, own_key, own_value, refilled, before, out, window, sem):
    out[...] = before[...]
    kv = refilled.shape[2]
    tokens = NPAGE * PAGE * kv
    for i in range(count):
        branch = who[i]

        @pl.when(branch >= 0)
        def _():
            @pl.loop(0, NPAGE, unroll=8)
            def _(p):
                pltpu.make_async_copy(
                    refilled.at[table[branch * NPAGE + p]], window.at[i, p], sem.at[i]
                ).start()

    for i in range(count):
        branch = who[i]

        @pl.when(branch >= 0)
        def _():
            pltpu.make_async_copy(window.at[i], window.at[i], sem.at[i]).wait()
            rows = query[branch]
            if kv == 1:
                flat = window[i, :, :, 0, :].reshape(tokens, 2 * HD)
            else:
                flat = window.at[i].reshape(tokens, 2 * HD)
            scores = lax.dot_general(
                rows, flat[:, :HD], (((1,), (1,)), ((), ())), preferred_element_type=jnp.float32
            )
            token = lax.broadcasted_iota(jnp.int32, scores.shape, 1)
            head = lax.broadcasted_iota(jnp.int32, scores.shape, 0)
            scores = jnp.where(token % kv == head // (H // KVH), scores, -jnp.inf)
            own = jnp.sum(
                rows.astype(jnp.float32) * own_key[branch].astype(jnp.float32), -1, keepdims=True
            )
            peak = jnp.maximum(jnp.max(scores, -1, keepdims=True), own)
            terms = jnp.exp(scores - peak)
            own_term = jnp.exp(own - peak)
            total = jnp.sum(terms, -1, keepdims=True) + own_term
            weights = (terms / total).astype(jnp.bfloat16)
            own_weight = (own_term / total).astype(jnp.bfloat16).astype(jnp.float32)
            mixed = jnp.dot(weights, flat[:, HD:], preferred_element_type=jnp.float32)
            mixed = mixed + own_weight * own_value[branch].astype(jnp.float32)
            out[branch] = mixed.astype(out.dtype)


def attend(who, table, rows, refilled, before):
    count = who.shape[0]
    query, own_key, own_value = rows
    return pl.pallas_call(
        functools.partial(attend_kernel, count),
        out_shape=jax.ShapeDtypeStruct(before.shape, before.dtype),
        in_specs=[SMEM] * 2 + [VMEM] * 3 + [HBM, VMEM],
        out_specs=VMEM,
        scratch_shapes=[
            pltpu.VMEM((count, NPAGE) + refilled.shape[1:], refilled.dtype),
            pltpu.SemaphoreType.DMA((count,)),
        ],
        input_output_aliases={6: 0},
        compiler_params=pltpu.CompilerParams(vmem_limit_bytes=32 * 1024 * 1024),
        cost_estimate=pl.CostEstimate(
            flops=count * 2 * 2 * 16 * 1536 * 128, bytes_accessed=count * 800_000, transcendentals=0
        ),
        name="attend",
    )(who, table, query, own_key, own_value, refilled, before)


def token_rows(hidden, w_query, w_key, w_value, query_gain, key_gain):
    features = lax.all_gather(hidden, "mp", axis=1, tiled=True)
    branch_count = features.shape[0]
    head_group = H // KVH
    heads = w_query.shape[1] // HD
    kv_local = w_key.shape[1] // HD
    query_full = jnp.dot(features, w_query, preferred_element_type=jnp.float32)
    query_full = query_full.reshape(branch_count, heads, HD)
    query_rows = (normalize(query_full, query_gain) / math.sqrt(HD)).astype(jnp.bfloat16)
    key_full = jnp.dot(features, w_key, preferred_element_type=jnp.float32)
    key_rows = normalize(key_full.reshape(branch_count, kv_local, HD), key_gain).astype(jnp.bfloat16)
    value_rows = jnp.dot(features, w_value, preferred_element_type=jnp.float32)
    value_rows = value_rows.reshape(branch_count, kv_local, HD).astype(jnp.bfloat16)
    return (
        query_rows,
        jnp.repeat(key_rows, head_group, axis=1),
        jnp.repeat(value_rows, head_group, axis=1),
    )


def shards(
    hidden, w_query, w_key, w_value, query_gain, key_gain, kv_pool, page_table, parent, surviving
):
    groups = lax.axis_size("dp")
    me = lax.axis_index("dp")
    ny = groups // NZ
    branch_count = hidden.shape[0]
    links = 2 + ny - 1
    my_table = lax.dynamic_slice_in_dim(
        page_table, me * branch_count, branch_count, 0
    ).reshape(-1)
    sends = first_sends(parent, surviving, groups, branch_count, me)
    packed = first_windows(links, sends, my_table, kv_pool)
    parent, surviving, packed = lax.optimization_barrier((parent, surviving, packed))
    along = [[], []]
    for g in range(groups):
        z = g // ny
        along[0].append((g, g + ny if z % 2 == 0 else g - ny))
        along[1].append((g, g if z in (0, NZ - 1) else g + ny if z % 2 else g - ny))
    pairs = along + [
        [(g, g // ny * ny + (g % ny + shift) % ny) for g in range(groups)] for shift in range(1, ny)
    ]

    def travel(packed):
        return [lax.ppermute(window, "dp", pair) for window, pair in zip(packed, pairs)]

    moving = [travel(packed[piece * links : (piece + 1) * links]) for piece in range(PIECES)]
    rounds, sends, saves, takers, kept, own_takers = my_tables(
        parent, surviving, groups, branch_count, me
    )
    table = jnp.concatenate([sends, saves, takers, my_table])

    def took(r):
        return lax.dynamic_slice_in_dim(takers, r * links, links, 0)

    refilled, store = own_windows(kept, own_takers, my_table, kv_pool, packed[0])
    rows = token_rows(hidden, w_query, w_key, w_value, query_gain, key_gain)
    attention = jnp.zeros((branch_count, rows[0].shape[1], HD), jnp.bfloat16)
    for r in range(1, PREFIX):
        for piece in range(PIECES):
            store, refilled, packed = step(
                links, piece, r, r - 1, table, moving.pop(0), kv_pool, attention, store, refilled
            )
            moving.append(travel(packed))
        if r == 1:
            attention = attend(
                jnp.concatenate([kept, own_takers]), my_table, rows, refilled, attention
            )
        attention = attend(took(r - 1), my_table, rows, refilled, attention)
    for piece in range(PIECES):
        store, refilled, _ = step(
            links, piece, None, PREFIX - 1, table, moving.pop(0), kv_pool, attention, store, refilled
        )

    def more(state):
        return state[0] < rounds

    def one_round(state):
        r, store, refilled, attention = state
        moving = []
        for piece in range(PIECES):
            store, refilled, packed = step(
                links, piece, r, r, table, [], kv_pool, attention, store, refilled, sending=True
            )
            moving.append(travel(packed))
        attention = attend(took(r - 1), my_table, rows, refilled, attention)
        for piece in range(PIECES):
            store, refilled, _ = step(
                links, piece, r, r, table, moving.pop(0), kv_pool, attention, store, refilled, sending=False
            )
        return r + 1, store, refilled, attention

    r, store, refilled, attention = lax.while_loop(
        more, one_round, (jnp.int32(PREFIX), store, refilled, attention)
    )
    attention = attend(took(r - 1), my_table, rows, refilled, attention)
    return (refilled, attention.reshape(branch_count, -1))


def solution(mesh):
    return jax.shard_map(
        shards,
        mesh=mesh,
        in_specs=(
            P("dp", "mp"),
            P(None, "mp"),
            P(None, "mp"),
            P(None, "mp"),
            P(),
            P(),
            P("dp", None, "mp", None),
            P(),
            P(),
            P(),
        ),
        out_specs=(P("dp", None, "mp", None), P("dp", "mp")),
        check_vma=False,
    )
```

```python
import functools
import math

import jax
import jax.numpy as jnp
from jax import lax
from jax.experimental import pallas as pl
from jax.experimental.pallas import tpu as pltpu
from jax.sharding import PartitionSpec as P

H = 64
KVH = 8
HD = 128
PAGE = 16
NPAGE = 48
CAP = 2
KEEP = 4
NZ = 4
ROUNDS = 24
PREFIX = 8
FIRST = 2
PIECES = 2
ROOM = 53 * 1024 * 1024
NEVER = 1 << 20


def normalize(values, gain):
    return values * lax.rsqrt(jnp.mean(values * values, -1, keepdims=True) + 1e-06) * gain


def line_times(need):
    ny = need.shape[1]
    at_z = jnp.any(need, axis=1)
    steps = jnp.arange(NZ)[:, None] - jnp.arange(NZ)[None, :]
    hops = jnp.max(
        jnp.where(at_z & (steps > 0)[:, :, None, None], steps[:, :, None, None], 0), axis=0
    )
    across = need & (jnp.arange(ny)[:, None] != jnp.arange(ny)[None, :])[None, :, None, :, None]
    across = jnp.any(across, axis=1)
    far_across = jnp.any(across & (steps[:, :, None, None] == hops[None]), axis=0)
    rank_key = (hops * 2 + far_across) * KEEP - jnp.arange(KEEP)
    pos = jnp.sum((rank_key[..., None, :] > rank_key[..., :, None]).astype(jnp.int32), axis=-1)
    count = [jnp.sum((hops >= h + 1).astype(jnp.int32), axis=-1) for h in range(NZ - 1)]
    never = jnp.full((ny, KEEP), NEVER, jnp.int32)
    times = []
    starts = {}
    for lz in range(NZ):
        row = []
        begin = None
        for sz in range(lz, -1, -1):
            away = lz - sz
            if away == 0:
                begin = jnp.zeros((ny,), jnp.int32)
            else:
                begin = jnp.maximum(
                    begin + count[away - 1][sz + 1] if lz < NZ - 1 else begin,
                    jnp.maximum(starts[(lz - 1, sz)] + 1, FIRST),
                )
            starts[(lz, sz)] = begin
            if lz == NZ - 1:
                row.append(never)
            else:
                row.append(jnp.where(hops[sz] > away, begin[:, None] + pos[sz], NEVER))
        row = row[::-1] + [never] * (NZ - 1 - lz)
        times.append(jnp.stack(row))
    return jnp.stack(times)


def plan(parent, surviving, groups, branch_count):
    ny = groups // NZ
    alive = (surviving > 0).reshape(groups, branch_count)
    local = jnp.arange(branch_count)
    rank = jnp.sum((alive[:, None, :] & (local[None, :] < local[:, None])[None]).astype(jnp.int32), axis=-1)
    item = (jnp.arange(groups)[:, None] * KEEP + rank).reshape(-1)
    ids = jnp.arange(groups * branch_count)
    item_of_parent = jnp.sum(jnp.where(parent[:, None] == ids[None, :], item[None, :], 0), axis=1)
    wanted = jnp.where(surviving > 0, -1, item_of_parent).reshape(groups, branch_count)
    items = jnp.arange(groups * KEEP)
    child = jnp.max(
        jnp.where(wanted[:, :, None] == items[None, None, :], local[None, :, None], -1), axis=1
    ).reshape(NZ, ny, NZ, ny, KEEP)
    branch = jnp.sum(
        jnp.where(
            alive[:, :, None] & (rank[:, :, None] == jnp.arange(KEEP)[None, None, :]),
            local[None, :, None],
            0,
        ),
        axis=1,
    ).reshape(NZ, ny, KEEP)
    need = child >= 0
    up = line_times(need)
    down = line_times(need[::-1, :, ::-1])[::-1, ::-1]
    here = jnp.arange(NZ)
    from_below = jnp.concatenate([jnp.full_like(up[:1], NEVER), up[:-1]])
    from_above = jnp.concatenate([down[1:], jnp.full_like(down[:1], NEVER)])
    side = (here[:, None] - here[None, :])[:, :, None, None]
    arrival = jnp.where(side > 0, from_below, from_above)
    ready = jnp.where(side == 0, 0, jnp.maximum(arrival + 1, FIRST))
    ready = ready.transpose(0, 2, 1, 3).reshape(NZ, ny, 1, NZ * KEEP)
    crossing = need.transpose(0, 3, 1, 2, 4)
    crossing = crossing & (jnp.arange(ny)[:, None] != jnp.arange(ny)[None, :])[None, :, :, None, None]
    crossing = crossing.reshape(NZ, ny, ny, NZ * KEEP)
    slots = NZ * KEEP
    order = jnp.where(crossing, ready * slots + jnp.arange(slots), NEVER * slots)
    order = jnp.minimum(order, NEVER)
    before = jnp.sum((order[..., None, :] < order[..., :, None]).astype(jnp.int32), axis=-1)
    lead = jnp.where(crossing, ready - before, -NEVER)
    run = jnp.max(
        jnp.where(order[..., None, :] <= order[..., :, None], lead[..., None, :], -NEVER), axis=-1
    )
    cross = jnp.where(crossing, run + before, NEVER).reshape(NZ, ny, ny, NZ, KEEP)
    return child, branch, up, down, cross


def last_round(*times):
    ends = [jnp.max(jnp.where(t < NEVER, t, -1)) for t in times]
    return functools.reduce(jnp.maximum, ends) + 1


def my_tables(parent, surviving, groups, branch_count, me):
    ny = groups // NZ
    child, branch, up, down, cross = plan(parent, surviving, groups, branch_count)
    rounds = last_round(up, down, cross)
    z, y = me // ny, me % ny

    def pick(array, *index):
        for i in index:
            array = lax.dynamic_index_in_dim(array, i, 0, keepdims=False)
        return array

    def line(times, lz):
        padded = jnp.concatenate(
            [jnp.full_like(times[:1], NEVER), times, jnp.full_like(times[:1], NEVER)]
        )
        mine = pick(padded, lz + 1)
        return lax.dynamic_index_in_dim(mine, y, 1, keepdims=False).reshape(-1)

    round_ids = jnp.arange(ROUNDS)

    def table(times, values):
        hit = times[None, :] == round_ids[:, None]
        return jnp.sum(jnp.where(hit, values[None, :] + 1, 0), axis=1) - 1

    slots = NZ * KEEP
    slot_ids = jnp.arange(slots)
    own = (slot_ids // KEEP) == z
    own_branch = pick(branch, z, y)
    source = jnp.where(own, slots + own_branch[slot_ids % KEEP], slot_ids)
    takers_of = pick(child, z, y)

    def takers_on(line_y):
        return lax.dynamic_index_in_dim(takers_of, line_y, 1, keepdims=False).reshape(-1)

    def taker_table(times, line_y):
        return table(times, takers_on(line_y))

    even = z % 2 == 0
    out_up, out_down = line(up, z), line(down, z)
    in_up, in_down = line(up, z - 1), line(down, z + 1)
    outs = [jnp.where(even, out_up, out_down), jnp.where(even, out_down, out_up)]
    ins = [jnp.where(even, in_down, in_up), jnp.where(even, in_up, in_down)]
    sends = [table(times, source) for times in outs]
    saves = [table(times, slot_ids) for times in ins]
    takers = [taker_table(times, y) for times in ins]
    for shift in range(1, ny):
        y_to, y_from = (y + shift) % ny, (y + ny - shift) % ny
        sends.append(table(pick(cross, z, y, y_to).reshape(-1), source))
        takers.append(taker_table(pick(cross, z, y_from, y).reshape(-1), y_from))
    own_takers = lax.dynamic_index_in_dim(takers_on(y).reshape(NZ, KEEP), z, 0, keepdims=False)
    alive = lax.dynamic_index_in_dim(
        (surviving > 0).reshape(groups, branch_count), me, 0, keepdims=False
    )
    kept = jnp.where(jnp.arange(KEEP) < jnp.sum(alive.astype(jnp.int32)), own_branch, -1)
    return (
        rounds,
        jnp.stack(sends, 1).reshape(-1),
        jnp.stack(saves, 1).reshape(-1),
        jnp.stack(takers, 1).reshape(-1),
        kept,
        own_takers,
    )


SMEM = pl.BlockSpec(memory_space=pltpu.SMEM)
VMEM = pl.BlockSpec(memory_space=pltpu.VMEM)
HBM = pl.BlockSpec(memory_space=pltpu.HBM)
ANY = pl.BlockSpec(memory_space=pl.ANY)


def first_kernel(groups, branch_count, parent, surviving, page_table, pool, *refs):
    ny = groups // NZ
    packed, sem = refs[:-1], refs[-1]
    me = lax.axis_index("dp")
    z, y = me // ny, me % ny
    shape = (branch_count, groups * branch_count)
    child = lax.broadcasted_iota(jnp.int32, shape, 1)
    local = lax.broadcasted_iota(jnp.int32, shape, 0)
    column = lax.broadcasted_iota(jnp.int32, (branch_count, 1), 0)
    mine = (surviving[...] == 0) & (parent[...] == me * branch_count + local)
    target = lax.div(child, branch_count)
    target_z = lax.div(target, ny)
    target_y = target - target_z * ny

    def seen(mask):
        return jnp.max(mask.astype(jnp.int32), axis=1, keepdims=True)

    def leading(key):
        rows = []
        for _ in range(FIRST):
            best = jnp.max(key)
            rows.append(
                jnp.where(best >= 0, branch_count - 1 - lax.rem(best, branch_count), -1)
            )
            key = jnp.where(key == best, -1, key)
        return rows

    ways = []
    for steps in (target_z - z, z - target_z):
        hops = jnp.max(jnp.where(mine, steps, 0), axis=1, keepdims=True)
        far_across = seen(mine & (steps == hops) & (target_y != y))
        key = (hops * 2 + far_across) * branch_count + branch_count - 1 - column
        ways.append(leading(jnp.where(hops > 0, key, -1)))
    even = lax.rem(z, 2) == 0
    sends = [
        [jnp.where(even, u, d) for u, d in zip(*ways)],
        [jnp.where(even, d, u) for u, d in zip(*ways)],
    ]
    for shift in range(1, ny):
        to = lax.rem(y + shift, ny)
        crossing = seen(mine & (target_z == z) & (target_y == to))
        sends.append(leading(jnp.where(crossing > 0, branch_count - 1 - column, -1)))
    for l, rows in enumerate(sends):
        for r, row in enumerate(rows):

            @pl.when(row >= 0)
            def _():
                @pl.loop(0, NPAGE, unroll=8)
                def _(p):
                    page = page_table[me * branch_count + row, p]
                    pltpu.make_async_copy(
                        pool.at[page], packed[l].at[r * NPAGE + p], sem.at[l, r]
                    ).start()

    for l, rows in enumerate(sends):
        for r, row in enumerate(rows):
            box = packed[l].at[pl.ds(r * NPAGE, NPAGE)]

            @pl.when(row >= 0)
            def _():
                pltpu.make_async_copy(box, box, sem.at[l, r]).wait()


def first_windows(groups, branch_count, parent, surviving, page_table, pool):
    links = 2 + groups // NZ - 1
    windows = jax.ShapeDtypeStruct((FIRST * NPAGE,) + pool.shape[1:], pool.dtype)
    return pl.pallas_call(
        functools.partial(first_kernel, groups, branch_count),
        out_shape=[windows] * links,
        in_specs=[VMEM] * 2 + [SMEM, HBM],
        out_specs=[VMEM] * links,
        scratch_shapes=[pltpu.SemaphoreType.DMA((links, FIRST))],
        compiler_params=pltpu.CompilerParams(vmem_limit_bytes=ROOM),
        cost_estimate=pl.CostEstimate(flops=0, bytes_accessed=6_000_000, transcendentals=0),
        name="first_windows",
    )(parent.reshape(1, -1), surviving.reshape(1, -1), page_table, pool)


def step_kernel(links, packs, files, traced, *refs):
    if traced:
        at, refs = refs[0][0], refs[1:]
        packs = [(at, first, pages) for _, first, pages in packs]
        files = [(at, first, pages) for _, first, pages in files]
    table = refs[0]
    count = links if files else 0
    arrived = refs[1 : 1 + count]
    pool = refs[1 + count]
    store, refilled = refs[5 + count : 7 + count]
    packed = refs[7 + count : -4]
    file_sem, save_sem, pack_sem, fresh_sem = refs[-4:]
    slots = NZ * KEEP
    saves_at = ROUNDS * links
    takers_at = saves_at + ROUNDS * 2
    pages_at = takers_at + ROUNDS * links

    comes = []
    offset = 0
    for r, first, pages in files:
        for l in range(links):
            part = arrived[l].at[pl.ds(offset, pages)]
            save = table[saves_at + r * 2 + l] if l < 2 else None
            comes.append((l, save, table[takers_at + r * links + l], part, first, pages))
        offset += pages

    def is_fresh(source):
        fresh = [source == save for _, save, _, _, _, _ in comes if save is not None]
        return (source >= 0) & functools.reduce(jnp.logical_or, fresh) if fresh else False

    goes = []
    for i, (r, first, pages) in enumerate(packs):
        for l in range(links):
            goes.append((table[r * links + l], packed[i * links + l], first, pages))

    for i, (source, box, first, pages) in enumerate(goes):

        @pl.when(source >= slots)
        def _():
            @pl.loop(0, pages, unroll=8)
            def _(p):
                page = table[pages_at + (source - slots) * NPAGE + first + p]
                pltpu.make_async_copy(pool.at[page], box.at[p], pack_sem.at[i]).start()

        @pl.when((source >= 0) & (source < slots) & jnp.logical_not(is_fresh(source)))
        def _():
            pltpu.make_async_copy(
                store.at[jnp.clip(source, 0, slots - 1), pl.ds(first, pages)],
                box,
                pack_sem.at[i],
            ).start()

        for _, save, _, part, file_first, file_pages in comes:
            if save is not None and file_first <= first < file_first + file_pages:

                @pl.when((source >= 0) & (source == save))
                def _():
                    pltpu.make_async_copy(
                        part.at[pl.ds(first - file_first, pages)], box, fresh_sem.at[i]
                    ).start()

    for i, (_, save, taker, part, first, pages) in enumerate(comes):
        if save is not None:

            @pl.when(save >= 0)
            def _():
                pltpu.make_async_copy(
                    part, store.at[jnp.maximum(save, 0), pl.ds(first, pages)], save_sem.at[i]
                ).start()

        @pl.when(taker >= 0)
        def _():
            @pl.loop(0, pages, unroll=8)
            def _(p):
                page = table[pages_at + taker * NPAGE + first + p]
                pltpu.make_async_copy(part.at[p], refilled.at[page], file_sem.at[i]).start()

    for i, (source, box, first, pages) in enumerate(goes):

        @pl.when((source >= 0) & jnp.logical_not(is_fresh(source)))
        def _():
            pltpu.make_async_copy(box, box, pack_sem.at[i]).wait()

        if comes:

            @pl.when(is_fresh(source))
            def _():
                pltpu.make_async_copy(box, box, fresh_sem.at[i]).wait()

    for i, (_, save, taker, part, first, pages) in enumerate(comes):
        if save is not None:

            @pl.when(save >= 0)
            def _():
                pltpu.make_async_copy(part, part, save_sem.at[i]).wait()

        @pl.when(taker >= 0)
        def _():
            pltpu.make_async_copy(part, part, file_sem.at[i]).wait()


def step(links, packs, files, at, table, arrived, pool, token, store, refilled):
    at = [] if at is None else [jnp.stack([at])]
    count = len(arrived)
    lead = len(at) + 1 + count
    boxes = [
        jax.ShapeDtypeStruct((pages,) + pool.shape[1:], pool.dtype)
        for _, _, pages in packs
        for _ in range(links)
    ]
    out = pl.pallas_call(
        functools.partial(step_kernel, links, packs, files, bool(at)),
        out_shape=[
            jax.ShapeDtypeStruct(store.shape, store.dtype),
            jax.ShapeDtypeStruct(refilled.shape, refilled.dtype),
        ]
        + boxes,
        in_specs=[SMEM] * (len(at) + 1) + [VMEM] * count + [HBM, ANY, HBM, HBM],
        out_specs=[HBM] * 2 + [VMEM] * len(boxes),
        scratch_shapes=[
            pltpu.SemaphoreType.DMA((max(len(files), 1) * links,)),
            pltpu.SemaphoreType.DMA((max(len(files), 1) * links,)),
            pltpu.SemaphoreType.DMA((max(len(packs), 1) * links,)),
            pltpu.SemaphoreType.DMA((max(len(packs), 1) * links,)),
        ],
        input_output_aliases={lead + 2: 0, lead + 3: 1},
        compiler_params=pltpu.CompilerParams(vmem_limit_bytes=ROOM),
        cost_estimate=pl.CostEstimate(flops=0, bytes_accessed=6_000_000, transcendentals=0),
        name="step",
    )(*at, table, *arrived, pool, token, store, refilled)
    boxes = out[2:]
    return out[0], out[1], [list(boxes[i : i + links]) for i in range(0, len(boxes), links)]


def own_kernel(kept, own_takers, table, pool, token, refilled, store, window, in_sem, out_sem):
    for k in range(KEEP):
        source = kept[k]

        @pl.when(source >= 0)
        def _():
            @pl.loop(0, NPAGE, unroll=8)
            def _(p):
                pltpu.make_async_copy(
                    pool.at[table[source * NPAGE + p]], window.at[k, p], in_sem.at[k]
                ).start()

    for k in range(KEEP):
        source = kept[k]

        @pl.when(source >= 0)
        def _():
            pltpu.make_async_copy(window.at[k], window.at[k], in_sem.at[k]).wait()

        for to, lane in ((source, 0), (own_takers[k], 1)):

            @pl.when((source >= 0) & (to >= 0))
            def _():
                @pl.loop(0, NPAGE, unroll=8)
                def _(p):
                    pltpu.make_async_copy(
                        window.at[k, p], refilled.at[table[to * NPAGE + p]], out_sem.at[k, lane]
                    ).start()

    for k in range(KEEP):
        source = kept[k]

        for to, lane in ((source, 0), (own_takers[k], 1)):

            @pl.when((source >= 0) & (to >= 0))
            def _():
                pltpu.make_async_copy(window.at[k], window.at[k], out_sem.at[k, lane]).wait()


def own_windows(kept, own_takers, table, pool, token):
    return pl.pallas_call(
        own_kernel,
        out_shape=[
            jax.ShapeDtypeStruct(pool.shape, pool.dtype),
            jax.ShapeDtypeStruct((NZ * KEEP, NPAGE) + pool.shape[1:], pool.dtype),
        ],
        in_specs=[SMEM] * 3 + [HBM, ANY],
        out_specs=[HBM] * 2,
        scratch_shapes=[
            pltpu.VMEM((KEEP, NPAGE) + pool.shape[1:], pool.dtype),
            pltpu.SemaphoreType.DMA((KEEP,)),
            pltpu.SemaphoreType.DMA((KEEP, 2)),
        ],
        compiler_params=pltpu.CompilerParams(vmem_limit_bytes=ROOM),
        cost_estimate=pl.CostEstimate(flops=0, bytes_accessed=9_000_000, transcendentals=0),
        name="own_windows",
    )(kept, own_takers, table, pool, token)


def attend_kernel(count, who, table, rows, refilled, *refs):
    out, window, row, result, sem, row_sem, out_sem = refs[-7:]
    kv = refilled.shape[2]
    tokens = NPAGE * PAGE * kv
    branch = [who[i] for i in range(count)]
    for i in range(count):

        @pl.when(branch[i] >= 0)
        def _():
            pltpu.make_async_copy(rows.at[branch[i]], row.at[i], row_sem.at[i]).start()

            @pl.loop(0, NPAGE, unroll=8)
            def _(p):
                pltpu.make_async_copy(
                    refilled.at[table[branch[i] * NPAGE + p]], window.at[i, p], sem.at[i]
                ).start()

    for i in range(count):

        @pl.when(branch[i] >= 0)
        def _():
            pltpu.make_async_copy(row.at[i], row.at[i], row_sem.at[i]).wait()
            pltpu.make_async_copy(window.at[i], window.at[i], sem.at[i]).wait()

    @pl.when(functools.reduce(jnp.maximum, branch) >= 0)
    def _():
        flat = [
            window[i, :, :, 0, :].reshape(tokens, 2 * HD)
            if kv == 1
            else window.at[i].reshape(tokens, 2 * HD)
            for i in range(count)
        ]
        query = [row[i, 0] for i in range(count)]
        scores = [
            lax.dot_general(
                query[i], flat[i][:, :HD], (((1,), (1,)), ((), ())), preferred_element_type=jnp.float32
            )
            for i in range(count)
        ]
        token = lax.broadcasted_iota(jnp.int32, scores[0].shape, 1)
        head = lax.broadcasted_iota(jnp.int32, scores[0].shape, 0)
        fits = (token & (kv - 1)) == lax.div(head, H // KVH)
        for i in range(count):
            masked = jnp.where(fits, scores[i], -jnp.inf)
            own = jnp.sum(
                query[i].astype(jnp.float32) * row[i, 1].astype(jnp.float32), -1, keepdims=True
            )
            peak = jnp.maximum(jnp.max(masked, -1, keepdims=True), own)
            terms = jnp.exp(masked - peak)
            own_term = jnp.exp(own - peak)
            total = jnp.sum(terms, -1, keepdims=True) + own_term
            weights = (terms / total).astype(jnp.bfloat16)
            own_weight = (own_term / total).astype(jnp.bfloat16).astype(jnp.float32)
            mixed = jnp.dot(weights, flat[i][:, HD:], preferred_element_type=jnp.float32)
            mixed = mixed + own_weight * row[i, 2].astype(jnp.float32)
            result[i] = mixed.astype(result.dtype)

    for i in range(count):

        @pl.when(branch[i] >= 0)
        def _():
            pltpu.make_async_copy(result.at[i], out.at[branch[i]], out_sem.at[i]).start()

    for i in range(count):

        @pl.when(branch[i] >= 0)
        def _():
            pltpu.make_async_copy(result.at[i], result.at[i], out_sem.at[i]).wait()


def attend(who, table, rows, refilled, before):
    count = who.shape[0]
    heads = rows.shape[2]
    return pl.pallas_call(
        functools.partial(attend_kernel, count),
        out_shape=jax.ShapeDtypeStruct((rows.shape[0], heads, HD), jnp.bfloat16),
        in_specs=[SMEM] * 2 + [ANY, HBM] + [ANY] * len(before),
        out_specs=ANY,
        scratch_shapes=[
            pltpu.VMEM((count, NPAGE) + refilled.shape[1:], refilled.dtype),
            pltpu.VMEM((count, 3, heads, HD), rows.dtype),
            pltpu.VMEM((count, heads, HD), jnp.bfloat16),
            pltpu.SemaphoreType.DMA((count,)),
            pltpu.SemaphoreType.DMA((count,)),
            pltpu.SemaphoreType.DMA((count,)),
        ],
        input_output_aliases={4: 0} if before else {},
        compiler_params=pltpu.CompilerParams(vmem_limit_bytes=ROOM),
        cost_estimate=pl.CostEstimate(
            flops=count * 2 * 2 * 16 * 1536 * 128, bytes_accessed=count * 800_000, transcendentals=0
        ),
        name="attend",
    )(who, table, rows, refilled, *before)


def token_rows(hidden, w_query, w_key, w_value, query_gain, key_gain):
    features = lax.all_gather(hidden, "mp", axis=1, tiled=True)
    branch_count = features.shape[0]
    head_group = H // KVH
    heads = w_query.shape[1] // HD
    kv_local = w_key.shape[1] // HD
    query_full = jnp.dot(features, w_query, preferred_element_type=jnp.float32)
    query_full = query_full.reshape(branch_count, heads, HD)
    query_rows = (normalize(query_full, query_gain) / math.sqrt(HD)).astype(jnp.bfloat16)
    key_full = jnp.dot(features, w_key, preferred_element_type=jnp.float32)
    key_rows = normalize(key_full.reshape(branch_count, kv_local, HD), key_gain).astype(jnp.bfloat16)
    value_rows = jnp.dot(features, w_value, preferred_element_type=jnp.float32)
    value_rows = value_rows.reshape(branch_count, kv_local, HD).astype(jnp.bfloat16)
    return jnp.stack(
        [
            query_rows,
            jnp.repeat(key_rows, head_group, axis=1),
            jnp.repeat(value_rows, head_group, axis=1),
        ],
        axis=1,
    )


def shards(
    hidden, w_query, w_key, w_value, query_gain, key_gain, kv_pool, page_table, parent, surviving
):
    groups = lax.axis_size("dp")
    me = lax.axis_index("dp")
    ny = groups // NZ
    branch_count = hidden.shape[0]
    links = 2 + ny - 1
    packed = first_windows(groups, branch_count, parent, surviving, page_table, kv_pool)
    parent, surviving, page_table, packed = lax.optimization_barrier(
        (parent, surviving, page_table, packed)
    )
    along = [[], []]
    for g in range(groups):
        z = g // ny
        along[0].append((g, g + ny if z % 2 == 0 else g - ny))
        along[1].append((g, g if z in (0, NZ - 1) else g + ny if z % 2 else g - ny))
    pairs = along + [
        [(g, g // ny * ny + (g % ny + shift) % ny) for g in range(groups)] for shift in range(1, ny)
    ]

    def travel(packed):
        return [lax.ppermute(window, "dp", pair) for window, pair in zip(packed, pairs)]

    arrived = travel(packed)
    my_table = lax.dynamic_slice_in_dim(
        page_table, me * branch_count, branch_count, 0
    ).reshape(-1)
    rounds, sends, saves, takers, kept, own_takers = my_tables(
        parent, surviving, groups, branch_count, me
    )
    table = jnp.concatenate([sends, saves, takers, my_table])

    def took(r):
        return lax.dynamic_slice_in_dim(takers, r * links, links, 0)

    refilled, store = own_windows(kept, own_takers, my_table, kv_pool, packed[0])
    rows = token_rows(hidden, w_query, w_key, w_value, query_gain, key_gain)
    first_taker = jnp.max(own_takers)
    other_taker = jnp.max(jnp.where(own_takers == first_taker, -1, own_takers))
    here = jnp.concatenate([kept, jnp.stack([first_taker, other_taker])])
    waiting = [here[:3], here[3:]] + [took(r) for r in range(FIRST)]
    attention = []

    def pieces(r):
        part = NPAGE // PIECES
        return [(r, piece * part, part) for piece in range(PIECES)]

    store, refilled, packed = step(
        links,
        pieces(FIRST),
        [(r, 0, NPAGE) for r in range(FIRST)],
        None,
        table,
        arrived,
        kv_pool,
        rows,
        store,
        refilled,
    )
    moving = [travel(windows) for windows in packed]

    def attend_next(attention):
        who = waiting.pop(0)
        return [attend(who, my_table, rows, refilled, attention)]

    attention = attend_next(attention)
    for r in range(FIRST + 1, PREFIX):
        for pack, file in zip(pieces(r), pieces(r - 1)):
            store, refilled, packed = step(
                links, [pack], [file], None, table, moving.pop(0), kv_pool, attention[0], store, refilled
            )
            moving.append(travel(packed[0]))
        waiting.append(took(r - 1))
        for _ in range(2 if len(waiting) > 1 else 1):
            attention = attend_next(attention)
    for file in pieces(PREFIX - 1):
        store, refilled, _ = step(
            links, [], [file], None, table, moving.pop(0), kv_pool, attention[0], store, refilled
        )
    while waiting:
        attention = attend_next(attention)

    def more(state):
        return state[0] < rounds

    def one_round(state):
        r, store, refilled, attention = state
        moving = []
        for pack in pieces(None):
            store, refilled, packed = step(
                links, [pack], [], r, table, [], kv_pool, attention, store, refilled
            )
            moving.append(travel(packed[0]))
        attention = attend(took(r - 1), my_table, rows, refilled, [attention])
        for file in pieces(None):
            store, refilled, _ = step(
                links, [], [file], r, table, moving.pop(0), kv_pool, attention, store, refilled
            )
        return r + 1, store, refilled, attention

    r, store, refilled, attention = lax.while_loop(
        more, one_round, (jnp.int32(PREFIX), store, refilled, attention[0])
    )
    attention = attend(took(r - 1), my_table, rows, refilled, [attention])
    return (refilled, attention.reshape(branch_count, -1))


def solution(mesh):
    return jax.shard_map(
        shards,
        mesh=mesh,
        in_specs=(
            P("dp", "mp"),
            P(None, "mp"),
            P(None, "mp"),
            P(None, "mp"),
            P(),
            P(),
            P("dp", None, "mp", None),
            P(),
            P(),
            P(),
        ),
        out_specs=(P("dp", None, "mp", None), P("dp", "mp")),
        check_vma=False,
    )
```

```python
import functools
import math

import jax
import jax.numpy as jnp
from jax import lax
from jax.experimental import pallas as pl
from jax.experimental.pallas import tpu as pltpu
from jax.sharding import PartitionSpec as P

H = 64
KVH = 8
HD = 128
PAGE = 16
NPAGE = 48
CAP = 2
KEEP = 4
NZ = 4
ROUNDS = 24
PREFIX = 8
FIRST = 2
REST = 2
PIECES = 2
ROOM = 48 * 1024 * 1024
NEVER = 1 << 20


def normalize(values, gain):
    return values * lax.rsqrt(jnp.mean(values * values, -1, keepdims=True) + 1e-06) * gain


def line_times(need):
    ny = need.shape[1]
    at_z = jnp.any(need, axis=1)
    steps = jnp.arange(NZ)[:, None] - jnp.arange(NZ)[None, :]
    hops = jnp.max(
        jnp.where(at_z & (steps > 0)[:, :, None, None], steps[:, :, None, None], 0), axis=0
    )
    across = need & (jnp.arange(ny)[:, None] != jnp.arange(ny)[None, :])[None, :, None, :, None]
    across = jnp.any(across, axis=1)
    far_across = jnp.any(across & (steps[:, :, None, None] == hops[None]), axis=0)
    rank_key = (hops * 2 + far_across) * KEEP - jnp.arange(KEEP)
    pos = jnp.sum((rank_key[..., None, :] > rank_key[..., :, None]).astype(jnp.int32), axis=-1)
    count = [jnp.sum((hops >= h + 1).astype(jnp.int32), axis=-1) for h in range(NZ - 1)]
    never = jnp.full((ny, KEEP), NEVER, jnp.int32)
    times = []
    starts = {}
    for lz in range(NZ):
        row = []
        begin = None
        for sz in range(lz, -1, -1):
            away = lz - sz
            if away == 0:
                begin = jnp.zeros((ny,), jnp.int32)
            else:
                begin = jnp.maximum(
                    begin + count[away - 1][sz + 1] if lz < NZ - 1 else begin,
                    jnp.maximum(starts[(lz - 1, sz)] + REST, FIRST),
                )
            starts[(lz, sz)] = begin
            if lz == NZ - 1:
                row.append(never)
            else:
                row.append(jnp.where(hops[sz] > away, begin[:, None] + pos[sz], NEVER))
        row = row[::-1] + [never] * (NZ - 1 - lz)
        times.append(jnp.stack(row))
    return jnp.stack(times)


def plan(parent, surviving, groups, branch_count):
    ny = groups // NZ
    alive = (surviving > 0).reshape(groups, branch_count)
    local = jnp.arange(branch_count)
    rank = jnp.sum((alive[:, None, :] & (local[None, :] < local[:, None])[None]).astype(jnp.int32), axis=-1)
    item = (jnp.arange(groups)[:, None] * KEEP + rank).reshape(-1)
    ids = jnp.arange(groups * branch_count)
    item_of_parent = jnp.sum(jnp.where(parent[:, None] == ids[None, :], item[None, :], 0), axis=1)
    wanted = jnp.where(surviving > 0, -1, item_of_parent).reshape(groups, branch_count)
    items = jnp.arange(groups * KEEP)
    child = jnp.max(
        jnp.where(wanted[:, :, None] == items[None, None, :], local[None, :, None], -1), axis=1
    ).reshape(NZ, ny, NZ, ny, KEEP)
    branch = jnp.sum(
        jnp.where(
            alive[:, :, None] & (rank[:, :, None] == jnp.arange(KEEP)[None, None, :]),
            local[None, :, None],
            0,
        ),
        axis=1,
    ).reshape(NZ, ny, KEEP)
    need = child >= 0
    up = line_times(need)
    down = line_times(need[::-1, :, ::-1])[::-1, ::-1]
    here = jnp.arange(NZ)
    from_below = jnp.concatenate([jnp.full_like(up[:1], NEVER), up[:-1]])
    from_above = jnp.concatenate([down[1:], jnp.full_like(down[:1], NEVER)])
    side = (here[:, None] - here[None, :])[:, :, None, None]
    arrival = jnp.where(side > 0, from_below, from_above)
    ready = jnp.where(side == 0, 0, jnp.maximum(arrival + 1, FIRST))
    ready = ready.transpose(0, 2, 1, 3).reshape(NZ, ny, 1, NZ * KEEP)
    crossing = need.transpose(0, 3, 1, 2, 4)
    crossing = crossing & (jnp.arange(ny)[:, None] != jnp.arange(ny)[None, :])[None, :, :, None, None]
    crossing = crossing.reshape(NZ, ny, ny, NZ * KEEP)
    slots = NZ * KEEP
    order = jnp.where(crossing, ready * slots + jnp.arange(slots), NEVER * slots)
    order = jnp.minimum(order, NEVER)
    before = jnp.sum((order[..., None, :] < order[..., :, None]).astype(jnp.int32), axis=-1)
    lead = jnp.where(crossing, ready - before, -NEVER)
    run = jnp.max(
        jnp.where(order[..., None, :] <= order[..., :, None], lead[..., None, :], -NEVER), axis=-1
    )
    cross = jnp.where(crossing, run + before, NEVER).reshape(NZ, ny, ny, NZ, KEEP)
    return child, branch, up, down, cross


def last_round(*times):
    ends = [jnp.max(jnp.where(t < NEVER, t, -1)) for t in times]
    return functools.reduce(jnp.maximum, ends) + 1


def my_tables(parent, surviving, groups, branch_count, me):
    ny = groups // NZ
    child, branch, up, down, cross = plan(parent, surviving, groups, branch_count)
    rounds = last_round(up, down, cross)
    z, y = me // ny, me % ny

    def pick(array, *index):
        for i in index:
            array = lax.dynamic_index_in_dim(array, i, 0, keepdims=False)
        return array

    def line(times, lz):
        padded = jnp.concatenate(
            [jnp.full_like(times[:1], NEVER), times, jnp.full_like(times[:1], NEVER)]
        )
        mine = pick(padded, lz + 1)
        return lax.dynamic_index_in_dim(mine, y, 1, keepdims=False).reshape(-1)

    round_ids = jnp.arange(ROUNDS)

    def table(times, values):
        hit = times[None, :] == round_ids[:, None]
        return jnp.sum(jnp.where(hit, values[None, :] + 1, 0), axis=1) - 1

    slots = NZ * KEEP
    slot_ids = jnp.arange(slots)
    own = (slot_ids // KEEP) == z
    own_branch = pick(branch, z, y)
    source = jnp.where(own, slots + own_branch[slot_ids % KEEP], slot_ids)
    takers_of = pick(child, z, y)

    def takers_on(line_y):
        return lax.dynamic_index_in_dim(takers_of, line_y, 1, keepdims=False).reshape(-1)

    def taker_table(times, line_y):
        return table(times, takers_on(line_y))

    even = z % 2 == 0
    out_up, out_down = line(up, z), line(down, z)
    in_up, in_down = line(up, z - 1), line(down, z + 1)
    outs = [jnp.where(even, out_up, out_down), jnp.where(even, out_down, out_up)]
    ins = [jnp.where(even, in_down, in_up), jnp.where(even, in_up, in_down)]
    sends = [table(times, source) for times in outs]
    saves = [table(times, slot_ids) for times in ins]
    takers = [taker_table(times, y) for times in ins]
    for shift in range(1, ny):
        y_to, y_from = (y + shift) % ny, (y + ny - shift) % ny
        sends.append(table(pick(cross, z, y, y_to).reshape(-1), source))
        takers.append(taker_table(pick(cross, z, y_from, y).reshape(-1), y_from))
    own_takers = lax.dynamic_index_in_dim(takers_on(y).reshape(NZ, KEEP), z, 0, keepdims=False)
    alive = lax.dynamic_index_in_dim(
        (surviving > 0).reshape(groups, branch_count), me, 0, keepdims=False
    )
    kept = jnp.where(jnp.arange(KEEP) < jnp.sum(alive.astype(jnp.int32)), own_branch, -1)
    return (
        rounds,
        jnp.stack(sends, 1).reshape(-1),
        jnp.stack(saves, 1).reshape(-1),
        jnp.stack(takers, 1).reshape(-1),
        kept,
        own_takers,
    )


SMEM = pl.BlockSpec(memory_space=pltpu.SMEM)
VMEM = pl.BlockSpec(memory_space=pltpu.VMEM)
HBM = pl.BlockSpec(memory_space=pltpu.HBM)
ANY = pl.BlockSpec(memory_space=pl.ANY)


def first_kernel(groups, branch_count, parent, surviving, page_table, pool, *refs):
    ny = groups // NZ
    packed, sem = refs[:-1], refs[-1]
    me = lax.axis_index("dp")
    z, y = me // ny, me % ny
    shape = (branch_count, groups * branch_count)
    child = lax.broadcasted_iota(jnp.int32, shape, 1)
    local = lax.broadcasted_iota(jnp.int32, shape, 0)
    column = lax.broadcasted_iota(jnp.int32, (branch_count, 1), 0)
    mine = (surviving[...] == 0) & (parent[...] == me * branch_count + local)
    target = lax.div(child, branch_count)
    target_z = lax.div(target, ny)
    target_y = target - target_z * ny

    def seen(mask):
        return jnp.max(mask.astype(jnp.int32), axis=1, keepdims=True)

    def leading(key):
        rows = []
        for _ in range(FIRST):
            best = jnp.max(key)
            rows.append(
                jnp.where(best >= 0, branch_count - 1 - lax.rem(best, branch_count), -1)
            )
            key = jnp.where(key == best, -1, key)
        return rows

    ways = []
    for steps in (target_z - z, z - target_z):
        hops = jnp.max(jnp.where(mine, steps, 0), axis=1, keepdims=True)
        far_across = seen(mine & (steps == hops) & (target_y != y))
        key = (hops * 2 + far_across) * branch_count + branch_count - 1 - column
        ways.append(leading(jnp.where(hops > 0, key, -1)))
    even = lax.rem(z, 2) == 0
    sends = [
        [jnp.where(even, u, d) for u, d in zip(*ways)],
        [jnp.where(even, d, u) for u, d in zip(*ways)],
    ]
    for shift in range(1, ny):
        to = lax.rem(y + shift, ny)
        crossing = seen(mine & (target_z == z) & (target_y == to))
        sends.append(leading(jnp.where(crossing > 0, branch_count - 1 - column, -1)))
    for l, rows in enumerate(sends):
        for r, row in enumerate(rows):

            @pl.when(row >= 0)
            def _():
                @pl.loop(0, NPAGE, unroll=8)
                def _(p):
                    page = page_table[p, me * branch_count + row]
                    pltpu.make_async_copy(
                        pool.at[page], packed[l].at[r * NPAGE + p], sem.at[l, r]
                    ).start()

    for l, rows in enumerate(sends):
        for r, row in enumerate(rows):
            box = packed[l].at[pl.ds(r * NPAGE, NPAGE)]

            @pl.when(row >= 0)
            def _():
                pltpu.make_async_copy(box, box, sem.at[l, r]).wait()


def first_windows(groups, branch_count, parent, surviving, page_table, pool):
    links = 2 + groups // NZ - 1
    windows = jax.ShapeDtypeStruct((FIRST * NPAGE,) + pool.shape[1:], pool.dtype)
    return pl.pallas_call(
        functools.partial(first_kernel, groups, branch_count),
        out_shape=[windows] * links,
        in_specs=[VMEM] * 2 + [SMEM, HBM],
        out_specs=[VMEM] * links,
        scratch_shapes=[pltpu.SemaphoreType.DMA((links, FIRST))],
        compiler_params=pltpu.CompilerParams(vmem_limit_bytes=ROOM),
        cost_estimate=pl.CostEstimate(flops=0, bytes_accessed=6_000_000, transcendentals=0),
        name="first_windows",
    )(parent.reshape(1, -1), surviving.reshape(1, -1), page_table.T, pool)


def step_kernel(links, packs, files, traced, count, *refs):
    if traced:
        at, refs = refs[0][0], refs[1:]
        packs = [(at,) + entry[1:] for entry in packs]
        files = [(at,) + entry[1:] for entry in files]
    table = refs[0]
    arrived = refs[1 : 1 + count]
    pool = refs[1 + count]
    store, refilled = refs[5 + count : 7 + count]
    packed = refs[7 + count : -4]
    file_sem, save_sem, pack_sem, fresh_sem = refs[-4:]
    slots = NZ * KEEP
    saves_at = ROUNDS * links
    takers_at = saves_at + ROUNDS * 2
    pages_at = takers_at + ROUNDS * links

    comes = []
    for r, l, first, pages, kept, array, offset in files:
        part = arrived[array].at[pl.ds(offset, pages)]
        save = table[saves_at + r * 2 + l] if l < 2 else None
        comes.append((save, table[takers_at + r * links + l], part, first, pages, kept))

    def is_fresh(source):
        fresh = [source == save for save, _, _, _, _, _ in comes if save is not None]
        return (source >= 0) & functools.reduce(jnp.logical_or, fresh) if fresh else False

    goes = []
    for r, first, pages, which in packs:
        for l in which:
            goes.append((table[r * links + l], packed[len(goes)], first, pages))

    for i, (source, box, first, pages) in enumerate(goes):

        @pl.when(source >= slots)
        def _():
            @pl.loop(0, pages, unroll=8)
            def _(p):
                page = table[pages_at + (source - slots) * NPAGE + first + p]
                pltpu.make_async_copy(pool.at[page], box.at[p], pack_sem.at[i]).start()

        @pl.when((source >= 0) & (source < slots) & jnp.logical_not(is_fresh(source)))
        def _():
            pltpu.make_async_copy(
                store.at[jnp.clip(source, 0, slots - 1), pl.ds(first, pages)],
                box,
                pack_sem.at[i],
            ).start()

        for save, _, part, file_first, file_pages, _ in comes:
            if save is not None and file_first <= first < file_first + file_pages:

                @pl.when((source >= 0) & (source == save))
                def _():
                    pltpu.make_async_copy(
                        part.at[pl.ds(first - file_first, pages)], box, fresh_sem.at[i]
                    ).start()

    for i, (save, taker, part, first, pages, kept) in enumerate(comes):
        if kept and save is not None:

            @pl.when(save >= 0)
            def _():
                pltpu.make_async_copy(
                    part, store.at[jnp.maximum(save, 0), pl.ds(first, pages)], save_sem.at[i]
                ).start()

        if kept:

            @pl.when(taker >= 0)
            def _():
                @pl.loop(0, pages, unroll=8)
                def _(p):
                    page = table[pages_at + taker * NPAGE + first + p]
                    pltpu.make_async_copy(part.at[p], refilled.at[page], file_sem.at[i]).start()

    for i, (source, box, first, pages) in enumerate(goes):

        @pl.when((source >= 0) & jnp.logical_not(is_fresh(source)))
        def _():
            pltpu.make_async_copy(box, box, pack_sem.at[i]).wait()

        if comes:

            @pl.when(is_fresh(source))
            def _():
                pltpu.make_async_copy(box, box, fresh_sem.at[i]).wait()

    for i, (save, taker, part, first, pages, kept) in enumerate(comes):
        if kept and save is not None:

            @pl.when(save >= 0)
            def _():
                pltpu.make_async_copy(part, part, save_sem.at[i]).wait()

        if kept:

            @pl.when(taker >= 0)
            def _():
                pltpu.make_async_copy(part, part, file_sem.at[i]).wait()


def step(links, packs, files, at, table, arrived, pool, token, store, refilled):
    at = [] if at is None else [jnp.stack([at])]
    count = len(arrived)
    lead = len(at) + 1 + count
    boxes = [
        jax.ShapeDtypeStruct((pages,) + pool.shape[1:], pool.dtype)
        for _, _, pages, which in packs
        for _ in which
    ]
    out = pl.pallas_call(
        functools.partial(step_kernel, links, packs, files, bool(at), count),
        out_shape=[
            jax.ShapeDtypeStruct(store.shape, store.dtype),
            jax.ShapeDtypeStruct(refilled.shape, refilled.dtype),
        ]
        + boxes,
        in_specs=[SMEM] * (len(at) + 1) + [VMEM] * count + [HBM, ANY, HBM, HBM],
        out_specs=[HBM] * 2 + [VMEM] * len(boxes),
        scratch_shapes=[
            pltpu.SemaphoreType.DMA((max(len(files), 1),)),
            pltpu.SemaphoreType.DMA((max(len(files), 1),)),
            pltpu.SemaphoreType.DMA((max(len(boxes), 1),)),
            pltpu.SemaphoreType.DMA((max(len(boxes), 1),)),
        ],
        input_output_aliases={lead + 2: 0, lead + 3: 1},
        compiler_params=pltpu.CompilerParams(vmem_limit_bytes=ROOM),
        cost_estimate=pl.CostEstimate(flops=0, bytes_accessed=6_000_000, transcendentals=0),
        name="step",
    )(*at, table, *arrived, pool, token, store, refilled)
    return out[0], out[1], list(out[2:])


def own_kernel(kept, own_takers, table, pool, token, refilled, store, window, in_sem, out_sem):
    for k in range(KEEP):
        source = kept[k]

        @pl.when(source >= 0)
        def _():
            @pl.loop(0, NPAGE, unroll=8)
            def _(p):
                pltpu.make_async_copy(
                    pool.at[table[source * NPAGE + p]], window.at[k, p], in_sem.at[k]
                ).start()

    for k in range(KEEP):
        source = kept[k]

        @pl.when(source >= 0)
        def _():
            pltpu.make_async_copy(window.at[k], window.at[k], in_sem.at[k]).wait()

        for to, lane in ((source, 0), (own_takers[k], 1)):

            @pl.when((source >= 0) & (to >= 0))
            def _():
                @pl.loop(0, NPAGE, unroll=8)
                def _(p):
                    pltpu.make_async_copy(
                        window.at[k, p], refilled.at[table[to * NPAGE + p]], out_sem.at[k, lane]
                    ).start()

    for k in range(KEEP):
        source = kept[k]

        for to, lane in ((source, 0), (own_takers[k], 1)):

            @pl.when((source >= 0) & (to >= 0))
            def _():
                pltpu.make_async_copy(window.at[k], window.at[k], out_sem.at[k, lane]).wait()


def own_windows(kept, own_takers, table, pool, token):
    return pl.pallas_call(
        own_kernel,
        out_shape=[
            jax.ShapeDtypeStruct(pool.shape, pool.dtype),
            jax.ShapeDtypeStruct((NZ * KEEP, NPAGE) + pool.shape[1:], pool.dtype),
        ],
        in_specs=[SMEM] * 3 + [HBM, ANY],
        out_specs=[HBM] * 2,
        scratch_shapes=[
            pltpu.VMEM((KEEP, NPAGE) + pool.shape[1:], pool.dtype),
            pltpu.SemaphoreType.DMA((KEEP,)),
            pltpu.SemaphoreType.DMA((KEEP, 2)),
        ],
        compiler_params=pltpu.CompilerParams(vmem_limit_bytes=ROOM),
        cost_estimate=pl.CostEstimate(flops=0, bytes_accessed=9_000_000, transcendentals=0),
        name="own_windows",
    )(kept, own_takers, table, pool, token)


def attend_kernel(count, who, table, rows, refilled, *refs):
    out, window, row, result, sem, row_sem, out_sem = refs[-7:]
    kv = refilled.shape[2]
    tokens = NPAGE * PAGE * kv
    branch = [who[i] for i in range(count)]
    for i in range(count):

        @pl.when(branch[i] >= 0)
        def _():
            pltpu.make_async_copy(rows.at[branch[i]], row.at[i], row_sem.at[i]).start()

            @pl.loop(0, NPAGE, unroll=8)
            def _(p):
                pltpu.make_async_copy(
                    refilled.at[table[branch[i] * NPAGE + p]], window.at[i, p], sem.at[i]
                ).start()

    for i in range(count):

        @pl.when(branch[i] >= 0)
        def _():
            pltpu.make_async_copy(row.at[i], row.at[i], row_sem.at[i]).wait()
            pltpu.make_async_copy(window.at[i], window.at[i], sem.at[i]).wait()

    @pl.when(functools.reduce(jnp.maximum, branch) >= 0)
    def _():
        flat = [
            window[i, :, :, 0, :].reshape(tokens, 2 * HD)
            if kv == 1
            else window.at[i].reshape(tokens, 2 * HD)
            for i in range(count)
        ]
        query = [row[i, 0] for i in range(count)]
        scores = [
            lax.dot_general(
                query[i], flat[i][:, :HD], (((1,), (1,)), ((), ())), preferred_element_type=jnp.float32
            )
            for i in range(count)
        ]
        token = lax.broadcasted_iota(jnp.int32, scores[0].shape, 1)
        head = lax.broadcasted_iota(jnp.int32, scores[0].shape, 0)
        fits = (token & (kv - 1)) == lax.div(head, H // KVH)
        for i in range(count):
            masked = jnp.where(fits, scores[i], -jnp.inf)
            own = jnp.sum(
                query[i].astype(jnp.float32) * row[i, 1].astype(jnp.float32), -1, keepdims=True
            )
            peak = jnp.maximum(jnp.max(masked, -1, keepdims=True), own)
            terms = jnp.exp(masked - peak)
            own_term = jnp.exp(own - peak)
            total = jnp.sum(terms, -1, keepdims=True) + own_term
            weights = (terms / total).astype(jnp.bfloat16)
            own_weight = (own_term / total).astype(jnp.bfloat16).astype(jnp.float32)
            mixed = jnp.dot(weights, flat[i][:, HD:], preferred_element_type=jnp.float32)
            mixed = mixed + own_weight * row[i, 2].astype(jnp.float32)
            result[i] = mixed.astype(result.dtype)

    for i in range(count):

        @pl.when(branch[i] >= 0)
        def _():
            pltpu.make_async_copy(result.at[i], out.at[branch[i]], out_sem.at[i]).start()

    for i in range(count):

        @pl.when(branch[i] >= 0)
        def _():
            pltpu.make_async_copy(result.at[i], result.at[i], out_sem.at[i]).wait()


def attend(who, table, rows, refilled, before):
    count = who.shape[0]
    heads = rows.shape[2]
    return pl.pallas_call(
        functools.partial(attend_kernel, count),
        out_shape=jax.ShapeDtypeStruct((rows.shape[0], heads, HD), jnp.bfloat16),
        in_specs=[SMEM] * 2 + [ANY, HBM] + [ANY] * len(before),
        out_specs=ANY,
        scratch_shapes=[
            pltpu.VMEM((count, NPAGE) + refilled.shape[1:], refilled.dtype),
            pltpu.VMEM((count, 3, heads, HD), rows.dtype),
            pltpu.VMEM((count, heads, HD), jnp.bfloat16),
            pltpu.SemaphoreType.DMA((count,)),
            pltpu.SemaphoreType.DMA((count,)),
            pltpu.SemaphoreType.DMA((count,)),
        ],
        input_output_aliases={4: 0} if before else {},
        compiler_params=pltpu.CompilerParams(vmem_limit_bytes=ROOM),
        cost_estimate=pl.CostEstimate(
            flops=count * 2 * 2 * 16 * 1536 * 128, bytes_accessed=count * 800_000, transcendentals=0
        ),
        name="attend",
    )(who, table, rows, refilled, *before)


def token_rows(hidden, w_query, w_key, w_value, query_gain, key_gain):
    features = lax.all_gather(hidden, "mp", axis=1, tiled=True)
    branch_count = features.shape[0]
    head_group = H // KVH
    heads = w_query.shape[1] // HD
    kv_local = w_key.shape[1] // HD
    query_full = jnp.dot(features, w_query, preferred_element_type=jnp.float32)
    query_full = query_full.reshape(branch_count, heads, HD)
    query_rows = (normalize(query_full, query_gain) / math.sqrt(HD)).astype(jnp.bfloat16)
    key_full = jnp.dot(features, w_key, preferred_element_type=jnp.float32)
    key_rows = normalize(key_full.reshape(branch_count, kv_local, HD), key_gain).astype(jnp.bfloat16)
    value_rows = jnp.dot(features, w_value, preferred_element_type=jnp.float32)
    value_rows = value_rows.reshape(branch_count, kv_local, HD).astype(jnp.bfloat16)
    return jnp.stack(
        [
            query_rows,
            jnp.repeat(key_rows, head_group, axis=1),
            jnp.repeat(value_rows, head_group, axis=1),
        ],
        axis=1,
    )


def shards(
    hidden, w_query, w_key, w_value, query_gain, key_gain, kv_pool, page_table, parent, surviving
):
    groups = lax.axis_size("dp")
    me = lax.axis_index("dp")
    ny = groups // NZ
    branch_count = hidden.shape[0]
    links = 2 + ny - 1
    packed = first_windows(groups, branch_count, parent, surviving, page_table, kv_pool)
    parent, surviving, page_table, packed = lax.optimization_barrier(
        (parent, surviving, page_table, packed)
    )
    sides = lax.axis_size("mp")

    def everywhere(move):
        return [
            (g * sides + m, to[0] * sides + to[1])
            for g in range(groups)
            for m in range(sides)
            for to in [move(g, m)]
        ]

    def outer(g, m):
        return g + ny if g // ny % 2 == 0 else g - ny, m

    def inner(g, m):
        if g // ny in (0, NZ - 1):
            return g, m ^ 1
        return g + ny if g // ny % 2 else g - ny, m

    def sideways(shift):
        return lambda g, m: (g // ny * ny + (g % ny + shift) % ny, m)

    pairs = [everywhere(outer), everywhere(inner)]
    pairs += [everywhere(sideways(shift)) for shift in range(1, ny)]
    along, beside, every = [0, 1], list(range(2, links)), list(range(links))

    def travel(packed, which):
        return [lax.ppermute(window, ("dp", "mp"), pairs[l]) for window, l in zip(packed, which)]

    arrived = travel(packed, every)
    my_table = lax.dynamic_slice_in_dim(
        page_table, me * branch_count, branch_count, 0
    ).reshape(-1)
    rounds, sends, saves, takers, kept, own_takers = my_tables(
        parent, surviving, groups, branch_count, me
    )
    table = jnp.concatenate([sends, saves, takers, my_table])

    def took(r):
        return lax.dynamic_slice_in_dim(takers, r * links, links, 0)

    refilled, store = own_windows(kept, own_takers, my_table, kv_pool, packed[0])
    rows = token_rows(hidden, w_query, w_key, w_value, query_gain, key_gain)
    first_taker = jnp.max(own_takers)
    other_taker = jnp.max(jnp.where(own_takers == first_taker, -1, own_takers))
    here = jnp.concatenate([kept, jnp.stack([first_taker, other_taker])])
    waiting = [here[:3], here[3:]]
    attention = []

    def attend_next(attention):
        return [attend(waiting.pop(0), my_table, rows, refilled, attention)]

    came = arrived
    past = list(range(FIRST))
    next_along = None
    for r in range(FIRST, PREFIX):
        files = [
            (at, l, 0, NPAGE, True, l, i * NPAGE) for i, at in enumerate(past) for l in every
        ]
        fresh = [entry[:4] + (False,) + entry[5:] for entry in files if entry[1] in along]
        token = attention[0] if attention else rows
        moved = [] if next_along is None else travel(next_along, along)
        which = every if next_along is None else beside
        store, refilled, packed = step(
            links,
            [(r, 0, NPAGE, which)],
            fresh,
            None,
            table,
            came[:2],
            kv_pool,
            token,
            store,
            refilled,
        )
        moved += travel(packed, which)
        store, refilled, next_along = step(
            links,
            [(r + 1, 0, NPAGE, along)] if r + 1 < PREFIX else [],
            files,
            None,
            table,
            came,
            kv_pool,
            token,
            store,
            refilled,
        )
        waiting += [took(at) for at in past]
        for _ in range(2 if len(waiting) > 1 else 1):
            attention = attend_next(attention)
        came, past = moved, [r]
    store, refilled, _ = step(
        links,
        [],
        [(PREFIX - 1, l, 0, NPAGE, True, l, 0) for l in every],
        None,
        table,
        came,
        kv_pool,
        attention[0],
        store,
        refilled,
    )
    while waiting:
        attention = attend_next(attention)

    def more(state):
        return state[0] < rounds

    def one_round(state):
        r, store, refilled, attention = state
        part = NPAGE // PIECES
        moving = []
        for piece in range(PIECES):
            store, refilled, packed = step(
                links, [(None, piece * part, part, every)], [], r, table, [], kv_pool, attention, store, refilled
            )
            moving.append(travel(packed, every))
        attention = attend(took(r - 1), my_table, rows, refilled, [attention])
        for piece in range(PIECES):
            store, refilled, _ = step(
                links,
                [],
                [(None, l, piece * part, part, True, l, 0) for l in every],
                r,
                table,
                moving.pop(0),
                kv_pool,
                attention,
                store,
                refilled,
            )
        return r + 1, store, refilled, attention

    r, store, refilled, attention = lax.while_loop(
        more, one_round, (jnp.int32(PREFIX), store, refilled, attention[0])
    )
    attention = attend(took(r - 1), my_table, rows, refilled, [attention])
    return (refilled, attention.reshape(branch_count, -1))


def solution(mesh):
    return jax.shard_map(
        shards,
        mesh=mesh,
        in_specs=(
            P("dp", "mp"),
            P(None, "mp"),
            P(None, "mp"),
            P(None, "mp"),
            P(),
            P(),
            P("dp", None, "mp", None),
            P(),
            P(),
            P(),
        ),
        out_specs=(P("dp", None, "mp", None), P("dp", "mp")),
        check_vma=False,
    )
```

```python
import functools
import math

import jax
import jax.numpy as jnp
from jax import lax
from jax.experimental import pallas as pl
from jax.experimental.pallas import tpu as pltpu
from jax.sharding import PartitionSpec as P

H = 64
KVH = 8
HD = 128
PAGE = 16
NPAGE = 48
CAP = 2
KEEP = 4
NZ = 4
ROUNDS = 40
LANES = 128
PREFIX = 8
FIRST = 2
REST = 2
PIECES = 2
ROOM = 48 * 1024 * 1024
NEVER = 1 << 20


def normalize(values, gain):
    return values * lax.rsqrt(jnp.mean(values * values, -1, keepdims=True) + 1e-06) * gain


def plan_kernel(groups, branch_count, parent_row, alive_row, parent_column, alive_column, out, state):
    ny = groups // NZ
    branches = groups * branch_count
    shifts = list(range(1, ny))
    slots = NZ * KEEP
    me = lax.axis_index("dp")

    def iota(shape, axis):
        return lax.broadcasted_iota(jnp.int32, shape, axis)

    square = (branches, branches)
    down_ids, across_ids = iota(square, 0), iota(square, 1)
    same = lax.div(down_ids, branch_count) == lax.div(across_ids, branch_count)
    alive_r, alive_c = alive_row[...] > 0, alive_column[...] > 0
    before = jnp.where(same & (down_ids < across_ids) & alive_c, 1, 0)
    item_row = jnp.sum(before, axis=0, keepdims=True)
    item_row = item_row + lax.div(iota((1, branches), 1), branch_count) * KEEP
    before = jnp.where(same & (across_ids < down_ids) & alive_r, 1, 0)
    item_column = jnp.sum(before, axis=1, keepdims=True)
    item_column = item_column + lax.div(iota((branches, 1), 0), branch_count) * KEEP
    wanted = jnp.sum(
        jnp.where(parent_column[...] == across_ids, item_row, 0), axis=1, keepdims=True
    )
    wanted = jnp.where(alive_c, -1, wanted)
    wide = (branches, LANES)
    local = lax.rem(iota(wide, 0), branch_count)
    takes = jnp.where(wanted == iota(wide, 1), local, -1)
    child = jnp.max(takes.reshape(groups, branch_count, LANES), axis=1)
    holds = jnp.where((item_column == iota(wide, 1)) & alive_c, local, -1)
    branch = jnp.max(holds, axis=0, keepdims=True)

    shape = (groups, LANES)
    here, item = iota(shape, 0), iota(shape, 1)
    z, y = lax.div(here, ny), lax.rem(here, ny)
    source = lax.div(item, KEEP)
    item_z, item_y = lax.div(source, ny), lax.rem(source, ny)
    on_line = item_y == y
    need = child >= 0

    def across(mask):
        return jnp.max(jnp.where(mask, 1, 0), axis=0, keepdims=True)

    top = jnp.max(jnp.where(need, z, -1), axis=0, keepdims=True)
    bottom = jnp.min(jnp.where(need, z, NZ), axis=0, keepdims=True)
    top_crosses = across(need & (z == top) & (item_y != y))
    bottom_crosses = across(need & (z == bottom) & (item_y != y))
    tie = LANES - 1 - item
    up_hops, down_hops = jnp.maximum(top - z, 0), jnp.maximum(z - bottom, 0)
    up_key = (up_hops * 2 + top_crosses) * LANES + tie
    down_key = (down_hops * 2 + bottom_crosses) * LANES + tie
    go_up, go_down = on_line & (up_hops > 0), on_line & (down_hops > 0)

    def beside(x, shift):
        return jnp.where(
            y + shift < ny, pltpu.roll(x, groups - shift, 0), pltpu.roll(x, (ny - shift) % groups, 0)
        )

    crosses = [on_line & (beside(child, shift) >= 0) for shift in shifts]
    own = source == here
    start = [go_up & own, go_down & own] + [c & own for c in crosses]
    rows = len(start)
    for i, mask in enumerate(start):
        state[i] = jnp.where(mask, 0, NEVER)
        state[rows + i] = jnp.full(shape, -1, jnp.int32)

    def choose(i, r, key):
        ready = state[i]
        key = jnp.where(ready <= r, key(ready), -1)
        best = jnp.max(key, axis=1, keepdims=True)
        chosen = (key == best) & (best >= 0)
        state[i] = jnp.where(chosen, NEVER, ready)
        state[rows + i] = jnp.where(chosen, r, state[rows + i])
        return jnp.where(chosen, 1, 0)

    def one_round(r):
        ups = choose(0, r, lambda ready: up_key)
        downs = choose(1, r, lambda ready: down_key)
        for i in range(2, rows):
            choose(i, r, lambda ready: (ROUNDS - ready) * LANES + tie)
        ups = jnp.where(z > 0, pltpu.roll(ups, ny, 0), 0) > 0
        downs = jnp.where(z < NZ - 1, pltpu.roll(downs, groups - ny, 0), 0) > 0
        rested = jnp.where(r < FIRST, FIRST, r + REST)
        state[0] = jnp.where(ups & go_up, rested, state[0])
        state[1] = jnp.where(downs & go_down, rested, state[1])
        left = jnp.minimum(state[0], state[1])
        for i, cross in enumerate(crosses):
            there = jnp.where((ups | downs) & cross, jnp.maximum(r + 1, FIRST), state[2 + i])
            state[2 + i] = there
            left = jnp.minimum(left, there)
        return r + 1, jnp.min(left)

    rounds, _ = lax.while_loop(
        lambda carry: (carry[1] < NEVER) & (carry[0] < ROUNDS),
        lambda carry: one_round(carry[0]),
        (jnp.int32(0), jnp.int32(0)),
    )

    def row_of(x, group):
        return jnp.max(jnp.where(here == group, x, -1), axis=0, keepdims=True)

    my_z = lax.div(me, ny)
    my_y = me - my_z * ny
    even = lax.rem(my_z, 2) == 0
    item = iota((1, LANES), 1)
    group = lax.div(item, KEEP)
    slot = lax.div(group, ny) * KEEP + lax.rem(item, KEEP)
    value = jnp.where(group == me, slots + branch, slot)
    taker = row_of(child, me)
    up_out, down_out = row_of(state[rows], me), row_of(state[rows + 1], me)
    up_in, down_in = row_of(state[rows], me - ny), row_of(state[rows + 1], me + ny)
    outs = [jnp.where(even, up_out, down_out), jnp.where(even, down_out, up_out)]
    ins = [jnp.where(even, down_in, up_in), jnp.where(even, up_in, down_in)]
    for shift in shifts:
        outs.append(row_of(state[rows + 1 + shift], me))
        from_y = lax.rem(my_y + ny - shift, ny)
        ins.append(row_of(state[rows + 1 + shift], my_z * ny + from_y))
    table = [(times, value) for times in outs]
    table += [(times, slot) for times in ins[:2]]
    table += [(times, taker) for times in ins]
    at = iota((ROUNDS, LANES), 0)
    lane = iota((ROUNDS, LANES), 1)
    result = jnp.full((ROUNDS, LANES), -1, jnp.int32)
    for c, (times, values) in enumerate(table):
        column = jnp.max(jnp.where(times == at, values, -1), axis=1, keepdims=True)
        result = jnp.where(lane == c, column, result)
    out[pl.ds(0, ROUNDS), :] = result
    extra = iota((8, LANES), 0)
    out[pl.ds(ROUNDS, 8), :] = jnp.where(
        extra == 0, rounds, jnp.where(extra == 1, branch, jnp.where(extra == 2, taker, 0))
    )


class Plan:
    def __init__(self, links, groups, branch_count):
        self.links = links
        self.width = 2 * links + 2
        self.rounds_at = ROUNDS * self.width
        self.branch_at = self.rounds_at + 1
        self.taker_at = self.branch_at + groups * KEEP
        self.pages_at = self.taker_at + groups * KEEP

    def send(self, table, r, l):
        return table[r * self.width + l]

    def save(self, table, r, l):
        return table[r * self.width + self.links + l]

    def taker(self, table, r, l):
        return table[r * self.width + self.links + 2 + l]

    def page(self, table, branch, p):
        return table[self.pages_at + branch * NPAGE + p]

    def kept(self, table, k):
        return table[self.branch_at + lax.axis_index("dp") * KEEP + k]

    def own_taker(self, table, k):
        return table[self.taker_at + lax.axis_index("dp") * KEEP + k]


def routing(parent, surviving, page_table, groups, branch_count, links):
    ny = groups // NZ
    rows = 2 + ny - 1
    out = pl.pallas_call(
        functools.partial(plan_kernel, groups, branch_count),
        out_shape=jax.ShapeDtypeStruct((ROUNDS + 8, LANES), jnp.int32),
        in_specs=[VMEM] * 4,
        out_specs=VMEM,
        scratch_shapes=[pltpu.VMEM((2 * rows, groups, LANES), jnp.int32)],
        compiler_params=pltpu.CompilerParams(vmem_limit_bytes=ROOM),
        cost_estimate=pl.CostEstimate(flops=0, bytes_accessed=6_000_000, transcendentals=0),
        name="plan",
    )(
        parent.reshape(1, -1),
        surviving.reshape(1, -1),
        parent.reshape(-1, 1),
        surviving.reshape(-1, 1),
    )
    pages = lax.dynamic_slice_in_dim(
        page_table, lax.axis_index("dp") * branch_count, branch_count, 0
    )
    items = groups * KEEP
    return jnp.concatenate(
        [
            out[:ROUNDS, : 2 * links + 2].reshape(-1),
            out[ROUNDS, :1],
            out[ROUNDS + 1, :items],
            out[ROUNDS + 2, :items],
            pages.reshape(-1),
        ]
    )


SMEM = pl.BlockSpec(memory_space=pltpu.SMEM)
VMEM = pl.BlockSpec(memory_space=pltpu.VMEM)
HBM = pl.BlockSpec(memory_space=pltpu.HBM)
ANY = pl.BlockSpec(memory_space=pl.ANY)


def first_kernel(groups, branch_count, parent, surviving, page_table, pool, *refs):
    ny = groups // NZ
    packed, sem = refs[:-1], refs[-1]
    me = lax.axis_index("dp")
    z, y = me // ny, me % ny
    shape = (branch_count, groups * branch_count)
    child = lax.broadcasted_iota(jnp.int32, shape, 1)
    local = lax.broadcasted_iota(jnp.int32, shape, 0)
    column = lax.broadcasted_iota(jnp.int32, (branch_count, 1), 0)
    mine = (surviving[...] == 0) & (parent[...] == me * branch_count + local)
    target = lax.div(child, branch_count)
    target_z = lax.div(target, ny)
    target_y = target - target_z * ny

    def seen(mask):
        return jnp.max(mask.astype(jnp.int32), axis=1, keepdims=True)

    def leading(key):
        rows = []
        for _ in range(FIRST):
            best = jnp.max(key)
            rows.append(
                jnp.where(best >= 0, branch_count - 1 - lax.rem(best, branch_count), -1)
            )
            key = jnp.where(key == best, -1, key)
        return rows

    ways = []
    for steps in (target_z - z, z - target_z):
        hops = jnp.max(jnp.where(mine, steps, 0), axis=1, keepdims=True)
        far_across = seen(mine & (steps == hops) & (target_y != y))
        key = (hops * 2 + far_across) * branch_count + branch_count - 1 - column
        ways.append(leading(jnp.where(hops > 0, key, -1)))
    even = lax.rem(z, 2) == 0
    sends = [
        [jnp.where(even, u, d) for u, d in zip(*ways)],
        [jnp.where(even, d, u) for u, d in zip(*ways)],
    ]
    for shift in range(1, ny):
        to = lax.rem(y + shift, ny)
        crossing = seen(mine & (target_z == z) & (target_y == to))
        sends.append(leading(jnp.where(crossing > 0, branch_count - 1 - column, -1)))
    for l, rows in enumerate(sends):
        for r, row in enumerate(rows):

            @pl.when(row >= 0)
            def _():
                @pl.loop(0, NPAGE, unroll=8)
                def _(p):
                    page = page_table[p, me * branch_count + row]
                    pltpu.make_async_copy(
                        pool.at[page], packed[l].at[r * NPAGE + p], sem.at[l, r]
                    ).start()

    for l, rows in enumerate(sends):
        for r, row in enumerate(rows):
            box = packed[l].at[pl.ds(r * NPAGE, NPAGE)]

            @pl.when(row >= 0)
            def _():
                pltpu.make_async_copy(box, box, sem.at[l, r]).wait()


def first_windows(groups, branch_count, parent, surviving, page_table, pool):
    links = 2 + groups // NZ - 1
    windows = jax.ShapeDtypeStruct((FIRST * NPAGE,) + pool.shape[1:], pool.dtype)
    return pl.pallas_call(
        functools.partial(first_kernel, groups, branch_count),
        out_shape=[windows] * links,
        in_specs=[VMEM] * 2 + [SMEM, HBM],
        out_specs=[VMEM] * links,
        scratch_shapes=[pltpu.SemaphoreType.DMA((links, FIRST))],
        compiler_params=pltpu.CompilerParams(vmem_limit_bytes=ROOM),
        cost_estimate=pl.CostEstimate(flops=0, bytes_accessed=6_000_000, transcendentals=0),
        name="first_windows",
    )(parent.reshape(1, -1), surviving.reshape(1, -1), page_table.T, pool)


def step_kernel(plan, packs, files, traced, count, filing, attending, *refs):
    if traced:
        at, refs = refs[0][0], refs[1:]
        packs = [(at,) + entry[1:] for entry in packs]
        files = [(at,) + entry[1:] for entry in files]
    links = plan.links
    table = refs[0]
    arrived = refs[1 : 1 + count]
    pool, rows = refs[1 + count : 3 + count]
    store, refilled, out = refs[6 + count : 9 + count]
    packed = refs[9 + count : -8]
    row, result, row_sem, out_sem, file_sem, save_sem, pack_sem, fresh_sem = refs[-8:]
    slots = NZ * KEEP

    comes = []
    for r, l, first, pages, array, offset in files:
        part = arrived[array].at[pl.ds(offset, pages)]
        save = plan.save(table, r, l) if l < 2 else None
        comes.append((save, plan.taker(table, r, l), part, first, pages))

    def is_fresh(source):
        fresh = [source == save for save, _, _, _, _ in comes if save is not None]
        return (source >= 0) & functools.reduce(jnp.logical_or, fresh) if fresh else False

    goes = []
    for r, first, pages, which in packs:
        for l in which:
            goes.append((plan.send(table, r, l), packed[len(goes)], first, pages))

    for i, (source, box, first, pages) in enumerate(goes):

        @pl.when(source >= slots)
        def _():
            @pl.loop(0, pages, unroll=8)
            def _(p):
                page = plan.page(table, source - slots, first + p)
                pltpu.make_async_copy(pool.at[page], box.at[p], pack_sem.at[i]).start()

        @pl.when((source >= 0) & (source < slots) & jnp.logical_not(is_fresh(source)))
        def _():
            pltpu.make_async_copy(
                store.at[jnp.clip(source, 0, slots - 1), pl.ds(first, pages)],
                box,
                pack_sem.at[i],
            ).start()

        for save, _, part, file_first, file_pages in comes:
            if save is not None and file_first <= first < file_first + file_pages:

                @pl.when((source >= 0) & (source == save))
                def _():
                    pltpu.make_async_copy(
                        part.at[pl.ds(first - file_first, pages)], box, fresh_sem.at[i]
                    ).start()

    for i, (save, taker, part, first, pages) in enumerate(comes if filing else []):
        if save is not None:

            @pl.when(save >= 0)
            def _():
                pltpu.make_async_copy(
                    part, store.at[jnp.maximum(save, 0), pl.ds(first, pages)], save_sem.at[i]
                ).start()

        @pl.when(taker >= 0)
        def _():
            if attending:
                pltpu.make_async_copy(rows.at[taker], row.at[i], row_sem.at[i]).start()

            @pl.loop(0, pages, unroll=8)
            def _(p):
                page = plan.page(table, taker, first + p)
                pltpu.make_async_copy(part.at[p], refilled.at[page], file_sem.at[i]).start()

    if attending:
        attend_to(
            [taker for _, taker, _, _, _ in comes],
            [part for _, _, part, _, _ in comes],
            row,
            result,
            row_sem,
            out,
            out_sem,
        )

    for i, (source, box, first, pages) in enumerate(goes):

        @pl.when((source >= 0) & jnp.logical_not(is_fresh(source)))
        def _():
            pltpu.make_async_copy(box, box, pack_sem.at[i]).wait()

        if comes:

            @pl.when(is_fresh(source))
            def _():
                pltpu.make_async_copy(box, box, fresh_sem.at[i]).wait()

    for i, (save, taker, part, first, pages) in enumerate(comes if filing else []):
        if save is not None:

            @pl.when(save >= 0)
            def _():
                pltpu.make_async_copy(part, part, save_sem.at[i]).wait()

        @pl.when(taker >= 0)
        def _():
            pltpu.make_async_copy(part, part, file_sem.at[i]).wait()


def step(plan, packs, files, at, table, arrived, pool, rows, store, refilled, attention, filing=True, attending=False):
    at = [] if at is None else [jnp.stack([at])]
    count = len(arrived)
    lead = len(at) + 1 + count
    heads = rows.shape[2]
    boxes = [
        jax.ShapeDtypeStruct((pages,) + pool.shape[1:], pool.dtype)
        for _, _, pages, which in packs
        for _ in which
    ]
    some = max(len(files), 1)
    out = pl.pallas_call(
        functools.partial(step_kernel, plan, packs, files, bool(at), count, filing, attending),
        out_shape=[
            jax.ShapeDtypeStruct(array.shape, array.dtype) for array in (store, refilled, attention)
        ]
        + boxes,
        in_specs=[SMEM] * (len(at) + 1) + [VMEM] * count + [HBM, ANY, HBM, HBM, ANY],
        out_specs=[HBM] * 2 + [ANY] + [VMEM] * len(boxes),
        scratch_shapes=[
            pltpu.VMEM((some, 3, heads, HD), rows.dtype),
            pltpu.VMEM((some, heads, HD), attention.dtype),
        ]
        + [pltpu.SemaphoreType.DMA((some,))] * 4
        + [pltpu.SemaphoreType.DMA((max(len(boxes), 1),))] * 2,
        input_output_aliases={lead + 2: 0, lead + 3: 1, lead + 4: 2},
        compiler_params=pltpu.CompilerParams(vmem_limit_bytes=ROOM),
        cost_estimate=pl.CostEstimate(flops=0, bytes_accessed=6_000_000, transcendentals=0),
        name="step",
    )(*at, table, *arrived, pool, rows, store, refilled, attention)
    return out[0], out[1], out[2], list(out[3:])


def own_kernel(plan, table, pool, token, refilled, store, window, in_sem, out_sem):
    moves = [
        (plan.kept(table, k), [plan.kept(table, k), plan.own_taker(table, k)]) for k in range(KEEP)
    ]
    for k, (source, _) in enumerate(moves):

        @pl.when(source >= 0)
        def _():
            @pl.loop(0, NPAGE, unroll=8)
            def _(p):
                pltpu.make_async_copy(
                    pool.at[plan.page(table, source, p)], window.at[k, p], in_sem.at[k]
                ).start()

    for k, (source, targets) in enumerate(moves):

        @pl.when(source >= 0)
        def _():
            pltpu.make_async_copy(window.at[k], window.at[k], in_sem.at[k]).wait()

        for lane, to in enumerate(targets):

            @pl.when((source >= 0) & (to >= 0))
            def _():
                @pl.loop(0, NPAGE, unroll=8)
                def _(p):
                    pltpu.make_async_copy(
                        window.at[k, p], refilled.at[plan.page(table, to, p)], out_sem.at[k, lane]
                    ).start()

    for k, (source, targets) in enumerate(moves):
        for lane, to in enumerate(targets):

            @pl.when((source >= 0) & (to >= 0))
            def _():
                pltpu.make_async_copy(window.at[k], window.at[k], out_sem.at[k, lane]).wait()


def own_windows(plan, table, pool, token):
    return pl.pallas_call(
        functools.partial(own_kernel, plan),
        out_shape=[
            jax.ShapeDtypeStruct(pool.shape, pool.dtype),
            jax.ShapeDtypeStruct((NZ * KEEP, NPAGE) + pool.shape[1:], pool.dtype),
        ],
        in_specs=[SMEM, HBM, ANY],
        out_specs=[HBM] * 2,
        scratch_shapes=[
            pltpu.VMEM((KEEP, NPAGE) + pool.shape[1:], pool.dtype),
            pltpu.SemaphoreType.DMA((KEEP,)),
            pltpu.SemaphoreType.DMA((KEEP, 2)),
        ],
        compiler_params=pltpu.CompilerParams(vmem_limit_bytes=ROOM),
        cost_estimate=pl.CostEstimate(flops=0, bytes_accessed=9_000_000, transcendentals=0),
        name="own_windows",
    )(table, pool, token)


def attend_to(branch, windows, row, result, row_sem, out, out_sem):
    count = len(branch)
    for i in range(count):

        @pl.when(branch[i] >= 0)
        def _():
            pltpu.make_async_copy(row.at[i], row.at[i], row_sem.at[i]).wait()

    @pl.when(functools.reduce(jnp.maximum, branch) >= 0)
    def _():
        kv = windows[0].shape[2]
        tokens = NPAGE * PAGE * kv
        flat = [
            window[:, :, 0, :].reshape(tokens, 2 * HD) if kv == 1 else window.reshape(tokens, 2 * HD)
            for window in windows
        ]
        query = [row[i, 0] for i in range(count)]
        scores = [
            lax.dot_general(
                query[i], flat[i][:, :HD], (((1,), (1,)), ((), ())), preferred_element_type=jnp.float32
            )
            for i in range(count)
        ]
        token = lax.broadcasted_iota(jnp.int32, scores[0].shape, 1)
        head = lax.broadcasted_iota(jnp.int32, scores[0].shape, 0)
        fits = (token & (kv - 1)) == lax.div(head, H // KVH)
        for i in range(count):
            masked = jnp.where(fits, scores[i], -jnp.inf)
            own = jnp.sum(
                query[i].astype(jnp.float32) * row[i, 1].astype(jnp.float32), -1, keepdims=True
            )
            peak = jnp.maximum(jnp.max(masked, -1, keepdims=True), own)
            terms = jnp.exp(masked - peak)
            own_term = jnp.exp(own - peak)
            total = jnp.sum(terms, -1, keepdims=True) + own_term
            weights = (terms / total).astype(jnp.bfloat16)
            own_weight = (own_term / total).astype(jnp.bfloat16).astype(jnp.float32)
            mixed = jnp.dot(weights, flat[i][:, HD:], preferred_element_type=jnp.float32)
            mixed = mixed + own_weight * row[i, 2].astype(jnp.float32)
            result[i] = mixed.astype(result.dtype)

    for i in range(count):

        @pl.when(branch[i] >= 0)
        def _():
            pltpu.make_async_copy(result.at[i], out.at[branch[i]], out_sem.at[i]).start()

    for i in range(count):

        @pl.when(branch[i] >= 0)
        def _():
            pltpu.make_async_copy(result.at[i], result.at[i], out_sem.at[i]).wait()


def attend_kernel(plan, whom, traced, *refs):
    if traced:
        at, refs = refs[0][0], refs[1:]
        whom = [(at, l) for _, l in whom]
    table, rows, refilled = refs[:3]
    out, window, row, result, sem, row_sem, out_sem = refs[-7:]
    own = [plan.own_taker(table, k) for k in range(KEEP)]
    takers = []
    for _ in range(CAP):
        taker = functools.reduce(jnp.maximum, own)
        own = [jnp.where(other == taker, -1, other) for other in own]
        takers.append(taker)
    branch = []
    for r, i in whom:
        if r is None:
            branch.append(plan.kept(table, i) if i < KEEP else takers[i - KEEP])
        else:
            branch.append(plan.taker(table, r, i))
    for i, who in enumerate(branch):

        @pl.when(who >= 0)
        def _():
            pltpu.make_async_copy(rows.at[who], row.at[i], row_sem.at[i]).start()

            @pl.loop(0, NPAGE, unroll=8)
            def _(p):
                pltpu.make_async_copy(
                    refilled.at[plan.page(table, who, p)], window.at[i, p], sem.at[i]
                ).start()

    for i, who in enumerate(branch):

        @pl.when(who >= 0)
        def _():
            pltpu.make_async_copy(window.at[i], window.at[i], sem.at[i]).wait()

    attend_to(
        branch, [window.at[i] for i in range(len(branch))], row, result, row_sem, out, out_sem
    )


def attend(plan, whom, at, table, rows, refilled, before):
    at = [] if at is None else [jnp.stack([at])]
    count = len(whom)
    heads = rows.shape[2]
    lead = len(at)
    return pl.pallas_call(
        functools.partial(attend_kernel, plan, whom, bool(at)),
        out_shape=jax.ShapeDtypeStruct((rows.shape[0], heads, HD), jnp.bfloat16),
        in_specs=[SMEM] * (lead + 1) + [ANY, HBM] + [ANY] * len(before),
        out_specs=ANY,
        scratch_shapes=[
            pltpu.VMEM((count, NPAGE) + refilled.shape[1:], refilled.dtype),
            pltpu.VMEM((count, 3, heads, HD), rows.dtype),
            pltpu.VMEM((count, heads, HD), jnp.bfloat16),
            pltpu.SemaphoreType.DMA((count,)),
            pltpu.SemaphoreType.DMA((count,)),
            pltpu.SemaphoreType.DMA((count,)),
        ],
        input_output_aliases={lead + 3: 0} if before else {},
        compiler_params=pltpu.CompilerParams(vmem_limit_bytes=ROOM),
        cost_estimate=pl.CostEstimate(
            flops=count * 2 * 2 * 16 * 1536 * 128, bytes_accessed=count * 800_000, transcendentals=0
        ),
        name="attend",
    )(*at, table, rows, refilled, *before)


def token_rows(hidden, w_query, w_key, w_value, query_gain, key_gain):
    features = lax.all_gather(hidden, "mp", axis=1, tiled=True)
    branch_count = features.shape[0]
    head_group = H // KVH
    heads = w_query.shape[1] // HD
    kv_local = w_key.shape[1] // HD
    query_full = jnp.dot(features, w_query, preferred_element_type=jnp.float32)
    query_full = query_full.reshape(branch_count, heads, HD)
    query_rows = (normalize(query_full, query_gain) / math.sqrt(HD)).astype(jnp.bfloat16)
    key_full = jnp.dot(features, w_key, preferred_element_type=jnp.float32)
    key_rows = normalize(key_full.reshape(branch_count, kv_local, HD), key_gain).astype(jnp.bfloat16)
    value_rows = jnp.dot(features, w_value, preferred_element_type=jnp.float32)
    value_rows = value_rows.reshape(branch_count, kv_local, HD).astype(jnp.bfloat16)
    return jnp.stack(
        [
            query_rows,
            jnp.repeat(key_rows, head_group, axis=1),
            jnp.repeat(value_rows, head_group, axis=1),
        ],
        axis=1,
    )


def shards(
    hidden, w_query, w_key, w_value, query_gain, key_gain, kv_pool, page_table, parent, surviving
):
    groups = lax.axis_size("dp")
    me = lax.axis_index("dp")
    ny = groups // NZ
    branch_count = hidden.shape[0]
    links = 2 + ny - 1
    packed = first_windows(groups, branch_count, parent, surviving, page_table, kv_pool)
    parent, surviving, page_table, packed = lax.optimization_barrier(
        (parent, surviving, page_table, packed)
    )
    sides = lax.axis_size("mp")

    def everywhere(move):
        return [
            (g * sides + m, to[0] * sides + to[1])
            for g in range(groups)
            for m in range(sides)
            for to in [move(g, m)]
        ]

    def outer(g, m):
        return g + ny if g // ny % 2 == 0 else g - ny, m

    def inner(g, m):
        if g // ny in (0, NZ - 1):
            return g, m ^ 1
        return g + ny if g // ny % 2 else g - ny, m

    def sideways(shift):
        return lambda g, m: (g // ny * ny + (g % ny + shift) % ny, m)

    pairs = [everywhere(outer), everywhere(inner)]
    pairs += [everywhere(sideways(shift)) for shift in range(1, ny)]
    along, beside, every = [0, 1], list(range(2, links)), list(range(links))

    def travel(packed, which):
        return [lax.ppermute(window, ("dp", "mp"), pairs[l]) for window, l in zip(packed, which)]

    arrived = travel(packed, every)
    plan = Plan(links, groups, branch_count)
    table = routing(parent, surviving, page_table, groups, branch_count, links)
    rounds = table[plan.rounds_at]
    refilled, store = own_windows(plan, table, kv_pool, packed[0])
    rows = token_rows(hidden, w_query, w_key, w_value, query_gain, key_gain)
    waiting = [[(None, i) for i in range(3)], [(None, i) for i in range(3, KEEP + CAP)]]
    waiting += [[(r, l) for l in every] for r in range(FIRST)]

    def attend_next(attention):
        return attend(plan, waiting.pop(0), None, table, rows, refilled, attention)

    attention = attend_next([])
    files = [(r, l, 0, NPAGE, l, r * NPAGE) for r in range(FIRST) for l in every]
    store, refilled, attention, packed = step(
        plan,
        [(FIRST, 0, NPAGE, every)],
        [file for file in files if file[1] in along],
        None,
        table,
        arrived[:2],
        kv_pool,
        rows,
        store,
        refilled,
        attention,
        filing=False,
    )
    moved = travel(packed, every)
    for r in range(FIRST, PREFIX):
        if r > FIRST:
            files = [(r - 1, l, 0, NPAGE, l, 0) for l in along]
            files += [(r - 2, l, 0, NPAGE, l, 0) for l in beside if r - 2 >= FIRST]
            arrived = came_along + came_beside
        packs = [(r, 0, NPAGE, beside)] if r > FIRST else []
        packs += [(r + 1, 0, NPAGE, along)] if r + 1 < PREFIX else []
        store, refilled, attention, packed = step(
            plan, packs, files, None, table, arrived, kv_pool, rows, store, refilled, attention
        )
        if r > FIRST:
            came_along, came_beside = moving_along, moving_beside
            moving_beside = travel(packed[: len(beside)], beside)
            packed = packed[len(beside) :]
            waiting.append([(at, l) for at, l, _, _, _, _ in files])
        else:
            came_along, came_beside, moving_beside = moved[:2], [], moved[2:]
        if packed:
            moving_along = travel(packed, along)
        for _ in range(2 if len(waiting) > 1 else 1):
            attention = attend_next([attention])
    while waiting:
        attention = attend_next([attention])
    last = PREFIX - 1
    arrived = came_along + came_beside + moving_beside
    files = [(last, l, 0, NPAGE, l, 0) for l in along]
    files += [(last - 1, l, 0, NPAGE, l, 0) for l in beside]
    files += [(last, l, 0, NPAGE, l + len(beside), 0) for l in beside]
    store, refilled, attention, _ = step(
        plan, [], files, None, table, arrived, kv_pool, rows, store, refilled, attention, attending=True
    )

    def more(state):
        return state[0] < rounds

    def one_round(state):
        r, store, refilled, attention = state
        part = NPAGE // PIECES
        moving = []
        for piece in range(PIECES):
            store, refilled, attention, packed = step(
                plan, [(None, piece * part, part, every)], [], r, table, [], kv_pool, rows, store, refilled, attention
            )
            moving.append(travel(packed, every))
        for piece in range(PIECES):
            files = [(None, l, piece * part, part, l, 0) for l in every]
            store, refilled, attention, _ = step(
                plan, [], files, r, table, moving.pop(0), kv_pool, rows, store, refilled, attention
            )
        attention = attend(plan, [(r, l) for l in every], r, table, rows, refilled, [attention])
        return r + 1, store, refilled, attention

    _, store, refilled, attention = lax.while_loop(
        more, one_round, (jnp.int32(PREFIX), store, refilled, attention)
    )
    return (refilled, attention.reshape(branch_count, -1))


def solution(mesh):
    return jax.shard_map(
        shards,
        mesh=mesh,
        in_specs=(
            P("dp", "mp"),
            P(None, "mp"),
            P(None, "mp"),
            P(None, "mp"),
            P(),
            P(),
            P("dp", None, "mp", None),
            P(),
            P(),
            P(),
        ),
        out_specs=(P("dp", None, "mp", None), P("dp", "mp")),
        check_vma=False,
    )
```

```python
import functools
import math

import jax
import jax.numpy as jnp
from jax import lax
from jax.experimental import pallas as pl
from jax.experimental.pallas import tpu as pltpu
from jax.sharding import PartitionSpec as P

H = 64
KVH = 8
HD = 128
PAGE = 16
NPAGE = 48
CAP = 2
KEEP = 4
NZ = 4
ROUNDS = 40
LANES = 128
PREFIX = 8
FIRST = 2
REST = 2
PIECES = 2
ROOM = 48 * 1024 * 1024
NEVER = 1 << 20


def normalize(values, gain):
    return values * lax.rsqrt(jnp.mean(values * values, -1, keepdims=True) + 1e-06) * gain


def plan_kernel(groups, branch_count, parent_row, alive_row, parent_column, alive_column, out, state):
    ny = groups // NZ
    branches = groups * branch_count
    shifts = list(range(1, ny))
    slots = NZ * KEEP
    me = lax.axis_index("dp")

    def iota(shape, axis):
        return lax.broadcasted_iota(jnp.int32, shape, axis)

    square = (branches, branches)
    down_ids, across_ids = iota(square, 0), iota(square, 1)
    same = lax.div(down_ids, branch_count) == lax.div(across_ids, branch_count)
    alive_r, alive_c = alive_row[...] > 0, alive_column[...] > 0
    before = jnp.where(same & (down_ids < across_ids) & alive_c, 1, 0)
    item_row = jnp.sum(before, axis=0, keepdims=True)
    item_row = item_row + lax.div(iota((1, branches), 1), branch_count) * KEEP
    before = jnp.where(same & (across_ids < down_ids) & alive_r, 1, 0)
    item_column = jnp.sum(before, axis=1, keepdims=True)
    item_column = item_column + lax.div(iota((branches, 1), 0), branch_count) * KEEP
    wanted = jnp.sum(
        jnp.where(parent_column[...] == across_ids, item_row, 0), axis=1, keepdims=True
    )
    wanted = jnp.where(alive_c, -1, wanted)
    wide = (branches, LANES)
    local = lax.rem(iota(wide, 0), branch_count)
    takes = jnp.where(wanted == iota(wide, 1), local, -1)
    child = jnp.max(takes.reshape(groups, branch_count, LANES), axis=1)
    holds = jnp.where((item_column == iota(wide, 1)) & alive_c, local, -1)
    branch = jnp.max(holds, axis=0, keepdims=True)

    shape = (groups, LANES)
    here, item = iota(shape, 0), iota(shape, 1)
    z, y = lax.div(here, ny), lax.rem(here, ny)
    source = lax.div(item, KEEP)
    item_z, item_y = lax.div(source, ny), lax.rem(source, ny)
    on_line = item_y == y
    need = child >= 0

    def across(mask):
        return jnp.max(jnp.where(mask, 1, 0), axis=0, keepdims=True)

    top = jnp.max(jnp.where(need, z, -1), axis=0, keepdims=True)
    bottom = jnp.min(jnp.where(need, z, NZ), axis=0, keepdims=True)
    top_crosses = across(need & (z == top) & (item_y != y))
    bottom_crosses = across(need & (z == bottom) & (item_y != y))
    tie = LANES - 1 - item
    up_hops, down_hops = jnp.maximum(top - z, 0), jnp.maximum(z - bottom, 0)
    up_key = (up_hops * 2 + top_crosses) * LANES + tie
    down_key = (down_hops * 2 + bottom_crosses) * LANES + tie
    go_up, go_down = on_line & (up_hops > 0), on_line & (down_hops > 0)

    def beside(x, shift):
        return jnp.where(
            y + shift < ny, pltpu.roll(x, groups - shift, 0), pltpu.roll(x, (ny - shift) % groups, 0)
        )

    crosses = [on_line & (beside(child, shift) >= 0) for shift in shifts]
    own = source == here
    start = [go_up & own, go_down & own] + [c & own for c in crosses]
    rows = len(start)
    for i, mask in enumerate(start):
        state[i] = jnp.where(mask, 0, NEVER)
        state[rows + i] = jnp.full(shape, -1, jnp.int32)

    def choose(i, r, key):
        ready = state[i]
        key = jnp.where(ready <= r, key(ready), -1)
        best = jnp.max(key, axis=1, keepdims=True)
        chosen = (key == best) & (best >= 0)
        state[i] = jnp.where(chosen, NEVER, ready)
        state[rows + i] = jnp.where(chosen, r, state[rows + i])
        return jnp.where(chosen, 1, 0)

    def one_round(r):
        ups = choose(0, r, lambda ready: up_key)
        downs = choose(1, r, lambda ready: down_key)
        for i in range(2, rows):
            choose(i, r, lambda ready: (ROUNDS - ready) * LANES + tie)
        ups = jnp.where(z > 0, pltpu.roll(ups, ny, 0), 0) > 0
        downs = jnp.where(z < NZ - 1, pltpu.roll(downs, groups - ny, 0), 0) > 0
        rested = jnp.where(r < FIRST, FIRST, r + REST)
        state[0] = jnp.where(ups & go_up, rested, state[0])
        state[1] = jnp.where(downs & go_down, rested, state[1])
        left = jnp.minimum(state[0], state[1])
        for i, cross in enumerate(crosses):
            there = jnp.where((ups | downs) & cross, jnp.maximum(r + 1, FIRST), state[2 + i])
            state[2 + i] = there
            left = jnp.minimum(left, there)
        return r + 1, jnp.min(left)

    rounds, _ = lax.while_loop(
        lambda carry: (carry[1] < NEVER) & (carry[0] < ROUNDS),
        lambda carry: one_round(carry[0]),
        (jnp.int32(0), jnp.int32(0)),
    )

    def row_of(x, group):
        return jnp.max(jnp.where(here == group, x, -1), axis=0, keepdims=True)

    my_z = lax.div(me, ny)
    my_y = me - my_z * ny
    even = lax.rem(my_z, 2) == 0
    item = iota((1, LANES), 1)
    group = lax.div(item, KEEP)
    slot = lax.div(group, ny) * KEEP + lax.rem(item, KEEP)
    value = jnp.where(group == me, slots + branch, slot)
    taker = row_of(child, me)
    up_out, down_out = row_of(state[rows], me), row_of(state[rows + 1], me)
    up_in, down_in = row_of(state[rows], me - ny), row_of(state[rows + 1], me + ny)
    outs = [jnp.where(even, up_out, down_out), jnp.where(even, down_out, up_out)]
    ins = [jnp.where(even, down_in, up_in), jnp.where(even, up_in, down_in)]
    for shift in shifts:
        outs.append(row_of(state[rows + 1 + shift], me))
        from_y = lax.rem(my_y + ny - shift, ny)
        ins.append(row_of(state[rows + 1 + shift], my_z * ny + from_y))
    table = [(times, value) for times in outs]
    table += [(times, slot) for times in ins[:2]]
    table += [(times, taker) for times in ins]
    at = iota((ROUNDS, LANES), 0)
    lane = iota((ROUNDS, LANES), 1)
    result = jnp.full((ROUNDS, LANES), -1, jnp.int32)
    for c, (times, values) in enumerate(table):
        column = jnp.max(jnp.where(times == at, values, -1), axis=1, keepdims=True)
        result = jnp.where(lane == c, column, result)
    out[pl.ds(0, ROUNDS), :] = result
    extra = iota((8, LANES), 0)
    out[pl.ds(ROUNDS, 8), :] = jnp.where(
        extra == 0, rounds, jnp.where(extra == 1, branch, jnp.where(extra == 2, taker, 0))
    )


class Plan:
    def __init__(self, links, groups, branch_count):
        self.links = links
        self.width = 2 * links + 2
        self.rounds_at = ROUNDS * self.width
        self.branch_at = self.rounds_at + 1
        self.taker_at = self.branch_at + groups * KEEP
        self.pages_at = self.taker_at + groups * KEEP

    def send(self, table, r, l):
        return table[r * self.width + l]

    def save(self, table, r, l):
        return table[r * self.width + self.links + l]

    def taker(self, table, r, l):
        return table[r * self.width + self.links + 2 + l]

    def page(self, table, branch, p):
        return table[self.pages_at + branch * NPAGE + p]

    def kept(self, table, k):
        return table[self.branch_at + lax.axis_index("dp") * KEEP + k]

    def own_taker(self, table, k):
        return table[self.taker_at + lax.axis_index("dp") * KEEP + k]


def routing(parent, surviving, page_table, groups, branch_count, links):
    ny = groups // NZ
    rows = 2 + ny - 1
    out = pl.pallas_call(
        functools.partial(plan_kernel, groups, branch_count),
        out_shape=jax.ShapeDtypeStruct((ROUNDS + 8, LANES), jnp.int32),
        in_specs=[VMEM] * 4,
        out_specs=VMEM,
        scratch_shapes=[pltpu.VMEM((2 * rows, groups, LANES), jnp.int32)],
        compiler_params=pltpu.CompilerParams(vmem_limit_bytes=ROOM),
        cost_estimate=pl.CostEstimate(flops=0, bytes_accessed=6_000_000, transcendentals=0),
        name="plan",
    )(
        parent.reshape(1, -1),
        surviving.reshape(1, -1),
        parent.reshape(-1, 1),
        surviving.reshape(-1, 1),
    )
    pages = lax.dynamic_slice_in_dim(
        page_table, lax.axis_index("dp") * branch_count, branch_count, 0
    )
    items = groups * KEEP
    return jnp.concatenate(
        [
            out[:ROUNDS, : 2 * links + 2].reshape(-1),
            out[ROUNDS, :1],
            out[ROUNDS + 1, :items],
            out[ROUNDS + 2, :items],
            pages.reshape(-1),
        ]
    )


SMEM = pl.BlockSpec(memory_space=pltpu.SMEM)
VMEM = pl.BlockSpec(memory_space=pltpu.VMEM)
HBM = pl.BlockSpec(memory_space=pltpu.HBM)
ANY = pl.BlockSpec(memory_space=pl.ANY)


def first_kernel(groups, branch_count, parent, surviving, page_table, pool, *refs):
    ny = groups // NZ
    packed, sem = refs[:-1], refs[-1]
    me = lax.axis_index("dp")
    z, y = me // ny, me % ny
    shape = (branch_count, groups * branch_count)
    child = lax.broadcasted_iota(jnp.int32, shape, 1)
    local = lax.broadcasted_iota(jnp.int32, shape, 0)
    column = lax.broadcasted_iota(jnp.int32, (branch_count, 1), 0)
    mine = (surviving[...] == 0) & (parent[...] == me * branch_count + local)
    target = lax.div(child, branch_count)
    target_z = lax.div(target, ny)
    target_y = target - target_z * ny

    def seen(mask):
        return jnp.max(mask.astype(jnp.int32), axis=1, keepdims=True)

    def leading(key):
        rows = []
        for _ in range(FIRST):
            best = jnp.max(key)
            rows.append(
                jnp.where(best >= 0, branch_count - 1 - lax.rem(best, branch_count), -1)
            )
            key = jnp.where(key == best, -1, key)
        return rows

    ways = []
    for steps in (target_z - z, z - target_z):
        hops = jnp.max(jnp.where(mine, steps, 0), axis=1, keepdims=True)
        far_across = seen(mine & (steps == hops) & (target_y != y))
        key = (hops * 2 + far_across) * branch_count + branch_count - 1 - column
        ways.append(leading(jnp.where(hops > 0, key, -1)))
    even = lax.rem(z, 2) == 0
    sends = [
        [jnp.where(even, u, d) for u, d in zip(*ways)],
        [jnp.where(even, d, u) for u, d in zip(*ways)],
    ]
    for shift in range(1, ny):
        to = lax.rem(y + shift, ny)
        crossing = seen(mine & (target_z == z) & (target_y == to))
        sends.append(leading(jnp.where(crossing > 0, branch_count - 1 - column, -1)))
    for l, rows in enumerate(sends):
        for r, row in enumerate(rows):

            @pl.when(row >= 0)
            def _():
                @pl.loop(0, NPAGE, unroll=8)
                def _(p):
                    page = page_table[p, me * branch_count + row]
                    pltpu.make_async_copy(
                        pool.at[page], packed[l].at[r * NPAGE + p], sem.at[l, r]
                    ).start()

    for l, rows in enumerate(sends):
        for r, row in enumerate(rows):
            box = packed[l].at[pl.ds(r * NPAGE, NPAGE)]

            @pl.when(row >= 0)
            def _():
                pltpu.make_async_copy(box, box, sem.at[l, r]).wait()


def first_windows(groups, branch_count, parent, surviving, page_table, pool):
    links = 2 + groups // NZ - 1
    windows = jax.ShapeDtypeStruct((FIRST * NPAGE,) + pool.shape[1:], pool.dtype)
    return pl.pallas_call(
        functools.partial(first_kernel, groups, branch_count),
        out_shape=[windows] * links,
        in_specs=[VMEM] * 2 + [SMEM, HBM],
        out_specs=[VMEM] * links,
        scratch_shapes=[pltpu.SemaphoreType.DMA((links, FIRST))],
        compiler_params=pltpu.CompilerParams(vmem_limit_bytes=ROOM),
        cost_estimate=pl.CostEstimate(flops=0, bytes_accessed=6_000_000, transcendentals=0),
        name="first_windows",
    )(parent.reshape(1, -1), surviving.reshape(1, -1), page_table.T, pool)


def step_kernel(plan, packs, files, traced, count, filing, attending, *refs):
    if traced:
        at, refs = refs[0][0], refs[1:]
        packs = [(at,) + entry[1:] for entry in packs]
        files = [(at,) + entry[1:] for entry in files]
    links = plan.links
    table = refs[0]
    arrived = refs[1 : 1 + count]
    pool, rows = refs[1 + count : 3 + count]
    store, refilled, out = refs[6 + count : 9 + count]
    packed = refs[9 + count : -8]
    row, result, row_sem, out_sem, file_sem, save_sem, pack_sem, fresh_sem = refs[-8:]
    slots = NZ * KEEP

    comes = []
    for r, l, first, pages, array, offset in files:
        part = arrived[array].at[pl.ds(offset, pages)]
        save = plan.save(table, r, l) if l < 2 else None
        comes.append((save, plan.taker(table, r, l), part, first, pages))

    def is_fresh(source):
        fresh = [source == save for save, _, _, _, _ in comes if save is not None]
        return (source >= 0) & functools.reduce(jnp.logical_or, fresh) if fresh else False

    goes = []
    for r, first, pages, which in packs:
        for l in which:
            goes.append((plan.send(table, r, l), packed[len(goes)], first, pages))

    for i, (source, box, first, pages) in enumerate(goes):

        @pl.when(source >= slots)
        def _():
            @pl.loop(0, pages, unroll=8)
            def _(p):
                page = plan.page(table, source - slots, first + p)
                pltpu.make_async_copy(pool.at[page], box.at[p], pack_sem.at[i]).start()

        @pl.when((source >= 0) & (source < slots) & jnp.logical_not(is_fresh(source)))
        def _():
            pltpu.make_async_copy(
                store.at[jnp.clip(source, 0, slots - 1), pl.ds(first, pages)],
                box,
                pack_sem.at[i],
            ).start()

        for save, _, part, file_first, file_pages in comes:
            if save is not None and file_first <= first < file_first + file_pages:

                @pl.when((source >= 0) & (source == save))
                def _():
                    pltpu.make_async_copy(
                        part.at[pl.ds(first - file_first, pages)], box, fresh_sem.at[i]
                    ).start()

    for i, (save, taker, part, first, pages) in enumerate(comes if filing else []):
        if save is not None:

            @pl.when(save >= 0)
            def _():
                pltpu.make_async_copy(
                    part, store.at[jnp.maximum(save, 0), pl.ds(first, pages)], save_sem.at[i]
                ).start()

        @pl.when(taker >= 0)
        def _():
            if attending:
                pltpu.make_async_copy(rows.at[taker], row.at[i], row_sem.at[i]).start()

            @pl.loop(0, pages, unroll=8)
            def _(p):
                page = plan.page(table, taker, first + p)
                pltpu.make_async_copy(part.at[p], refilled.at[page], file_sem.at[i]).start()

    if attending:
        attend_to(
            [taker for _, taker, _, _, _ in comes],
            [part for _, _, part, _, _ in comes],
            row,
            result,
            row_sem,
            out,
            out_sem,
        )

    for i, (source, box, first, pages) in enumerate(goes):

        @pl.when((source >= 0) & jnp.logical_not(is_fresh(source)))
        def _():
            pltpu.make_async_copy(box, box, pack_sem.at[i]).wait()

        if comes:

            @pl.when(is_fresh(source))
            def _():
                pltpu.make_async_copy(box, box, fresh_sem.at[i]).wait()

    for i, (save, taker, part, first, pages) in enumerate(comes if filing else []):
        if save is not None:

            @pl.when(save >= 0)
            def _():
                pltpu.make_async_copy(part, part, save_sem.at[i]).wait()

        @pl.when(taker >= 0)
        def _():
            pltpu.make_async_copy(part, part, file_sem.at[i]).wait()


def step(plan, packs, files, at, table, arrived, pool, rows, store, refilled, attention, filing=True, attending=False):
    at = [] if at is None else [jnp.stack([at])]
    count = len(arrived)
    lead = len(at) + 1 + count
    heads = rows.shape[2]
    boxes = [
        jax.ShapeDtypeStruct((pages,) + pool.shape[1:], pool.dtype)
        for _, _, pages, which in packs
        for _ in which
    ]
    some = max(len(files), 1)
    out = pl.pallas_call(
        functools.partial(step_kernel, plan, packs, files, bool(at), count, filing, attending),
        out_shape=[
            jax.ShapeDtypeStruct(array.shape, array.dtype) for array in (store, refilled, attention)
        ]
        + boxes,
        in_specs=[SMEM] * (len(at) + 1) + [VMEM] * count + [HBM, ANY, HBM, HBM, ANY],
        out_specs=[HBM] * 2 + [ANY] + [VMEM] * len(boxes),
        scratch_shapes=[
            pltpu.VMEM((some, 3, heads, HD), rows.dtype),
            pltpu.VMEM((some, heads, HD), attention.dtype),
        ]
        + [pltpu.SemaphoreType.DMA((some,))] * 4
        + [pltpu.SemaphoreType.DMA((max(len(boxes), 1),))] * 2,
        input_output_aliases={lead + 2: 0, lead + 3: 1, lead + 4: 2},
        compiler_params=pltpu.CompilerParams(vmem_limit_bytes=ROOM),
        cost_estimate=pl.CostEstimate(flops=0, bytes_accessed=6_000_000, transcendentals=0),
        name="step",
    )(*at, table, *arrived, pool, rows, store, refilled, attention)
    return out[0], out[1], out[2], list(out[3:])


def own_kernel(plan, table, pool, token, refilled, store, window, in_sem, out_sem):
    moves = [
        (plan.kept(table, k), [plan.kept(table, k), plan.own_taker(table, k)]) for k in range(KEEP)
    ]
    for k, (source, _) in enumerate(moves):

        @pl.when(source >= 0)
        def _():
            @pl.loop(0, NPAGE, unroll=8)
            def _(p):
                pltpu.make_async_copy(
                    pool.at[plan.page(table, source, p)], window.at[k, p], in_sem.at[k]
                ).start()

    for k, (source, targets) in enumerate(moves):

        @pl.when(source >= 0)
        def _():
            pltpu.make_async_copy(window.at[k], window.at[k], in_sem.at[k]).wait()

        for lane, to in enumerate(targets):

            @pl.when((source >= 0) & (to >= 0))
            def _():
                @pl.loop(0, NPAGE, unroll=8)
                def _(p):
                    pltpu.make_async_copy(
                        window.at[k, p], refilled.at[plan.page(table, to, p)], out_sem.at[k, lane]
                    ).start()

    for k, (source, targets) in enumerate(moves):
        for lane, to in enumerate(targets):

            @pl.when((source >= 0) & (to >= 0))
            def _():
                pltpu.make_async_copy(window.at[k], window.at[k], out_sem.at[k, lane]).wait()


def own_windows(plan, table, pool, token):
    return pl.pallas_call(
        functools.partial(own_kernel, plan),
        out_shape=[
            jax.ShapeDtypeStruct(pool.shape, pool.dtype),
            jax.ShapeDtypeStruct((NZ * KEEP, NPAGE) + pool.shape[1:], pool.dtype),
        ],
        in_specs=[SMEM, HBM, ANY],
        out_specs=[HBM] * 2,
        scratch_shapes=[
            pltpu.VMEM((KEEP, NPAGE) + pool.shape[1:], pool.dtype),
            pltpu.SemaphoreType.DMA((KEEP,)),
            pltpu.SemaphoreType.DMA((KEEP, 2)),
        ],
        compiler_params=pltpu.CompilerParams(vmem_limit_bytes=ROOM),
        cost_estimate=pl.CostEstimate(flops=0, bytes_accessed=9_000_000, transcendentals=0),
        name="own_windows",
    )(table, pool, token)


def attend_to(branch, windows, row, result, row_sem, out, out_sem):
    count = len(branch)
    for i in range(count):

        @pl.when(branch[i] >= 0)
        def _():
            pltpu.make_async_copy(row.at[i], row.at[i], row_sem.at[i]).wait()

    @pl.when(functools.reduce(jnp.maximum, branch) >= 0)
    def _():
        kv = windows[0].shape[2]
        tokens = NPAGE * PAGE * kv
        flat = [
            window[:, :, 0, :].reshape(tokens, 2 * HD) if kv == 1 else window.reshape(tokens, 2 * HD)
            for window in windows
        ]
        query = [row[i, 0] for i in range(count)]
        scores = [
            lax.dot_general(
                query[i], flat[i][:, :HD], (((1,), (1,)), ((), ())), preferred_element_type=jnp.float32
            )
            for i in range(count)
        ]
        token = lax.broadcasted_iota(jnp.int32, scores[0].shape, 1)
        head = lax.broadcasted_iota(jnp.int32, scores[0].shape, 0)
        fits = (token & (kv - 1)) == lax.div(head, H // KVH)
        for i in range(count):
            masked = jnp.where(fits, scores[i], -jnp.inf)
            own = jnp.sum(
                query[i].astype(jnp.float32) * row[i, 1].astype(jnp.float32), -1, keepdims=True
            )
            peak = jnp.maximum(jnp.max(masked, -1, keepdims=True), own)
            terms = jnp.exp(masked - peak)
            own_term = jnp.exp(own - peak)
            total = jnp.sum(terms, -1, keepdims=True) + own_term
            weights = (terms / total).astype(jnp.bfloat16)
            own_weight = (own_term / total).astype(jnp.bfloat16).astype(jnp.float32)
            mixed = jnp.dot(weights, flat[i][:, HD:], preferred_element_type=jnp.float32)
            mixed = mixed + own_weight * row[i, 2].astype(jnp.float32)
            result[i] = mixed.astype(result.dtype)

    for i in range(count):

        @pl.when(branch[i] >= 0)
        def _():
            pltpu.make_async_copy(result.at[i], out.at[branch[i]], out_sem.at[i]).start()

    for i in range(count):

        @pl.when(branch[i] >= 0)
        def _():
            pltpu.make_async_copy(result.at[i], result.at[i], out_sem.at[i]).wait()


def attend_kernel(plan, whom, traced, *refs):
    if traced:
        at, refs = refs[0][0], refs[1:]
        whom = [(at, l) for _, l in whom]
    table, rows, refilled = refs[:3]
    out, window, row, result, sem, row_sem, out_sem = refs[-7:]
    own = [plan.own_taker(table, k) for k in range(KEEP)]
    takers = []
    for _ in range(CAP):
        taker = functools.reduce(jnp.maximum, own)
        own = [jnp.where(other == taker, -1, other) for other in own]
        takers.append(taker)
    branch = []
    for r, i in whom:
        if r is None:
            branch.append(plan.kept(table, i) if i < KEEP else takers[i - KEEP])
        else:
            branch.append(plan.taker(table, r, i))
    for i, who in enumerate(branch):

        @pl.when(who >= 0)
        def _():
            pltpu.make_async_copy(rows.at[who], row.at[i], row_sem.at[i]).start()

            @pl.loop(0, NPAGE, unroll=8)
            def _(p):
                pltpu.make_async_copy(
                    refilled.at[plan.page(table, who, p)], window.at[i, p], sem.at[i]
                ).start()

    for i, who in enumerate(branch):

        @pl.when(who >= 0)
        def _():
            pltpu.make_async_copy(window.at[i], window.at[i], sem.at[i]).wait()

    attend_to(
        branch, [window.at[i] for i in range(len(branch))], row, result, row_sem, out, out_sem
    )


def attend(plan, whom, at, table, rows, refilled, before):
    at = [] if at is None else [jnp.stack([at])]
    count = len(whom)
    heads = rows.shape[2]
    lead = len(at)
    return pl.pallas_call(
        functools.partial(attend_kernel, plan, whom, bool(at)),
        out_shape=jax.ShapeDtypeStruct((rows.shape[0], heads, HD), jnp.bfloat16),
        in_specs=[SMEM] * (lead + 1) + [ANY, HBM] + [ANY] * len(before),
        out_specs=ANY,
        scratch_shapes=[
            pltpu.VMEM((count, NPAGE) + refilled.shape[1:], refilled.dtype),
            pltpu.VMEM((count, 3, heads, HD), rows.dtype),
            pltpu.VMEM((count, heads, HD), jnp.bfloat16),
            pltpu.SemaphoreType.DMA((count,)),
            pltpu.SemaphoreType.DMA((count,)),
            pltpu.SemaphoreType.DMA((count,)),
        ],
        input_output_aliases={lead + 3: 0} if before else {},
        compiler_params=pltpu.CompilerParams(vmem_limit_bytes=ROOM),
        cost_estimate=pl.CostEstimate(
            flops=count * 2 * 2 * 16 * 1536 * 128, bytes_accessed=count * 800_000, transcendentals=0
        ),
        name="attend",
    )(*at, table, rows, refilled, *before)


def token_rows(hidden, w_query, w_key, w_value, query_gain, key_gain):
    features = lax.all_gather(hidden, "mp", axis=1, tiled=True)
    branch_count = features.shape[0]
    head_group = H // KVH
    heads = w_query.shape[1] // HD
    kv_local = w_key.shape[1] // HD
    query_full = jnp.dot(features, w_query, preferred_element_type=jnp.float32)
    query_full = query_full.reshape(branch_count, heads, HD)
    query_rows = (normalize(query_full, query_gain) / math.sqrt(HD)).astype(jnp.bfloat16)
    key_full = jnp.dot(features, w_key, preferred_element_type=jnp.float32)
    key_rows = normalize(key_full.reshape(branch_count, kv_local, HD), key_gain).astype(jnp.bfloat16)
    value_rows = jnp.dot(features, w_value, preferred_element_type=jnp.float32)
    value_rows = value_rows.reshape(branch_count, kv_local, HD).astype(jnp.bfloat16)
    return jnp.stack(
        [
            query_rows,
            jnp.repeat(key_rows, head_group, axis=1),
            jnp.repeat(value_rows, head_group, axis=1),
        ],
        axis=1,
    )


def shards(
    hidden, w_query, w_key, w_value, query_gain, key_gain, kv_pool, page_table, parent, surviving
):
    groups = lax.axis_size("dp")
    me = lax.axis_index("dp")
    ny = groups // NZ
    branch_count = hidden.shape[0]
    links = 2 + ny - 1
    packed = first_windows(groups, branch_count, parent, surviving, page_table, kv_pool)
    parent, surviving, page_table, packed = lax.optimization_barrier(
        (parent, surviving, page_table, packed)
    )
    sides = lax.axis_size("mp")

    def everywhere(move):
        return [
            (g * sides + m, to[0] * sides + to[1])
            for g in range(groups)
            for m in range(sides)
            for to in [move(g, m)]
        ]

    def outer(g, m):
        return g + ny if g // ny % 2 == 0 else g - ny, m

    def inner(g, m):
        if g // ny in (0, NZ - 1):
            return g, m ^ 1
        return g + ny if g // ny % 2 else g - ny, m

    def sideways(shift):
        return lambda g, m: (g // ny * ny + (g % ny + shift) % ny, m)

    pairs = [everywhere(outer), everywhere(inner)]
    pairs += [everywhere(sideways(shift)) for shift in range(1, ny)]
    along, beside, every = [0, 1], list(range(2, links)), list(range(links))

    def travel(packed, which):
        return [lax.ppermute(window, ("dp", "mp"), pairs[l]) for window, l in zip(packed, which)]

    arrived = travel(packed, every)
    plan = Plan(links, groups, branch_count)
    table = routing(parent, surviving, page_table, groups, branch_count, links)
    rounds = table[plan.rounds_at]
    refilled, store = own_windows(plan, table, kv_pool, packed[0])
    rows = token_rows(hidden, w_query, w_key, w_value, query_gain, key_gain)
    waiting = [[(None, i) for i in range(3)], [(None, i) for i in range(3, KEEP + CAP)]]
    waiting += [[(r, l) for l in every] for r in range(FIRST)]

    def attend_next(attention):
        return attend(plan, waiting.pop(0), None, table, rows, refilled, attention)

    attention = attend_next([])
    files = [(r, l, 0, NPAGE, l, r * NPAGE) for r in range(FIRST) for l in every]
    store, refilled, attention, packed = step(
        plan,
        [(FIRST, 0, NPAGE, every)],
        [file for file in files if file[1] in along],
        None,
        table,
        arrived[:2],
        kv_pool,
        rows,
        store,
        refilled,
        attention,
        filing=False,
    )
    moved = travel(packed, every)
    for r in range(FIRST, PREFIX):
        if r > FIRST:
            files = [(r - 1, l, 0, NPAGE, l, 0) for l in along]
            files += [(r - 2, l, 0, NPAGE, l, 0) for l in beside if r - 2 >= FIRST]
            arrived = came_along + came_beside
        packs = [(r, 0, NPAGE, beside)] if r > FIRST else []
        packs += [(r + 1, 0, NPAGE, along)] if r + 1 < PREFIX else []
        store, refilled, attention, packed = step(
            plan, packs, files, None, table, arrived, kv_pool, rows, store, refilled, attention
        )
        if r > FIRST:
            came_along, came_beside = moving_along, moving_beside
            moving_beside = travel(packed[: len(beside)], beside)
            packed = packed[len(beside) :]
            waiting.append([(at, l) for at, l, _, _, _, _ in files])
        else:
            came_along, came_beside, moving_beside = moved[:2], [], moved[2:]
        if packed:
            if came_beside:
                packed, came_beside = lax.optimization_barrier((packed, came_beside))
            moving_along = travel(packed, along)
        for _ in range(2 if len(waiting) > 1 else 1):
            attention = attend_next([attention])
    while waiting:
        attention = attend_next([attention])
    last = PREFIX - 1
    endings = [(last - 1, beside, came_beside), (last, along, came_along), (last, beside, moving_beside)]
    for r, which, arrived in endings:
        files = [(r, l, 0, NPAGE, i, 0) for i, l in enumerate(which)]
        store, refilled, attention, _ = step(
            plan, [], files, None, table, arrived, kv_pool, rows, store, refilled, attention, attending=True
        )

    def more(state):
        return state[0] < rounds

    def one_round(state):
        r, store, refilled, attention = state
        part = NPAGE // PIECES
        moving = []
        for piece in range(PIECES):
            store, refilled, attention, packed = step(
                plan, [(None, piece * part, part, every)], [], r, table, [], kv_pool, rows, store, refilled, attention
            )
            moving.append(travel(packed, every))
        for piece in range(PIECES):
            files = [(None, l, piece * part, part, l, 0) for l in every]
            store, refilled, attention, _ = step(
                plan, [], files, r, table, moving.pop(0), kv_pool, rows, store, refilled, attention
            )
        attention = attend(plan, [(r, l) for l in every], r, table, rows, refilled, [attention])
        return r + 1, store, refilled, attention

    _, store, refilled, attention = lax.while_loop(
        more, one_round, (jnp.int32(PREFIX), store, refilled, attention)
    )
    return (refilled, attention.reshape(branch_count, -1))


def solution(mesh):
    return jax.shard_map(
        shards,
        mesh=mesh,
        in_specs=(
            P("dp", "mp"),
            P(None, "mp"),
            P(None, "mp"),
            P(None, "mp"),
            P(),
            P(),
            P("dp", None, "mp", None),
            P(),
            P(),
            P(),
        ),
        out_specs=(P("dp", None, "mp", None), P("dp", "mp")),
        check_vma=False,
    )
```

```python
import functools
import math

import jax
import jax.numpy as jnp
from jax import lax
from jax.experimental import pallas as pl
from jax.experimental.pallas import tpu as pltpu
from jax.sharding import PartitionSpec as P

H = 64
KVH = 8
HD = 128
PAGE = 16
NPAGE = 48
CAP = 2
KEEP = 4
NZ = 4
ROUNDS = 40
LANES = 128
PREFIX = 8
FIRST = 2
REST = 2
PIECES = 2
ROOM = 48 * 1024 * 1024
NEVER = 1 << 20


def normalize(values, gain):
    return values * lax.rsqrt(jnp.mean(values * values, -1, keepdims=True) + 1e-06) * gain


def plan_kernel(groups, branch_count, parent_row, alive_row, parent_column, alive_column, out, state):
    ny = groups // NZ
    branches = groups * branch_count
    shifts = list(range(1, ny))
    slots = NZ * KEEP
    me = lax.axis_index("dp")

    def iota(shape, axis):
        return lax.broadcasted_iota(jnp.int32, shape, axis)

    square = (branches, branches)
    down_ids, across_ids = iota(square, 0), iota(square, 1)
    same = lax.div(down_ids, branch_count) == lax.div(across_ids, branch_count)
    alive_r, alive_c = alive_row[...] > 0, alive_column[...] > 0
    before = jnp.where(same & (down_ids < across_ids) & alive_c, 1, 0)
    item_row = jnp.sum(before, axis=0, keepdims=True)
    item_row = item_row + lax.div(iota((1, branches), 1), branch_count) * KEEP
    before = jnp.where(same & (across_ids < down_ids) & alive_r, 1, 0)
    item_column = jnp.sum(before, axis=1, keepdims=True)
    item_column = item_column + lax.div(iota((branches, 1), 0), branch_count) * KEEP
    wanted = jnp.sum(
        jnp.where(parent_column[...] == across_ids, item_row, 0), axis=1, keepdims=True
    )
    wanted = jnp.where(alive_c, -1, wanted)
    wide = (branches, LANES)
    local = lax.rem(iota(wide, 0), branch_count)
    takes = jnp.where(wanted == iota(wide, 1), local, -1)
    child = jnp.max(takes.reshape(groups, branch_count, LANES), axis=1)
    holds = jnp.where((item_column == iota(wide, 1)) & alive_c, local, -1)
    branch = jnp.max(holds, axis=0, keepdims=True)

    shape = (groups, LANES)
    here, item = iota(shape, 0), iota(shape, 1)
    z, y = lax.div(here, ny), lax.rem(here, ny)
    source = lax.div(item, KEEP)
    item_z, item_y = lax.div(source, ny), lax.rem(source, ny)
    on_line = item_y == y
    need = child >= 0

    def across(mask):
        return jnp.max(jnp.where(mask, 1, 0), axis=0, keepdims=True)

    top = jnp.max(jnp.where(need, z, -1), axis=0, keepdims=True)
    bottom = jnp.min(jnp.where(need, z, NZ), axis=0, keepdims=True)
    top_crosses = across(need & (z == top) & (item_y != y))
    bottom_crosses = across(need & (z == bottom) & (item_y != y))
    tie = LANES - 1 - item
    up_hops, down_hops = jnp.maximum(top - z, 0), jnp.maximum(z - bottom, 0)
    up_key = (up_hops * 2 + top_crosses) * LANES + tie
    down_key = (down_hops * 2 + bottom_crosses) * LANES + tie
    go_up, go_down = on_line & (up_hops > 0), on_line & (down_hops > 0)

    def beside(x, shift):
        return jnp.where(
            y + shift < ny, pltpu.roll(x, groups - shift, 0), pltpu.roll(x, (ny - shift) % groups, 0)
        )

    crosses = [on_line & (beside(child, shift) >= 0) for shift in shifts]
    own = source == here
    start = [go_up & own, go_down & own] + [c & own for c in crosses]
    rows = len(start)
    for i, mask in enumerate(start):
        state[i] = jnp.where(mask, 0, NEVER)
        state[rows + i] = jnp.full(shape, -1, jnp.int32)

    def choose(i, r, key):
        ready = state[i]
        key = jnp.where(ready <= r, key(ready), -1)
        best = jnp.max(key, axis=1, keepdims=True)
        chosen = (key == best) & (best >= 0)
        state[i] = jnp.where(chosen, NEVER, ready)
        state[rows + i] = jnp.where(chosen, r, state[rows + i])
        return jnp.where(chosen, 1, 0)

    def one_round(r):
        ups = choose(0, r, lambda ready: up_key)
        downs = choose(1, r, lambda ready: down_key)
        for i in range(2, rows):
            choose(i, r, lambda ready: (ROUNDS - ready) * LANES + tie)
        ups = jnp.where(z > 0, pltpu.roll(ups, ny, 0), 0) > 0
        downs = jnp.where(z < NZ - 1, pltpu.roll(downs, groups - ny, 0), 0) > 0
        rested = jnp.where(r < FIRST, FIRST, r + REST)
        state[0] = jnp.where(ups & go_up, rested, state[0])
        state[1] = jnp.where(downs & go_down, rested, state[1])
        left = jnp.minimum(state[0], state[1])
        for i, cross in enumerate(crosses):
            there = jnp.where((ups | downs) & cross, jnp.maximum(r + 1, FIRST), state[2 + i])
            state[2 + i] = there
            left = jnp.minimum(left, there)
        return r + 1, jnp.min(left)

    rounds, _ = lax.while_loop(
        lambda carry: (carry[1] < NEVER) & (carry[0] < ROUNDS),
        lambda carry: one_round(carry[0]),
        (jnp.int32(0), jnp.int32(0)),
    )

    def row_of(x, group):
        return jnp.max(jnp.where(here == group, x, -1), axis=0, keepdims=True)

    my_z = lax.div(me, ny)
    my_y = me - my_z * ny
    even = lax.rem(my_z, 2) == 0
    item = iota((1, LANES), 1)
    group = lax.div(item, KEEP)
    slot = lax.div(group, ny) * KEEP + lax.rem(item, KEEP)
    value = jnp.where(group == me, slots + branch, slot)
    taker = row_of(child, me)
    up_out, down_out = row_of(state[rows], me), row_of(state[rows + 1], me)
    up_in, down_in = row_of(state[rows], me - ny), row_of(state[rows + 1], me + ny)
    outs = [jnp.where(even, up_out, down_out), jnp.where(even, down_out, up_out)]
    ins = [jnp.where(even, down_in, up_in), jnp.where(even, up_in, down_in)]
    for shift in shifts:
        outs.append(row_of(state[rows + 1 + shift], me))
        from_y = lax.rem(my_y + ny - shift, ny)
        ins.append(row_of(state[rows + 1 + shift], my_z * ny + from_y))
    table = [(times, value) for times in outs]
    table += [(times, slot) for times in ins[:2]]
    table += [(times, taker) for times in ins]
    at = iota((ROUNDS, LANES), 0)
    lane = iota((ROUNDS, LANES), 1)
    result = jnp.full((ROUNDS, LANES), -1, jnp.int32)
    for c, (times, values) in enumerate(table):
        column = jnp.max(jnp.where(times == at, values, -1), axis=1, keepdims=True)
        result = jnp.where(lane == c, column, result)
    out[pl.ds(0, ROUNDS), :] = result
    extra = iota((8, LANES), 0)
    out[pl.ds(ROUNDS, 8), :] = jnp.where(
        extra == 0, rounds, jnp.where(extra == 1, branch, jnp.where(extra == 2, taker, 0))
    )


class Plan:
    def __init__(self, links, groups, branch_count):
        self.links = links
        self.width = 2 * links + 2
        self.rounds_at = ROUNDS * self.width
        self.branch_at = self.rounds_at + 1
        self.taker_at = self.branch_at + groups * KEEP
        self.pages_at = self.taker_at + groups * KEEP

    def send(self, table, r, l):
        return table[r * self.width + l]

    def save(self, table, r, l):
        return table[r * self.width + self.links + l]

    def taker(self, table, r, l):
        return table[r * self.width + self.links + 2 + l]

    def page(self, table, branch, p):
        return table[self.pages_at + branch * NPAGE + p]

    def kept(self, table, k):
        return table[self.branch_at + lax.axis_index("dp") * KEEP + k]

    def own_taker(self, table, k):
        return table[self.taker_at + lax.axis_index("dp") * KEEP + k]


def routing(parent, surviving, page_table, groups, branch_count, links):
    ny = groups // NZ
    rows = 2 + ny - 1
    out = pl.pallas_call(
        functools.partial(plan_kernel, groups, branch_count),
        out_shape=jax.ShapeDtypeStruct((ROUNDS + 8, LANES), jnp.int32),
        in_specs=[VMEM] * 4,
        out_specs=VMEM,
        scratch_shapes=[pltpu.VMEM((2 * rows, groups, LANES), jnp.int32)],
        compiler_params=pltpu.CompilerParams(vmem_limit_bytes=ROOM),
        cost_estimate=pl.CostEstimate(flops=0, bytes_accessed=6_000_000, transcendentals=0),
        name="plan",
    )(
        parent.reshape(1, -1),
        surviving.reshape(1, -1),
        parent.reshape(-1, 1),
        surviving.reshape(-1, 1),
    )
    pages = lax.dynamic_slice_in_dim(
        page_table, lax.axis_index("dp") * branch_count, branch_count, 0
    )
    items = groups * KEEP
    return jnp.concatenate(
        [
            out[:ROUNDS, : 2 * links + 2].reshape(-1),
            out[ROUNDS, :1],
            out[ROUNDS + 1, :items],
            out[ROUNDS + 2, :items],
            pages.reshape(-1),
        ]
    )


SMEM = pl.BlockSpec(memory_space=pltpu.SMEM)
VMEM = pl.BlockSpec(memory_space=pltpu.VMEM)
HBM = pl.BlockSpec(memory_space=pltpu.HBM)
ANY = pl.BlockSpec(memory_space=pl.ANY)


def first_kernel(groups, branch_count, facts, pool, *refs):
    ny = groups // NZ
    packed, table, load_sem, sem = refs[:-3], refs[-3], refs[-2], refs[-1]
    load = pltpu.make_async_copy(facts, table, load_sem)
    load.start()
    me = lax.axis_index("dp")
    z, y = me // ny, me % ny
    shape = (branch_count, groups * branch_count)
    child = lax.broadcasted_iota(jnp.int32, shape, 1)
    local = lax.broadcasted_iota(jnp.int32, shape, 0)
    column = lax.broadcasted_iota(jnp.int32, (branch_count, 1), 0)
    parent, surviving = facts[pl.ds(NPAGE, 1), :], facts[pl.ds(NPAGE + 1, 1), :]
    mine = (surviving == 0) & (parent == me * branch_count + local)
    target = lax.div(child, branch_count)
    target_z = lax.div(target, ny)
    target_y = target - target_z * ny

    def seen(mask):
        return jnp.max(mask.astype(jnp.int32), axis=1, keepdims=True)

    def leading(key):
        rows = []
        for _ in range(FIRST):
            best = jnp.max(key)
            rows.append(
                jnp.where(best >= 0, branch_count - 1 - lax.rem(best, branch_count), -1)
            )
            key = jnp.where(key == best, -1, key)
        return rows

    ways = []
    for steps in (target_z - z, z - target_z):
        hops = jnp.max(jnp.where(mine, steps, 0), axis=1, keepdims=True)
        far_across = seen(mine & (steps == hops) & (target_y != y))
        key = (hops * 2 + far_across) * branch_count + branch_count - 1 - column
        ways.append(leading(jnp.where(hops > 0, key, -1)))
    even = lax.rem(z, 2) == 0
    sends = [
        [jnp.where(even, u, d) for u, d in zip(*ways)],
        [jnp.where(even, d, u) for u, d in zip(*ways)],
    ]
    for shift in range(1, ny):
        to = lax.rem(y + shift, ny)
        crossing = seen(mine & (target_z == z) & (target_y == to))
        sends.append(leading(jnp.where(crossing > 0, branch_count - 1 - column, -1)))
    load.wait()
    for l, rows in enumerate(sends):
        for r, row in enumerate(rows):

            @pl.when(row >= 0)
            def _():
                for p in range(NPAGE):
                    page = table[p, me * branch_count + row]
                    pltpu.make_async_copy(
                        pool.at[page], packed[l].at[r * NPAGE + p], sem.at[l, r]
                    ).start()

    for l, rows in enumerate(sends):
        for r, row in enumerate(rows):
            box = packed[l].at[pl.ds(r * NPAGE, NPAGE)]

            @pl.when(row >= 0)
            def _():
                pltpu.make_async_copy(box, box, sem.at[l, r]).wait()


def first_windows(groups, branch_count, facts, pool):
    links = 2 + groups // NZ - 1
    windows = jax.ShapeDtypeStruct((FIRST * NPAGE,) + pool.shape[1:], pool.dtype)
    return pl.pallas_call(
        functools.partial(first_kernel, groups, branch_count),
        out_shape=[windows] * links,
        in_specs=[VMEM, HBM],
        out_specs=[VMEM] * links,
        scratch_shapes=[
            pltpu.SMEM(facts.shape, facts.dtype),
            pltpu.SemaphoreType.DMA,
            pltpu.SemaphoreType.DMA((links, FIRST)),
        ],
        compiler_params=pltpu.CompilerParams(vmem_limit_bytes=ROOM),
        cost_estimate=pl.CostEstimate(flops=0, bytes_accessed=6_000_000, transcendentals=0),
        name="first_windows",
    )(facts, pool)


def step_kernel(plan, packs, files, traced, count, filing, attending, *refs):
    if traced:
        at, refs = refs[0][0], refs[1:]
        packs = [(at,) + entry[1:] for entry in packs]
        files = [(at,) + entry[1:] for entry in files]
    links = plan.links
    table = refs[0]
    arrived = refs[1 : 1 + count]
    pool, rows = refs[1 + count : 3 + count]
    store, refilled, out = refs[6 + count : 9 + count]
    packed = refs[9 + count : -8]
    row, result, row_sem, out_sem, file_sem, save_sem, pack_sem, fresh_sem = refs[-8:]
    slots = NZ * KEEP

    comes = []
    for r, l, first, pages, array, offset in files:
        part = arrived[array].at[pl.ds(offset, pages)]
        save = plan.save(table, r, l) if l < 2 else None
        comes.append((save, plan.taker(table, r, l), part, first, pages))

    def is_fresh(source):
        fresh = [source == save for save, _, _, _, _ in comes if save is not None]
        return (source >= 0) & functools.reduce(jnp.logical_or, fresh) if fresh else False

    goes = []
    for r, first, pages, which in packs:
        for l in which:
            goes.append((plan.send(table, r, l), packed[len(goes)], first, pages))

    for i, (source, box, first, pages) in enumerate(goes):

        @pl.when(source >= slots)
        def _():
            @pl.loop(0, pages, unroll=8)
            def _(p):
                page = plan.page(table, source - slots, first + p)
                pltpu.make_async_copy(pool.at[page], box.at[p], pack_sem.at[i]).start()

        @pl.when((source >= 0) & (source < slots) & jnp.logical_not(is_fresh(source)))
        def _():
            pltpu.make_async_copy(
                store.at[jnp.clip(source, 0, slots - 1), pl.ds(first, pages)],
                box,
                pack_sem.at[i],
            ).start()

        for save, _, part, file_first, file_pages in comes:
            if save is not None and file_first <= first < file_first + file_pages:

                @pl.when((source >= 0) & (source == save))
                def _():
                    pltpu.make_async_copy(
                        part.at[pl.ds(first - file_first, pages)], box, fresh_sem.at[i]
                    ).start()

    for i, (save, taker, part, first, pages) in enumerate(comes if filing else []):
        if save is not None:

            @pl.when(save >= 0)
            def _():
                pltpu.make_async_copy(
                    part, store.at[jnp.maximum(save, 0), pl.ds(first, pages)], save_sem.at[i]
                ).start()

        @pl.when(taker >= 0)
        def _():
            if attending:
                pltpu.make_async_copy(rows.at[taker], row.at[i], row_sem.at[i]).start()

            @pl.loop(0, pages, unroll=8)
            def _(p):
                page = plan.page(table, taker, first + p)
                pltpu.make_async_copy(part.at[p], refilled.at[page], file_sem.at[i]).start()

    if attending:
        attend_to(
            [taker for _, taker, _, _, _ in comes],
            [part for _, _, part, _, _ in comes],
            row,
            result,
            row_sem,
            out,
            out_sem,
        )

    for i, (source, box, first, pages) in enumerate(goes):

        @pl.when((source >= 0) & jnp.logical_not(is_fresh(source)))
        def _():
            pltpu.make_async_copy(box, box, pack_sem.at[i]).wait()

        if comes:

            @pl.when(is_fresh(source))
            def _():
                pltpu.make_async_copy(box, box, fresh_sem.at[i]).wait()

    for i, (save, taker, part, first, pages) in enumerate(comes if filing else []):
        if save is not None:

            @pl.when(save >= 0)
            def _():
                pltpu.make_async_copy(part, part, save_sem.at[i]).wait()

        @pl.when(taker >= 0)
        def _():
            pltpu.make_async_copy(part, part, file_sem.at[i]).wait()


def step(plan, packs, files, at, table, arrived, pool, rows, store, refilled, attention, filing=True, attending=False):
    at = [] if at is None else [jnp.stack([at])]
    count = len(arrived)
    lead = len(at) + 1 + count
    heads = rows.shape[2]
    boxes = [
        jax.ShapeDtypeStruct((pages,) + pool.shape[1:], pool.dtype)
        for _, _, pages, which in packs
        for _ in which
    ]
    some = max(len(files), 1)
    out = pl.pallas_call(
        functools.partial(step_kernel, plan, packs, files, bool(at), count, filing, attending),
        out_shape=[
            jax.ShapeDtypeStruct(array.shape, array.dtype) for array in (store, refilled, attention)
        ]
        + boxes,
        in_specs=[SMEM] * (len(at) + 1) + [VMEM] * count + [HBM, ANY, HBM, HBM, ANY],
        out_specs=[HBM] * 2 + [ANY] + [VMEM] * len(boxes),
        scratch_shapes=[
            pltpu.VMEM((some, 3, heads, HD), rows.dtype),
            pltpu.VMEM((some, heads, HD), attention.dtype),
        ]
        + [pltpu.SemaphoreType.DMA((some,))] * 4
        + [pltpu.SemaphoreType.DMA((max(len(boxes), 1),))] * 2,
        input_output_aliases={lead + 2: 0, lead + 3: 1, lead + 4: 2},
        compiler_params=pltpu.CompilerParams(vmem_limit_bytes=ROOM),
        cost_estimate=pl.CostEstimate(flops=0, bytes_accessed=6_000_000, transcendentals=0),
        name="step",
    )(*at, table, *arrived, pool, rows, store, refilled, attention)
    return out[0], out[1], out[2], list(out[3:])


def own_kernel(plan, table, pool, token, refilled, store, window, in_sem, out_sem):
    moves = [
        (plan.kept(table, k), [plan.kept(table, k), plan.own_taker(table, k)]) for k in range(KEEP)
    ]
    for k, (source, _) in enumerate(moves):

        @pl.when(source >= 0)
        def _():
            @pl.loop(0, NPAGE, unroll=8)
            def _(p):
                pltpu.make_async_copy(
                    pool.at[plan.page(table, source, p)], window.at[k, p], in_sem.at[k]
                ).start()

    for k, (source, targets) in enumerate(moves):

        @pl.when(source >= 0)
        def _():
            pltpu.make_async_copy(window.at[k], window.at[k], in_sem.at[k]).wait()

        for lane, to in enumerate(targets):

            @pl.when((source >= 0) & (to >= 0))
            def _():
                @pl.loop(0, NPAGE, unroll=8)
                def _(p):
                    pltpu.make_async_copy(
                        window.at[k, p], refilled.at[plan.page(table, to, p)], out_sem.at[k, lane]
                    ).start()

    for k, (source, targets) in enumerate(moves):
        for lane, to in enumerate(targets):

            @pl.when((source >= 0) & (to >= 0))
            def _():
                pltpu.make_async_copy(window.at[k], window.at[k], out_sem.at[k, lane]).wait()


def own_windows(plan, table, pool, token):
    return pl.pallas_call(
        functools.partial(own_kernel, plan),
        out_shape=[
            jax.ShapeDtypeStruct(pool.shape, pool.dtype),
            jax.ShapeDtypeStruct((NZ * KEEP, NPAGE) + pool.shape[1:], pool.dtype),
        ],
        in_specs=[SMEM, HBM, ANY],
        out_specs=[HBM] * 2,
        scratch_shapes=[
            pltpu.VMEM((KEEP, NPAGE) + pool.shape[1:], pool.dtype),
            pltpu.SemaphoreType.DMA((KEEP,)),
            pltpu.SemaphoreType.DMA((KEEP, 2)),
        ],
        compiler_params=pltpu.CompilerParams(vmem_limit_bytes=ROOM),
        cost_estimate=pl.CostEstimate(flops=0, bytes_accessed=9_000_000, transcendentals=0),
        name="own_windows",
    )(table, pool, token)


def attend_to(branch, windows, row, result, row_sem, out, out_sem):
    count = len(branch)
    for i in range(count):

        @pl.when(branch[i] >= 0)
        def _():
            pltpu.make_async_copy(row.at[i], row.at[i], row_sem.at[i]).wait()

    @pl.when(functools.reduce(jnp.maximum, branch) >= 0)
    def _():
        kv = windows[0].shape[2]
        tokens = NPAGE * PAGE * kv
        flat = [
            window[:, :, 0, :].reshape(tokens, 2 * HD) if kv == 1 else window.reshape(tokens, 2 * HD)
            for window in windows
        ]
        query = [row[i, 0] for i in range(count)]
        scores = [
            lax.dot_general(
                query[i], flat[i][:, :HD], (((1,), (1,)), ((), ())), preferred_element_type=jnp.float32
            )
            for i in range(count)
        ]
        token = lax.broadcasted_iota(jnp.int32, scores[0].shape, 1)
        head = lax.broadcasted_iota(jnp.int32, scores[0].shape, 0)
        fits = (token & (kv - 1)) == lax.div(head, H // KVH)
        for i in range(count):
            masked = jnp.where(fits, scores[i], -jnp.inf)
            own = jnp.sum(
                query[i].astype(jnp.float32) * row[i, 1].astype(jnp.float32), -1, keepdims=True
            )
            peak = jnp.maximum(jnp.max(masked, -1, keepdims=True), own)
            terms = jnp.exp(masked - peak)
            own_term = jnp.exp(own - peak)
            total = jnp.sum(terms, -1, keepdims=True) + own_term
            weights = (terms / total).astype(jnp.bfloat16)
            own_weight = (own_term / total).astype(jnp.bfloat16).astype(jnp.float32)
            mixed = jnp.dot(weights, flat[i][:, HD:], preferred_element_type=jnp.float32)
            mixed = mixed + own_weight * row[i, 2].astype(jnp.float32)
            result[i] = mixed.astype(result.dtype)

    for i in range(count):

        @pl.when(branch[i] >= 0)
        def _():
            pltpu.make_async_copy(result.at[i], out.at[branch[i]], out_sem.at[i]).start()

    for i in range(count):

        @pl.when(branch[i] >= 0)
        def _():
            pltpu.make_async_copy(result.at[i], result.at[i], out_sem.at[i]).wait()


def attend_kernel(plan, whom, traced, *refs):
    if traced:
        at, refs = refs[0][0], refs[1:]
        whom = [(at, l) for _, l in whom]
    table, rows, refilled = refs[:3]
    out, window, row, result, sem, row_sem, out_sem = refs[-7:]
    own = [plan.own_taker(table, k) for k in range(KEEP)]
    takers = []
    for _ in range(CAP):
        taker = functools.reduce(jnp.maximum, own)
        own = [jnp.where(other == taker, -1, other) for other in own]
        takers.append(taker)
    branch = []
    for r, i in whom:
        if r is None:
            branch.append(plan.kept(table, i) if i < KEEP else takers[i - KEEP])
        else:
            branch.append(plan.taker(table, r, i))
    for i, who in enumerate(branch):

        @pl.when(who >= 0)
        def _():
            pltpu.make_async_copy(rows.at[who], row.at[i], row_sem.at[i]).start()

            @pl.loop(0, NPAGE, unroll=8)
            def _(p):
                pltpu.make_async_copy(
                    refilled.at[plan.page(table, who, p)], window.at[i, p], sem.at[i]
                ).start()

    for i, who in enumerate(branch):

        @pl.when(who >= 0)
        def _():
            pltpu.make_async_copy(window.at[i], window.at[i], sem.at[i]).wait()

    attend_to(
        branch, [window.at[i] for i in range(len(branch))], row, result, row_sem, out, out_sem
    )


def attend(plan, whom, at, table, rows, refilled, before):
    at = [] if at is None else [jnp.stack([at])]
    count = len(whom)
    heads = rows.shape[2]
    lead = len(at)
    return pl.pallas_call(
        functools.partial(attend_kernel, plan, whom, bool(at)),
        out_shape=jax.ShapeDtypeStruct((rows.shape[0], heads, HD), jnp.bfloat16),
        in_specs=[SMEM] * (lead + 1) + [ANY, HBM] + [ANY] * len(before),
        out_specs=ANY,
        scratch_shapes=[
            pltpu.VMEM((count, NPAGE) + refilled.shape[1:], refilled.dtype),
            pltpu.VMEM((count, 3, heads, HD), rows.dtype),
            pltpu.VMEM((count, heads, HD), jnp.bfloat16),
            pltpu.SemaphoreType.DMA((count,)),
            pltpu.SemaphoreType.DMA((count,)),
            pltpu.SemaphoreType.DMA((count,)),
        ],
        input_output_aliases={lead + 3: 0} if before else {},
        compiler_params=pltpu.CompilerParams(vmem_limit_bytes=ROOM),
        cost_estimate=pl.CostEstimate(
            flops=count * 2 * 2 * 16 * 1536 * 128, bytes_accessed=count * 800_000, transcendentals=0
        ),
        name="attend",
    )(*at, table, rows, refilled, *before)


def token_rows(hidden, w_query, w_key, w_value, query_gain, key_gain):
    features = lax.all_gather(hidden, "mp", axis=1, tiled=True)
    branch_count = features.shape[0]
    head_group = H // KVH
    heads = w_query.shape[1] // HD
    kv_local = w_key.shape[1] // HD
    query_full = jnp.dot(features, w_query, preferred_element_type=jnp.float32)
    query_full = query_full.reshape(branch_count, heads, HD)
    query_rows = (normalize(query_full, query_gain) / math.sqrt(HD)).astype(jnp.bfloat16)
    key_full = jnp.dot(features, w_key, preferred_element_type=jnp.float32)
    key_rows = normalize(key_full.reshape(branch_count, kv_local, HD), key_gain).astype(jnp.bfloat16)
    value_rows = jnp.dot(features, w_value, preferred_element_type=jnp.float32)
    value_rows = value_rows.reshape(branch_count, kv_local, HD).astype(jnp.bfloat16)
    return jnp.stack(
        [
            query_rows,
            jnp.repeat(key_rows, head_group, axis=1),
            jnp.repeat(value_rows, head_group, axis=1),
        ],
        axis=1,
    )


def shards(
    hidden, w_query, w_key, w_value, query_gain, key_gain, kv_pool, page_table, parent, surviving
):
    groups = lax.axis_size("dp")
    me = lax.axis_index("dp")
    ny = groups // NZ
    branch_count = hidden.shape[0]
    links = 2 + ny - 1
    facts = jnp.concatenate(
        [page_table.T, parent[None], surviving[None], jnp.zeros((6, parent.shape[0]), jnp.int32)]
    )
    packed = first_windows(groups, branch_count, facts, kv_pool)
    parent, surviving, page_table, packed = lax.optimization_barrier(
        (parent, surviving, page_table, packed)
    )
    sides = lax.axis_size("mp")

    def everywhere(move):
        return [
            (g * sides + m, to[0] * sides + to[1])
            for g in range(groups)
            for m in range(sides)
            for to in [move(g, m)]
        ]

    def outer(g, m):
        return g + ny if g // ny % 2 == 0 else g - ny, m

    def inner(g, m):
        if g // ny in (0, NZ - 1):
            return g, m ^ 1
        return g + ny if g // ny % 2 else g - ny, m

    def sideways(shift):
        return lambda g, m: (g // ny * ny + (g % ny + shift) % ny, m)

    pairs = [everywhere(outer), everywhere(inner)]
    pairs += [everywhere(sideways(shift)) for shift in range(1, ny)]
    along, beside, every = [0, 1], list(range(2, links)), list(range(links))

    def travel(packed, which):
        return [lax.ppermute(window, ("dp", "mp"), pairs[l]) for window, l in zip(packed, which)]

    arrived = travel(packed, every)
    plan = Plan(links, groups, branch_count)
    table = routing(parent, surviving, page_table, groups, branch_count, links)
    rounds = table[plan.rounds_at]
    refilled, store = own_windows(plan, table, kv_pool, packed[0])
    rows = token_rows(hidden, w_query, w_key, w_value, query_gain, key_gain)
    waiting = [[(None, i) for i in range(3)], [(None, i) for i in range(3, KEEP + CAP)]]
    waiting += [[(r, l) for l in every] for r in range(FIRST)]

    def attend_next(attention):
        return attend(plan, waiting.pop(0), None, table, rows, refilled, attention)

    attention = attend_next([])
    files = [(r, l, 0, NPAGE, l, r * NPAGE) for r in range(FIRST) for l in every]
    store, refilled, attention, packed = step(
        plan,
        [(FIRST, 0, NPAGE, every)],
        [file for file in files if file[1] in along],
        None,
        table,
        arrived[:2],
        kv_pool,
        rows,
        store,
        refilled,
        attention,
        filing=False,
    )
    moved = travel(packed, every)
    for r in range(FIRST, PREFIX):
        if r > FIRST:
            files = [(r - 1, l, 0, NPAGE, l, 0) for l in along]
            files += [(r - 2, l, 0, NPAGE, l, 0) for l in beside if r - 2 >= FIRST]
            arrived = came_along + came_beside
        packs = [(r, 0, NPAGE, beside)] if r > FIRST else []
        packs += [(r + 1, 0, NPAGE, along)] if r + 1 < PREFIX else []
        rest = r + 1 == PREFIX
        store, refilled, attention, packed = step(
            plan, packs, files, None, table, arrived, kv_pool, rows, store, refilled, attention, filing=not rest
        )
        if rest:
            store, refilled, attention, _ = step(
                plan, [], files, None, table, arrived, kv_pool, rows, store, refilled, attention
            )
        if r > FIRST:
            came_along, came_beside = moving_along, moving_beside
            moving_beside = travel(packed[: len(beside)], beside)
            packed = packed[len(beside) :]
            waiting.append([(at, l) for at, l, _, _, _, _ in files])
        else:
            came_along, came_beside, moving_beside = moved[:2], [], moved[2:]
        if packed:
            if came_beside:
                packed, came_beside = lax.optimization_barrier((packed, came_beside))
            moving_along = travel(packed, along)
        for _ in range(2 if len(waiting) > 1 else 1):
            attention = attend_next([attention])
    while waiting:
        attention = attend_next([attention])
    last = PREFIX - 1
    endings = [(last - 1, beside, came_beside), (last, along, came_along), (last, beside, moving_beside)]
    for r, which, arrived in endings:
        files = [(r, l, 0, NPAGE, i, 0) for i, l in enumerate(which)]
        store, refilled, attention, _ = step(
            plan, [], files, None, table, arrived, kv_pool, rows, store, refilled, attention, attending=True
        )

    def more(state):
        return state[0] < rounds

    def one_round(state):
        r, store, refilled, attention = state
        part = NPAGE // PIECES
        moving = []
        for piece in range(PIECES):
            store, refilled, attention, packed = step(
                plan, [(None, piece * part, part, every)], [], r, table, [], kv_pool, rows, store, refilled, attention
            )
            moving.append(travel(packed, every))
        for piece in range(PIECES):
            files = [(None, l, piece * part, part, l, 0) for l in every]
            store, refilled, attention, _ = step(
                plan, [], files, r, table, moving.pop(0), kv_pool, rows, store, refilled, attention
            )
        attention = attend(plan, [(r, l) for l in every], r, table, rows, refilled, [attention])
        return r + 1, store, refilled, attention

    _, store, refilled, attention = lax.while_loop(
        more, one_round, (jnp.int32(PREFIX), store, refilled, attention)
    )
    return (refilled, attention.reshape(branch_count, -1))


def solution(mesh):
    return jax.shard_map(
        shards,
        mesh=mesh,
        in_specs=(
            P("dp", "mp"),
            P(None, "mp"),
            P(None, "mp"),
            P(None, "mp"),
            P(),
            P(),
            P("dp", None, "mp", None),
            P(),
            P(),
            P(),
        ),
        out_specs=(P("dp", None, "mp", None), P("dp", "mp")),
        check_vma=False,
    )
```

```python
import functools
import math

import jax
import jax.numpy as jnp
from jax import lax
from jax.experimental import pallas as pl
from jax.experimental.pallas import tpu as pltpu
from jax.sharding import PartitionSpec as P

H = 64
KVH = 8
HD = 128
PAGE = 16
NPAGE = 48
CAP = 2
KEEP = 4
NZ = 4
ROUNDS = 40
LANES = 128
PREFIX = 8
FIRST = 2
REST = 2
PIECES = 2
LITTLE = 24 * 1024 * 1024
ROOM = 44 * 1024 * 1024
MUCH = 52 * 1024 * 1024
NEVER = 1 << 20


def normalize(values, gain):
    return values * lax.rsqrt(jnp.mean(values * values, -1, keepdims=True) + 1e-06) * gain


def plan_kernel(groups, branch_count, parent_row, alive_row, parent_column, alive_column, out, state):
    ny = groups // NZ
    branches = groups * branch_count
    shifts = list(range(1, ny))
    slots = NZ * KEEP
    me = lax.axis_index("dp")

    def iota(shape, axis):
        return lax.broadcasted_iota(jnp.int32, shape, axis)

    square = (branches, branches)
    down_ids, across_ids = iota(square, 0), iota(square, 1)
    same = lax.div(down_ids, branch_count) == lax.div(across_ids, branch_count)
    alive_r, alive_c = alive_row[...] > 0, alive_column[...] > 0
    before = jnp.where(same & (down_ids < across_ids) & alive_c, 1, 0)
    item_row = jnp.sum(before, axis=0, keepdims=True)
    item_row = item_row + lax.div(iota((1, branches), 1), branch_count) * KEEP
    before = jnp.where(same & (across_ids < down_ids) & alive_r, 1, 0)
    item_column = jnp.sum(before, axis=1, keepdims=True)
    item_column = item_column + lax.div(iota((branches, 1), 0), branch_count) * KEEP
    wanted = jnp.sum(
        jnp.where(parent_column[...] == across_ids, item_row, 0), axis=1, keepdims=True
    )
    wanted = jnp.where(alive_c, -1, wanted)
    wide = (branches, LANES)
    local = lax.rem(iota(wide, 0), branch_count)
    takes = jnp.where(wanted == iota(wide, 1), local, -1)
    child = jnp.max(takes.reshape(groups, branch_count, LANES), axis=1)
    holds = jnp.where((item_column == iota(wide, 1)) & alive_c, local, -1)
    branch = jnp.max(holds, axis=0, keepdims=True)

    shape = (groups, LANES)
    here, item = iota(shape, 0), iota(shape, 1)
    z, y = lax.div(here, ny), lax.rem(here, ny)
    source = lax.div(item, KEEP)
    item_z, item_y = lax.div(source, ny), lax.rem(source, ny)
    on_line = item_y == y
    need = child >= 0

    def across(mask):
        return jnp.max(jnp.where(mask, 1, 0), axis=0, keepdims=True)

    top = jnp.max(jnp.where(need, z, -1), axis=0, keepdims=True)
    bottom = jnp.min(jnp.where(need, z, NZ), axis=0, keepdims=True)
    top_crosses = across(need & (z == top) & (item_y != y))
    bottom_crosses = across(need & (z == bottom) & (item_y != y))
    tie = LANES - 1 - item
    up_hops, down_hops = jnp.maximum(top - z, 0), jnp.maximum(z - bottom, 0)
    up_key = (up_hops * 2 + top_crosses) * LANES + tie
    down_key = (down_hops * 2 + bottom_crosses) * LANES + tie
    go_up, go_down = on_line & (up_hops > 0), on_line & (down_hops > 0)

    def beside(x, shift):
        return jnp.where(
            y + shift < ny, pltpu.roll(x, groups - shift, 0), pltpu.roll(x, (ny - shift) % groups, 0)
        )

    crosses = [on_line & (beside(child, shift) >= 0) for shift in shifts]
    own = source == here
    start = [go_up & own, go_down & own] + [c & own for c in crosses]
    rows = len(start)
    for i, mask in enumerate(start):
        state[i] = jnp.where(mask, 0, NEVER)
        state[rows + i] = jnp.full(shape, -1, jnp.int32)

    def choose(i, r, key):
        ready = state[i]
        key = jnp.where(ready <= r, key(ready), -1)
        best = jnp.max(key, axis=1, keepdims=True)
        chosen = (key == best) & (best >= 0)
        state[i] = jnp.where(chosen, NEVER, ready)
        state[rows + i] = jnp.where(chosen, r, state[rows + i])
        return jnp.where(chosen, 1, 0)

    def one_round(r):
        ups = choose(0, r, lambda ready: up_key)
        downs = choose(1, r, lambda ready: down_key)
        for i in range(2, rows):
            choose(i, r, lambda ready: (ROUNDS - ready) * LANES + tie)
        ups = jnp.where(z > 0, pltpu.roll(ups, ny, 0), 0) > 0
        downs = jnp.where(z < NZ - 1, pltpu.roll(downs, groups - ny, 0), 0) > 0
        rested = jnp.where(r < FIRST, FIRST, r + REST)
        state[0] = jnp.where(ups & go_up, rested, state[0])
        state[1] = jnp.where(downs & go_down, rested, state[1])
        left = jnp.minimum(state[0], state[1])
        for i, cross in enumerate(crosses):
            there = jnp.where((ups | downs) & cross, jnp.maximum(r + 1, FIRST), state[2 + i])
            state[2 + i] = there
            left = jnp.minimum(left, there)
        return r + 1, jnp.min(left)

    rounds, _ = lax.while_loop(
        lambda carry: (carry[1] < NEVER) & (carry[0] < ROUNDS),
        lambda carry: one_round(carry[0]),
        (jnp.int32(0), jnp.int32(0)),
    )

    def row_of(x, group):
        return jnp.max(jnp.where(here == group, x, -1), axis=0, keepdims=True)

    my_z = lax.div(me, ny)
    my_y = me - my_z * ny
    even = lax.rem(my_z, 2) == 0
    item = iota((1, LANES), 1)
    group = lax.div(item, KEEP)
    slot = lax.div(group, ny) * KEEP + lax.rem(item, KEEP)
    value = jnp.where(group == me, slots + branch, slot)
    taker = row_of(child, me)
    up_out, down_out = row_of(state[rows], me), row_of(state[rows + 1], me)
    up_in, down_in = row_of(state[rows], me - ny), row_of(state[rows + 1], me + ny)
    outs = [jnp.where(even, up_out, down_out), jnp.where(even, down_out, up_out)]
    ins = [jnp.where(even, down_in, up_in), jnp.where(even, up_in, down_in)]
    for shift in shifts:
        outs.append(row_of(state[rows + 1 + shift], me))
        from_y = lax.rem(my_y + ny - shift, ny)
        ins.append(row_of(state[rows + 1 + shift], my_z * ny + from_y))
    table = [(times, value) for times in outs]
    table += [(times, slot) for times in ins[:2]]
    table += [(times, taker) for times in ins]
    at = iota((ROUNDS, LANES), 0)
    lane = iota((ROUNDS, LANES), 1)
    result = jnp.full((ROUNDS, LANES), -1, jnp.int32)
    for c, (times, values) in enumerate(table):
        column = jnp.max(jnp.where(times == at, values, -1), axis=1, keepdims=True)
        result = jnp.where(lane == c, column, result)
    out[pl.ds(0, ROUNDS), :] = result
    extra = iota((8, LANES), 0)
    out[pl.ds(ROUNDS, 8), :] = jnp.where(
        extra == 0, rounds, jnp.where(extra == 1, branch, jnp.where(extra == 2, taker, 0))
    )


class Plan:
    def __init__(self, links, groups, branch_count):
        self.links = links
        self.width = 2 * links + 2
        self.rounds_at = ROUNDS * self.width
        self.branch_at = self.rounds_at + 1
        self.taker_at = self.branch_at + groups * KEEP
        self.pages_at = self.taker_at + groups * KEEP

    def send(self, table, r, l):
        return table[r * self.width + l]

    def save(self, table, r, l):
        return table[r * self.width + self.links + l]

    def taker(self, table, r, l):
        return table[r * self.width + self.links + 2 + l]

    def page(self, table, branch, p):
        return table[self.pages_at + branch * NPAGE + p]

    def kept(self, table, k):
        return table[self.branch_at + lax.axis_index("dp") * KEEP + k]

    def own_taker(self, table, k):
        return table[self.taker_at + lax.axis_index("dp") * KEEP + k]


def routing(parent, surviving, page_table, groups, branch_count, links):
    ny = groups // NZ
    rows = 2 + ny - 1
    out = pl.pallas_call(
        functools.partial(plan_kernel, groups, branch_count),
        out_shape=jax.ShapeDtypeStruct((ROUNDS + 8, LANES), jnp.int32),
        in_specs=[VMEM] * 4,
        out_specs=VMEM,
        scratch_shapes=[pltpu.VMEM((2 * rows, groups, LANES), jnp.int32)],
        compiler_params=pltpu.CompilerParams(vmem_limit_bytes=LITTLE),
        cost_estimate=pl.CostEstimate(flops=0, bytes_accessed=6_000_000, transcendentals=0),
        name="plan",
    )(
        parent.reshape(1, -1),
        surviving.reshape(1, -1),
        parent.reshape(-1, 1),
        surviving.reshape(-1, 1),
    )
    pages = lax.dynamic_slice_in_dim(
        page_table, lax.axis_index("dp") * branch_count, branch_count, 0
    )
    items = groups * KEEP
    return jnp.concatenate(
        [
            out[:ROUNDS, : 2 * links + 2].reshape(-1),
            out[ROUNDS, :1],
            out[ROUNDS + 1, :items],
            out[ROUNDS + 2, :items],
            pages.reshape(-1),
        ]
    )


SMEM = pl.BlockSpec(memory_space=pltpu.SMEM)
VMEM = pl.BlockSpec(memory_space=pltpu.VMEM)
HBM = pl.BlockSpec(memory_space=pltpu.HBM)
ANY = pl.BlockSpec(memory_space=pl.ANY)


def first_kernel(groups, branch_count, facts, pool, *refs):
    ny = groups // NZ
    packed, table, load_sem, sem = refs[:-3], refs[-3], refs[-2], refs[-1]
    load = pltpu.make_async_copy(facts, table, load_sem)
    load.start()
    me = lax.axis_index("dp")
    z, y = me // ny, me % ny
    shape = (branch_count, groups * branch_count)
    child = lax.broadcasted_iota(jnp.int32, shape, 1)
    local = lax.broadcasted_iota(jnp.int32, shape, 0)
    column = lax.broadcasted_iota(jnp.int32, (branch_count, 1), 0)
    parent, surviving = facts[pl.ds(NPAGE, 1), :], facts[pl.ds(NPAGE + 1, 1), :]
    mine = (surviving == 0) & (parent == me * branch_count + local)
    target = lax.div(child, branch_count)
    target_z = lax.div(target, ny)
    target_y = target - target_z * ny

    def seen(mask):
        return jnp.max(mask.astype(jnp.int32), axis=1, keepdims=True)

    def leading(key):
        rows = []
        for _ in range(FIRST):
            best = jnp.max(key)
            rows.append(
                jnp.where(best >= 0, branch_count - 1 - lax.rem(best, branch_count), -1)
            )
            key = jnp.where(key == best, -1, key)
        return rows

    ways = []
    for steps in (target_z - z, z - target_z):
        hops = jnp.max(jnp.where(mine, steps, 0), axis=1, keepdims=True)
        far_across = seen(mine & (steps == hops) & (target_y != y))
        key = (hops * 2 + far_across) * branch_count + branch_count - 1 - column
        ways.append(leading(jnp.where(hops > 0, key, -1)))
    even = lax.rem(z, 2) == 0
    sends = [
        [jnp.where(even, u, d) for u, d in zip(*ways)],
        [jnp.where(even, d, u) for u, d in zip(*ways)],
    ]
    for shift in range(1, ny):
        to = lax.rem(y + shift, ny)
        crossing = seen(mine & (target_z == z) & (target_y == to))
        sends.append(leading(jnp.where(crossing > 0, branch_count - 1 - column, -1)))
    load.wait()
    for l, rows in enumerate(sends):
        for r, row in enumerate(rows):

            @pl.when(row >= 0)
            def _():
                for p in range(NPAGE):
                    page = table[p, me * branch_count + row]
                    pltpu.make_async_copy(
                        pool.at[page], packed[l].at[r * NPAGE + p], sem.at[l, r]
                    ).start()

    for l, rows in enumerate(sends):
        for r, row in enumerate(rows):
            box = packed[l].at[pl.ds(r * NPAGE, NPAGE)]

            @pl.when(row >= 0)
            def _():
                pltpu.make_async_copy(box, box, sem.at[l, r]).wait()


def first_windows(groups, branch_count, facts, pool):
    links = 2 + groups // NZ - 1
    windows = jax.ShapeDtypeStruct((FIRST * NPAGE,) + pool.shape[1:], pool.dtype)
    return pl.pallas_call(
        functools.partial(first_kernel, groups, branch_count),
        out_shape=[windows] * links,
        in_specs=[VMEM, HBM],
        out_specs=[VMEM] * links,
        scratch_shapes=[
            pltpu.SMEM(facts.shape, facts.dtype),
            pltpu.SemaphoreType.DMA,
            pltpu.SemaphoreType.DMA((links, FIRST)),
        ],
        compiler_params=pltpu.CompilerParams(vmem_limit_bytes=LITTLE),
        cost_estimate=pl.CostEstimate(flops=0, bytes_accessed=6_000_000, transcendentals=0),
        name="first_windows",
    )(facts, pool)


def step_kernel(plan, packs, files, traced, count, filing, attending, *refs):
    if traced:
        at, refs = refs[0][0], refs[1:]
        packs = [(at,) + entry[1:] for entry in packs]
        files = [(at,) + entry[1:] for entry in files]
    links = plan.links
    table = refs[0]
    arrived = refs[1 : 1 + count]
    pool, rows = refs[1 + count : 3 + count]
    store, refilled, out = refs[6 + count : 9 + count]
    packed = refs[9 + count : -8]
    row, result, row_sem, out_sem, file_sem, save_sem, pack_sem, fresh_sem = refs[-8:]
    slots = NZ * KEEP

    comes = []
    for r, l, first, pages, array, offset in files:
        part = arrived[array].at[pl.ds(offset, pages)]
        save = plan.save(table, r, l) if l < 2 else None
        comes.append((save, plan.taker(table, r, l), part, first, pages))

    def is_fresh(source):
        fresh = [source == save for save, _, _, _, _ in comes if save is not None]
        return (source >= 0) & functools.reduce(jnp.logical_or, fresh) if fresh else False

    goes = []
    for r, first, pages, which in packs:
        for l in which:
            goes.append((plan.send(table, r, l), packed[len(goes)], first, pages))

    for i, (source, box, first, pages) in enumerate(goes):

        @pl.when(source >= slots)
        def _():
            @pl.loop(0, pages, unroll=8)
            def _(p):
                page = plan.page(table, source - slots, first + p)
                pltpu.make_async_copy(pool.at[page], box.at[p], pack_sem.at[i]).start()

        @pl.when((source >= 0) & (source < slots) & jnp.logical_not(is_fresh(source)))
        def _():
            pltpu.make_async_copy(
                store.at[jnp.clip(source, 0, slots - 1), pl.ds(first, pages)],
                box,
                pack_sem.at[i],
            ).start()

        for save, _, part, file_first, file_pages in comes:
            if save is not None and file_first <= first < file_first + file_pages:

                @pl.when((source >= 0) & (source == save))
                def _():
                    pltpu.make_async_copy(
                        part.at[pl.ds(first - file_first, pages)], box, fresh_sem.at[i]
                    ).start()

    for i, (save, taker, part, first, pages) in enumerate(comes if filing else []):
        if save is not None:

            @pl.when(save >= 0)
            def _():
                pltpu.make_async_copy(
                    part, store.at[jnp.maximum(save, 0), pl.ds(first, pages)], save_sem.at[i]
                ).start()

        @pl.when(taker >= 0)
        def _():
            if attending:
                pltpu.make_async_copy(rows.at[taker], row.at[i], row_sem.at[i]).start()

            @pl.loop(0, pages, unroll=8)
            def _(p):
                page = plan.page(table, taker, first + p)
                pltpu.make_async_copy(part.at[p], refilled.at[page], file_sem.at[i]).start()

    if attending:
        attend_to(
            [taker for _, taker, _, _, _ in comes],
            [part for _, _, part, _, _ in comes],
            row,
            result,
            row_sem,
            out,
            out_sem,
        )

    for i, (source, box, first, pages) in enumerate(goes):

        @pl.when((source >= 0) & jnp.logical_not(is_fresh(source)))
        def _():
            pltpu.make_async_copy(box, box, pack_sem.at[i]).wait()

        if comes:

            @pl.when(is_fresh(source))
            def _():
                pltpu.make_async_copy(box, box, fresh_sem.at[i]).wait()

    for i, (save, taker, part, first, pages) in enumerate(comes if filing else []):
        if save is not None:

            @pl.when(save >= 0)
            def _():
                pltpu.make_async_copy(part, part, save_sem.at[i]).wait()

        @pl.when(taker >= 0)
        def _():
            pltpu.make_async_copy(part, part, file_sem.at[i]).wait()


def step(plan, packs, files, at, table, arrived, pool, rows, store, refilled, attention, filing=True, attending=False):
    at = [] if at is None else [jnp.stack([at])]
    count = len(arrived)
    lead = len(at) + 1 + count
    heads = rows.shape[2]
    boxes = [
        jax.ShapeDtypeStruct((pages,) + pool.shape[1:], pool.dtype)
        for _, _, pages, which in packs
        for _ in which
    ]
    some = max(len(files), 1)
    out = pl.pallas_call(
        functools.partial(step_kernel, plan, packs, files, bool(at), count, filing, attending),
        out_shape=[
            jax.ShapeDtypeStruct(array.shape, array.dtype) for array in (store, refilled, attention)
        ]
        + boxes,
        in_specs=[SMEM] * (len(at) + 1) + [VMEM] * count + [HBM, ANY, HBM, HBM, ANY],
        out_specs=[HBM] * 2 + [ANY] + [VMEM] * len(boxes),
        scratch_shapes=[
            pltpu.VMEM((some, 3, heads, HD), rows.dtype),
            pltpu.VMEM((some, heads, HD), attention.dtype),
        ]
        + [pltpu.SemaphoreType.DMA((some,))] * 4
        + [pltpu.SemaphoreType.DMA((max(len(boxes), 1),))] * 2,
        input_output_aliases={lead + 2: 0, lead + 3: 1, lead + 4: 2},
        compiler_params=pltpu.CompilerParams(vmem_limit_bytes=MUCH if attending or at else ROOM),
        cost_estimate=pl.CostEstimate(flops=0, bytes_accessed=6_000_000, transcendentals=0),
        name="step",
    )(*at, table, *arrived, pool, rows, store, refilled, attention)
    return out[0], out[1], out[2], list(out[3:])


def own_kernel(plan, table, pool, token, refilled, store, window, in_sem, out_sem):
    moves = [
        (plan.kept(table, k), [plan.kept(table, k), plan.own_taker(table, k)]) for k in range(KEEP)
    ]
    for k, (source, _) in enumerate(moves):

        @pl.when(source >= 0)
        def _():
            @pl.loop(0, NPAGE, unroll=8)
            def _(p):
                pltpu.make_async_copy(
                    pool.at[plan.page(table, source, p)], window.at[k, p], in_sem.at[k]
                ).start()

    for k, (source, targets) in enumerate(moves):

        @pl.when(source >= 0)
        def _():
            pltpu.make_async_copy(window.at[k], window.at[k], in_sem.at[k]).wait()

        for lane, to in enumerate(targets):

            @pl.when((source >= 0) & (to >= 0))
            def _():
                @pl.loop(0, NPAGE, unroll=8)
                def _(p):
                    pltpu.make_async_copy(
                        window.at[k, p], refilled.at[plan.page(table, to, p)], out_sem.at[k, lane]
                    ).start()

    for k, (source, targets) in enumerate(moves):
        for lane, to in enumerate(targets):

            @pl.when((source >= 0) & (to >= 0))
            def _():
                pltpu.make_async_copy(window.at[k], window.at[k], out_sem.at[k, lane]).wait()


def own_windows(plan, table, pool, token):
    return pl.pallas_call(
        functools.partial(own_kernel, plan),
        out_shape=[
            jax.ShapeDtypeStruct(pool.shape, pool.dtype),
            jax.ShapeDtypeStruct((NZ * KEEP, NPAGE) + pool.shape[1:], pool.dtype),
        ],
        in_specs=[SMEM, HBM, ANY],
        out_specs=[HBM] * 2,
        scratch_shapes=[
            pltpu.VMEM((KEEP, NPAGE) + pool.shape[1:], pool.dtype),
            pltpu.SemaphoreType.DMA((KEEP,)),
            pltpu.SemaphoreType.DMA((KEEP, 2)),
        ],
        compiler_params=pltpu.CompilerParams(vmem_limit_bytes=ROOM),
        cost_estimate=pl.CostEstimate(flops=0, bytes_accessed=9_000_000, transcendentals=0),
        name="own_windows",
    )(table, pool, token)


def attend_to(branch, windows, row, result, row_sem, out, out_sem):
    count = len(branch)
    for i in range(count):

        @pl.when(branch[i] >= 0)
        def _():
            pltpu.make_async_copy(row.at[i], row.at[i], row_sem.at[i]).wait()

    @pl.when(functools.reduce(jnp.maximum, branch) >= 0)
    def _():
        kv = windows[0].shape[2]
        tokens = NPAGE * PAGE * kv
        flat = [
            window[:, :, 0, :].reshape(tokens, 2 * HD) if kv == 1 else window.reshape(tokens, 2 * HD)
            for window in windows
        ]
        query = [row[i, 0] for i in range(count)]
        scores = [
            lax.dot_general(
                query[i], flat[i][:, :HD], (((1,), (1,)), ((), ())), preferred_element_type=jnp.float32
            )
            for i in range(count)
        ]
        token = lax.broadcasted_iota(jnp.int32, scores[0].shape, 1)
        head = lax.broadcasted_iota(jnp.int32, scores[0].shape, 0)
        fits = (token & (kv - 1)) == lax.div(head, H // KVH)
        for i in range(count):
            masked = jnp.where(fits, scores[i], -jnp.inf)
            own = jnp.sum(
                query[i].astype(jnp.float32) * row[i, 1].astype(jnp.float32), -1, keepdims=True
            )
            peak = jnp.maximum(jnp.max(masked, -1, keepdims=True), own)
            terms = jnp.exp(masked - peak)
            own_term = jnp.exp(own - peak)
            total = jnp.sum(terms, -1, keepdims=True) + own_term
            weights = (terms / total).astype(jnp.bfloat16)
            own_weight = (own_term / total).astype(jnp.bfloat16).astype(jnp.float32)
            mixed = jnp.dot(weights, flat[i][:, HD:], preferred_element_type=jnp.float32)
            mixed = mixed + own_weight * row[i, 2].astype(jnp.float32)
            result[i] = mixed.astype(result.dtype)

    for i in range(count):

        @pl.when(branch[i] >= 0)
        def _():
            pltpu.make_async_copy(result.at[i], out.at[branch[i]], out_sem.at[i]).start()

    for i in range(count):

        @pl.when(branch[i] >= 0)
        def _():
            pltpu.make_async_copy(result.at[i], result.at[i], out_sem.at[i]).wait()


def attend_kernel(plan, whom, traced, *refs):
    if traced:
        at, refs = refs[0][0], refs[1:]
        whom = [(at, l) for _, l in whom]
    table, rows, refilled = refs[:3]
    out, window, row, result, sem, row_sem, out_sem = refs[-7:]
    own = [plan.own_taker(table, k) for k in range(KEEP)]
    takers = []
    for _ in range(CAP):
        taker = functools.reduce(jnp.maximum, own)
        own = [jnp.where(other == taker, -1, other) for other in own]
        takers.append(taker)
    branch = []
    for r, i in whom:
        if r is None:
            branch.append(plan.kept(table, i) if i < KEEP else takers[i - KEEP])
        else:
            branch.append(plan.taker(table, r, i))
    for i, who in enumerate(branch):

        @pl.when(who >= 0)
        def _():
            pltpu.make_async_copy(rows.at[who], row.at[i], row_sem.at[i]).start()

            @pl.loop(0, NPAGE, unroll=8)
            def _(p):
                pltpu.make_async_copy(
                    refilled.at[plan.page(table, who, p)], window.at[i, p], sem.at[i]
                ).start()

    for i, who in enumerate(branch):

        @pl.when(who >= 0)
        def _():
            pltpu.make_async_copy(window.at[i], window.at[i], sem.at[i]).wait()

    attend_to(
        branch, [window.at[i] for i in range(len(branch))], row, result, row_sem, out, out_sem
    )


def attend(plan, whom, at, table, rows, refilled, before):
    at = [] if at is None else [jnp.stack([at])]
    count = len(whom)
    heads = rows.shape[2]
    lead = len(at)
    return pl.pallas_call(
        functools.partial(attend_kernel, plan, whom, bool(at)),
        out_shape=jax.ShapeDtypeStruct((rows.shape[0], heads, HD), jnp.bfloat16),
        in_specs=[SMEM] * (lead + 1) + [ANY, HBM] + [ANY] * len(before),
        out_specs=ANY,
        scratch_shapes=[
            pltpu.VMEM((count, NPAGE) + refilled.shape[1:], refilled.dtype),
            pltpu.VMEM((count, 3, heads, HD), rows.dtype),
            pltpu.VMEM((count, heads, HD), jnp.bfloat16),
            pltpu.SemaphoreType.DMA((count,)),
            pltpu.SemaphoreType.DMA((count,)),
            pltpu.SemaphoreType.DMA((count,)),
        ],
        input_output_aliases={lead + 3: 0} if before else {},
        compiler_params=pltpu.CompilerParams(vmem_limit_bytes=ROOM),
        cost_estimate=pl.CostEstimate(
            flops=count * 2 * 2 * 16 * 1536 * 128, bytes_accessed=count * 800_000, transcendentals=0
        ),
        name="attend",
    )(*at, table, rows, refilled, *before)


def token_rows(hidden, w_query, w_key, w_value, query_gain, key_gain):
    features = lax.all_gather(hidden, "mp", axis=1, tiled=True)
    branch_count = features.shape[0]
    head_group = H // KVH
    heads = w_query.shape[1] // HD
    kv_local = w_key.shape[1] // HD
    query_full = jnp.dot(features, w_query, preferred_element_type=jnp.float32)
    query_full = query_full.reshape(branch_count, heads, HD)
    query_rows = (normalize(query_full, query_gain) / math.sqrt(HD)).astype(jnp.bfloat16)
    key_full = jnp.dot(features, w_key, preferred_element_type=jnp.float32)
    key_rows = normalize(key_full.reshape(branch_count, kv_local, HD), key_gain).astype(jnp.bfloat16)
    value_rows = jnp.dot(features, w_value, preferred_element_type=jnp.float32)
    value_rows = value_rows.reshape(branch_count, kv_local, HD).astype(jnp.bfloat16)
    return jnp.stack(
        [
            query_rows,
            jnp.repeat(key_rows, head_group, axis=1),
            jnp.repeat(value_rows, head_group, axis=1),
        ],
        axis=1,
    )


def shards(
    hidden, w_query, w_key, w_value, query_gain, key_gain, kv_pool, page_table, parent, surviving
):
    groups = lax.axis_size("dp")
    me = lax.axis_index("dp")
    ny = groups // NZ
    branch_count = hidden.shape[0]
    links = 2 + ny - 1
    facts = jnp.concatenate(
        [page_table.T, parent[None], surviving[None], jnp.zeros((6, parent.shape[0]), jnp.int32)]
    )
    packed = first_windows(groups, branch_count, facts, kv_pool)
    parent, surviving, page_table, packed = lax.optimization_barrier(
        (parent, surviving, page_table, packed)
    )
    sides = lax.axis_size("mp")

    def everywhere(move):
        return [
            (g * sides + m, to[0] * sides + to[1])
            for g in range(groups)
            for m in range(sides)
            for to in [move(g, m)]
        ]

    def outer(g, m):
        return g + ny if g // ny % 2 == 0 else g - ny, m

    def inner(g, m):
        if g // ny in (0, NZ - 1):
            return g, m ^ 1
        return g + ny if g // ny % 2 else g - ny, m

    def sideways(shift):
        return lambda g, m: (g // ny * ny + (g % ny + shift) % ny, m)

    pairs = [everywhere(outer), everywhere(inner)]
    pairs += [everywhere(sideways(shift)) for shift in range(1, ny)]
    along, beside, every = [0, 1], list(range(2, links)), list(range(links))

    def travel(packed, which):
        return [lax.ppermute(window, ("dp", "mp"), pairs[l]) for window, l in zip(packed, which)]

    arrived = travel(packed, every)
    plan = Plan(links, groups, branch_count)
    table = routing(parent, surviving, page_table, groups, branch_count, links)
    rounds = table[plan.rounds_at]
    refilled, store = own_windows(plan, table, kv_pool, packed[0])
    rows = token_rows(hidden, w_query, w_key, w_value, query_gain, key_gain)
    waiting = [[(None, i) for i in range(3)], [(None, i) for i in range(3, KEEP + CAP)]]
    waiting += [[(r, l) for l in every] for r in range(FIRST)]

    def attend_next(attention):
        return attend(plan, waiting.pop(0), None, table, rows, refilled, attention)

    attention = attend_next([])
    files = [(r, l, 0, NPAGE, l, r * NPAGE) for r in range(FIRST) for l in every]
    store, refilled, attention, packed = step(
        plan,
        [(FIRST, 0, NPAGE, every)],
        [file for file in files if file[1] in along],
        None,
        table,
        arrived[:2],
        kv_pool,
        rows,
        store,
        refilled,
        attention,
        filing=False,
    )
    moved = travel(packed, every)
    for r in range(FIRST, PREFIX):
        if r > FIRST:
            files = [(r - 1, l, 0, NPAGE, l, 0) for l in along]
            files += [(r - 2, l, 0, NPAGE, l, 0) for l in beside if r - 2 >= FIRST]
            arrived = came_along + came_beside
        packs = [(r, 0, NPAGE, beside)] if r > FIRST else []
        packs += [(r + 1, 0, NPAGE, along)] if r + 1 < PREFIX else []
        rest = r + 1 == PREFIX
        store, refilled, attention, packed = step(
            plan, packs, files, None, table, arrived, kv_pool, rows, store, refilled, attention, filing=not rest
        )
        if rest:
            store, refilled, attention, _ = step(
                plan, [], files, None, table, arrived, kv_pool, rows, store, refilled, attention
            )
        if r > FIRST:
            came_along, came_beside = moving_along, moving_beside
            moving_beside = travel(packed[: len(beside)], beside)
            packed = packed[len(beside) :]
            waiting.append([(at, l) for at, l, _, _, _, _ in files])
        else:
            came_along, came_beside, moving_beside = moved[:2], [], moved[2:]
        if packed:
            if came_beside:
                packed, came_beside = lax.optimization_barrier((packed, came_beside))
            moving_along = travel(packed, along)
        for _ in range(2 if len(waiting) > 1 else 1):
            attention = attend_next([attention])
    while waiting:
        attention = attend_next([attention])
    last = PREFIX - 1
    endings = [(last - 1, beside, came_beside), (last, along, came_along), (last, beside, moving_beside)]
    for r, which, arrived in endings:
        files = [(r, l, 0, NPAGE, i, 0) for i, l in enumerate(which)]
        store, refilled, attention, _ = step(
            plan, [], files, None, table, arrived, kv_pool, rows, store, refilled, attention, attending=True
        )

    def more(state):
        return state[0] < rounds

    def one_round(state):
        r, store, refilled, attention = state
        part = NPAGE // PIECES
        moving = []
        for piece in range(PIECES):
            store, refilled, attention, packed = step(
                plan, [(None, piece * part, part, every)], [], r, table, [], kv_pool, rows, store, refilled, attention
            )
            moving.append(travel(packed, every))
        for piece in range(PIECES):
            files = [(None, l, piece * part, part, l, 0) for l in every]
            store, refilled, attention, _ = step(
                plan, [], files, r, table, moving.pop(0), kv_pool, rows, store, refilled, attention
            )
        attention = attend(plan, [(r, l) for l in every], r, table, rows, refilled, [attention])
        return r + 1, store, refilled, attention

    _, store, refilled, attention = lax.while_loop(
        more, one_round, (jnp.int32(PREFIX), store, refilled, attention)
    )
    return (refilled, attention.reshape(branch_count, -1))


def solution(mesh):
    return jax.shard_map(
        shards,
        mesh=mesh,
        in_specs=(
            P("dp", "mp"),
            P(None, "mp"),
            P(None, "mp"),
            P(None, "mp"),
            P(),
            P(),
            P("dp", None, "mp", None),
            P(),
            P(),
            P(),
        ),
        out_specs=(P("dp", None, "mp", None), P("dp", "mp")),
        check_vma=False,
    )
```

```python
import functools
import math

import jax
import jax.numpy as jnp
from jax import lax
from jax.experimental import pallas as pl
from jax.experimental.pallas import tpu as pltpu
from jax.sharding import PartitionSpec as P

H = 64
KVH = 8
HD = 128
PAGE = 16
NPAGE = 48
CAP = 2
KEEP = 4
NZ = 4
ROUNDS = 40
LANES = 128
PREFIX = 8
FIRST = 2
REST = 2
PIECES = 2
LITTLE = 24 * 1024 * 1024
ROOM = 44 * 1024 * 1024
MUCH = 52 * 1024 * 1024
NEVER = 1 << 20


def normalize(values, gain):
    return values * lax.rsqrt(jnp.mean(values * values, -1, keepdims=True) + 1e-06) * gain


def plan_kernel(groups, branch_count, parent_row, alive_row, parent_column, alive_column, out, state):
    ny = groups // NZ
    branches = groups * branch_count
    shifts = list(range(1, ny))
    slots = NZ * KEEP
    me = lax.axis_index("dp")

    def iota(shape, axis):
        return lax.broadcasted_iota(jnp.int32, shape, axis)

    square = (branches, branches)
    down_ids, across_ids = iota(square, 0), iota(square, 1)
    same = lax.div(down_ids, branch_count) == lax.div(across_ids, branch_count)
    alive_r, alive_c = alive_row[...] > 0, alive_column[...] > 0
    before = jnp.where(same & (down_ids < across_ids) & alive_c, 1, 0)
    item_row = jnp.sum(before, axis=0, keepdims=True)
    item_row = item_row + lax.div(iota((1, branches), 1), branch_count) * KEEP
    before = jnp.where(same & (across_ids < down_ids) & alive_r, 1, 0)
    item_column = jnp.sum(before, axis=1, keepdims=True)
    item_column = item_column + lax.div(iota((branches, 1), 0), branch_count) * KEEP
    wanted = jnp.sum(
        jnp.where(parent_column[...] == across_ids, item_row, 0), axis=1, keepdims=True
    )
    wanted = jnp.where(alive_c, -1, wanted)
    wide = (branches, LANES)
    local = lax.rem(iota(wide, 0), branch_count)
    takes = jnp.where(wanted == iota(wide, 1), local, -1)
    child = jnp.max(takes.reshape(groups, branch_count, LANES), axis=1)
    holds = jnp.where((item_column == iota(wide, 1)) & alive_c, local, -1)
    branch = jnp.max(holds, axis=0, keepdims=True)

    shape = (groups, LANES)
    here, item = iota(shape, 0), iota(shape, 1)
    z, y = lax.div(here, ny), lax.rem(here, ny)
    source = lax.div(item, KEEP)
    item_z, item_y = lax.div(source, ny), lax.rem(source, ny)
    on_line = item_y == y
    need = child >= 0

    def across(mask):
        return jnp.max(jnp.where(mask, 1, 0), axis=0, keepdims=True)

    top = jnp.max(jnp.where(need, z, -1), axis=0, keepdims=True)
    bottom = jnp.min(jnp.where(need, z, NZ), axis=0, keepdims=True)
    top_crosses = across(need & (z == top) & (item_y != y))
    bottom_crosses = across(need & (z == bottom) & (item_y != y))
    tie = LANES - 1 - item
    up_hops, down_hops = jnp.maximum(top - z, 0), jnp.maximum(z - bottom, 0)
    up_key = (up_hops * 2 + top_crosses) * LANES + tie
    down_key = (down_hops * 2 + bottom_crosses) * LANES + tie
    go_up, go_down = on_line & (up_hops > 0), on_line & (down_hops > 0)

    def beside(x, shift):
        return jnp.where(
            y + shift < ny, pltpu.roll(x, groups - shift, 0), pltpu.roll(x, (ny - shift) % groups, 0)
        )

    crosses = [on_line & (beside(child, shift) >= 0) for shift in shifts]
    own = source == here
    start = [go_up & own, go_down & own] + [c & own for c in crosses]
    rows = len(start)
    for i, mask in enumerate(start):
        state[i] = jnp.where(mask, 0, NEVER)
        state[rows + i] = jnp.full(shape, -1, jnp.int32)

    def choose(i, r, key):
        ready = state[i]
        key = jnp.where(ready <= r, key(ready), -1)
        best = jnp.max(key, axis=1, keepdims=True)
        chosen = (key == best) & (best >= 0)
        state[i] = jnp.where(chosen, NEVER, ready)
        state[rows + i] = jnp.where(chosen, r, state[rows + i])
        return jnp.where(chosen, 1, 0)

    def one_round(r):
        ups = choose(0, r, lambda ready: up_key)
        downs = choose(1, r, lambda ready: down_key)
        for i in range(2, rows):
            choose(i, r, lambda ready: (ROUNDS - ready) * LANES + tie)
        ups = jnp.where(z > 0, pltpu.roll(ups, ny, 0), 0) > 0
        downs = jnp.where(z < NZ - 1, pltpu.roll(downs, groups - ny, 0), 0) > 0
        rested = jnp.where(r < FIRST, FIRST, r + REST)
        state[0] = jnp.where(ups & go_up, rested, state[0])
        state[1] = jnp.where(downs & go_down, rested, state[1])
        left = jnp.minimum(state[0], state[1])
        for i, cross in enumerate(crosses):
            there = jnp.where((ups | downs) & cross, jnp.maximum(r + 1, FIRST), state[2 + i])
            state[2 + i] = there
            left = jnp.minimum(left, there)
        return r + 1, jnp.min(left)

    rounds, _ = lax.while_loop(
        lambda carry: (carry[1] < NEVER) & (carry[0] < ROUNDS),
        lambda carry: one_round(carry[0]),
        (jnp.int32(0), jnp.int32(0)),
    )

    def row_of(x, group):
        return jnp.max(jnp.where(here == group, x, -1), axis=0, keepdims=True)

    my_z = lax.div(me, ny)
    my_y = me - my_z * ny
    even = lax.rem(my_z, 2) == 0
    item = iota((1, LANES), 1)
    group = lax.div(item, KEEP)
    slot = lax.div(group, ny) * KEEP + lax.rem(item, KEEP)
    value = jnp.where(group == me, slots + branch, slot)
    taker = row_of(child, me)
    up_out, down_out = row_of(state[rows], me), row_of(state[rows + 1], me)
    up_in, down_in = row_of(state[rows], me - ny), row_of(state[rows + 1], me + ny)
    outs = [jnp.where(even, up_out, down_out), jnp.where(even, down_out, up_out)]
    ins = [jnp.where(even, down_in, up_in), jnp.where(even, up_in, down_in)]
    for shift in shifts:
        outs.append(row_of(state[rows + 1 + shift], me))
        from_y = lax.rem(my_y + ny - shift, ny)
        ins.append(row_of(state[rows + 1 + shift], my_z * ny + from_y))
    table = [(times, value) for times in outs]
    table += [(times, slot) for times in ins[:2]]
    table += [(times, taker) for times in ins]
    at = iota((ROUNDS, LANES), 0)
    lane = iota((ROUNDS, LANES), 1)
    result = jnp.full((ROUNDS, LANES), -1, jnp.int32)
    for c, (times, values) in enumerate(table):
        column = jnp.max(jnp.where(times == at, values, -1), axis=1, keepdims=True)
        result = jnp.where(lane == c, column, result)
    out[pl.ds(0, ROUNDS), :] = result
    extra = iota((8, LANES), 0)
    out[pl.ds(ROUNDS, 8), :] = jnp.where(
        extra == 0, rounds, jnp.where(extra == 1, branch, jnp.where(extra == 2, taker, 0))
    )


class Plan:
    def __init__(self, links, groups, branch_count):
        self.links = links
        self.width = 2 * links + 2
        self.rounds_at = ROUNDS * self.width
        self.branch_at = self.rounds_at + 1
        self.taker_at = self.branch_at + groups * KEEP
        self.pages_at = self.taker_at + groups * KEEP

    def send(self, table, r, l):
        return table[r * self.width + l]

    def save(self, table, r, l):
        return table[r * self.width + self.links + l]

    def taker(self, table, r, l):
        return table[r * self.width + self.links + 2 + l]

    def page(self, table, branch, p):
        return table[self.pages_at + branch * NPAGE + p]

    def kept(self, table, k):
        return table[self.branch_at + lax.axis_index("dp") * KEEP + k]

    def own_taker(self, table, k):
        return table[self.taker_at + lax.axis_index("dp") * KEEP + k]


def routing(parent, surviving, page_table, groups, branch_count, links):
    ny = groups // NZ
    rows = 2 + ny - 1
    out = pl.pallas_call(
        functools.partial(plan_kernel, groups, branch_count),
        out_shape=jax.ShapeDtypeStruct((ROUNDS + 8, LANES), jnp.int32),
        in_specs=[VMEM] * 4,
        out_specs=VMEM,
        scratch_shapes=[pltpu.VMEM((2 * rows, groups, LANES), jnp.int32)],
        compiler_params=pltpu.CompilerParams(vmem_limit_bytes=LITTLE),
        cost_estimate=pl.CostEstimate(flops=0, bytes_accessed=6_000_000, transcendentals=0),
        name="plan",
    )(
        parent.reshape(1, -1),
        surviving.reshape(1, -1),
        parent.reshape(-1, 1),
        surviving.reshape(-1, 1),
    )
    pages = lax.dynamic_slice_in_dim(
        page_table, lax.axis_index("dp") * branch_count, branch_count, 0
    )
    items = groups * KEEP
    return jnp.concatenate(
        [
            out[:ROUNDS, : 2 * links + 2].reshape(-1),
            out[ROUNDS, :1],
            out[ROUNDS + 1, :items],
            out[ROUNDS + 2, :items],
            pages.reshape(-1),
        ]
    )


SMEM = pl.BlockSpec(memory_space=pltpu.SMEM)
VMEM = pl.BlockSpec(memory_space=pltpu.VMEM)
HBM = pl.BlockSpec(memory_space=pltpu.HBM)
ANY = pl.BlockSpec(memory_space=pl.ANY)


def first_kernel(groups, branch_count, facts, pool, *refs):
    ny = groups // NZ
    packed, (table, outbox, load_sem, sem, out_sem) = refs[:-5], refs[-5:]
    load = pltpu.make_async_copy(facts, table, load_sem)
    load.start()
    me = lax.axis_index("dp")
    z, y = me // ny, me % ny
    shape = (branch_count, groups * branch_count)
    child = lax.broadcasted_iota(jnp.int32, shape, 1)
    local = lax.broadcasted_iota(jnp.int32, shape, 0)
    column = lax.broadcasted_iota(jnp.int32, (branch_count, 1), 0)
    parent, surviving = facts[pl.ds(NPAGE, 1), :], facts[pl.ds(NPAGE + 1, 1), :]
    mine = (surviving == 0) & (parent == me * branch_count + local)
    target = lax.div(child, branch_count)
    target_z = lax.div(target, ny)
    target_y = target - target_z * ny

    def seen(mask):
        return jnp.max(mask.astype(jnp.int32), axis=1, keepdims=True)

    def leading(key):
        rows = []
        for _ in range(FIRST):
            best = jnp.max(key)
            rows.append(
                jnp.where(best >= 0, branch_count - 1 - lax.rem(best, branch_count), -1)
            )
            key = jnp.where(key == best, -1, key)
        return rows

    ways = []
    for steps in (target_z - z, z - target_z):
        hops = jnp.max(jnp.where(mine, steps, 0), axis=1, keepdims=True)
        far_across = seen(mine & (steps == hops) & (target_y != y))
        key = (hops * 2 + far_across) * branch_count + branch_count - 1 - column
        ways.append(leading(jnp.where(hops > 0, key, -1)))
    even = lax.rem(z, 2) == 0
    sends = [
        [jnp.where(even, u, d) for u, d in zip(*ways)],
        [jnp.where(even, d, u) for u, d in zip(*ways)],
    ]
    for shift in range(1, ny):
        to = lax.rem(y + shift, ny)
        crossing = seen(mine & (target_z == z) & (target_y == to))
        sends.append(leading(jnp.where(crossing > 0, branch_count - 1 - column, -1)))
    load.wait()
    for l, rows in enumerate(sends):
        for r, row in enumerate(rows):

            @pl.when(row >= 0)
            def _():
                for p in range(NPAGE):
                    page = table[p, me * branch_count + row]
                    pltpu.make_async_copy(
                        pool.at[page], outbox.at[l, r * NPAGE + p], sem.at[l, r]
                    ).start()

    for start in (True, False):
        for l, rows in enumerate(sends):
            for r, row in enumerate(rows):
                part = pl.ds(r * NPAGE, NPAGE)
                box = outbox.at[l, part]
                copy = pltpu.make_async_copy(box, packed[l].at[part], out_sem.at[l, r])

                @pl.when(row >= 0)
                def _():
                    if start:
                        pltpu.make_async_copy(box, box, sem.at[l, r]).wait()
                        copy.start()
                    else:
                        copy.wait()


def first_windows(groups, branch_count, facts, pool):
    links = 2 + groups // NZ - 1
    windows = jax.ShapeDtypeStruct((FIRST * NPAGE,) + pool.shape[1:], pool.dtype)
    return pl.pallas_call(
        functools.partial(first_kernel, groups, branch_count),
        out_shape=[windows] * links,
        in_specs=[VMEM, HBM],
        out_specs=[HBM] * links,
        scratch_shapes=[
            pltpu.SMEM(facts.shape, facts.dtype),
            pltpu.VMEM((links,) + windows.shape, windows.dtype),
            pltpu.SemaphoreType.DMA,
            pltpu.SemaphoreType.DMA((links, FIRST)),
            pltpu.SemaphoreType.DMA((links, FIRST)),
        ],
        compiler_params=pltpu.CompilerParams(vmem_limit_bytes=LITTLE),
        cost_estimate=pl.CostEstimate(flops=0, bytes_accessed=6_000_000, transcendentals=0),
        name="first_windows",
    )(facts, pool)


def step_kernel(plan, packs, files, traced, count, filing, attending, *refs):
    if traced:
        at, refs = refs[0][0], refs[1:]
        packs = [(at,) + entry[1:] for entry in packs]
        files = [(at,) + entry[1:] for entry in files]
    links = plan.links
    table = refs[0]
    arrived = refs[1 : 1 + count]
    pool, rows = refs[1 + count : 3 + count]
    store, refilled, out = refs[6 + count : 9 + count]
    packed = refs[9 + count : -8]
    row, result, row_sem, out_sem, file_sem, save_sem, pack_sem, fresh_sem = refs[-8:]
    slots = NZ * KEEP

    comes = []
    for r, l, first, pages, array, offset in files:
        part = arrived[array].at[pl.ds(offset, pages)]
        save = plan.save(table, r, l) if l < 2 else None
        comes.append((save, plan.taker(table, r, l), part, first, pages))

    def is_fresh(source):
        fresh = [source == save for save, _, _, _, _ in comes if save is not None]
        return (source >= 0) & functools.reduce(jnp.logical_or, fresh) if fresh else False

    goes = []
    for r, first, pages, which in packs:
        for l in which:
            goes.append((plan.send(table, r, l), packed[len(goes)], first, pages))

    for i, (source, box, first, pages) in enumerate(goes):

        @pl.when(source >= slots)
        def _():
            @pl.loop(0, pages, unroll=8)
            def _(p):
                page = plan.page(table, source - slots, first + p)
                pltpu.make_async_copy(pool.at[page], box.at[p], pack_sem.at[i]).start()

        @pl.when((source >= 0) & (source < slots) & jnp.logical_not(is_fresh(source)))
        def _():
            pltpu.make_async_copy(
                store.at[jnp.clip(source, 0, slots - 1), pl.ds(first, pages)],
                box,
                pack_sem.at[i],
            ).start()

        for save, _, part, file_first, file_pages in comes:
            if save is not None and file_first <= first < file_first + file_pages:

                @pl.when((source >= 0) & (source == save))
                def _():
                    pltpu.make_async_copy(
                        part.at[pl.ds(first - file_first, pages)], box, fresh_sem.at[i]
                    ).start()

    for i, (save, taker, part, first, pages) in enumerate(comes if filing else []):
        if save is not None:

            @pl.when(save >= 0)
            def _():
                pltpu.make_async_copy(
                    part, store.at[jnp.maximum(save, 0), pl.ds(first, pages)], save_sem.at[i]
                ).start()

        @pl.when(taker >= 0)
        def _():
            if attending:
                pltpu.make_async_copy(rows.at[taker], row.at[i], row_sem.at[i]).start()

            @pl.loop(0, pages, unroll=8)
            def _(p):
                page = plan.page(table, taker, first + p)
                pltpu.make_async_copy(part.at[p], refilled.at[page], file_sem.at[i]).start()

    if attending:
        attend_to(
            [taker for _, taker, _, _, _ in comes],
            [part for _, _, part, _, _ in comes],
            row,
            result,
            row_sem,
            out,
            out_sem,
        )

    for i, (source, box, first, pages) in enumerate(goes):

        @pl.when((source >= 0) & jnp.logical_not(is_fresh(source)))
        def _():
            pltpu.make_async_copy(box, box, pack_sem.at[i]).wait()

        if comes:

            @pl.when(is_fresh(source))
            def _():
                pltpu.make_async_copy(box, box, fresh_sem.at[i]).wait()

    for i, (save, taker, part, first, pages) in enumerate(comes if filing else []):
        if save is not None:

            @pl.when(save >= 0)
            def _():
                pltpu.make_async_copy(part, part, save_sem.at[i]).wait()

        @pl.when(taker >= 0)
        def _():
            pltpu.make_async_copy(part, part, file_sem.at[i]).wait()


def step(plan, packs, files, at, table, arrived, pool, rows, store, refilled, attention, filing=True, attending=False):
    at = [] if at is None else [jnp.stack([at])]
    count = len(arrived)
    lead = len(at) + 1 + count
    heads = rows.shape[2]
    boxes = [
        jax.ShapeDtypeStruct((pages,) + pool.shape[1:], pool.dtype)
        for _, _, pages, which in packs
        for _ in which
    ]
    some = max(len(files), 1)
    out = pl.pallas_call(
        functools.partial(step_kernel, plan, packs, files, bool(at), count, filing, attending),
        out_shape=[
            jax.ShapeDtypeStruct(array.shape, array.dtype) for array in (store, refilled, attention)
        ]
        + boxes,
        in_specs=[SMEM] * (len(at) + 1) + [VMEM if filing else ANY] * count + [HBM, ANY, HBM, HBM, ANY],
        out_specs=[HBM] * 2 + [ANY] + [VMEM] * len(boxes),
        scratch_shapes=[
            pltpu.VMEM((some, 3, heads, HD), rows.dtype),
            pltpu.VMEM((some, heads, HD), attention.dtype),
        ]
        + [pltpu.SemaphoreType.DMA((some,))] * 4
        + [pltpu.SemaphoreType.DMA((max(len(boxes), 1),))] * 2,
        input_output_aliases={lead + 2: 0, lead + 3: 1, lead + 4: 2},
        compiler_params=pltpu.CompilerParams(vmem_limit_bytes=MUCH if attending or at else ROOM),
        cost_estimate=pl.CostEstimate(flops=0, bytes_accessed=6_000_000, transcendentals=0),
        name="step",
    )(*at, table, *arrived, pool, rows, store, refilled, attention)
    return out[0], out[1], out[2], list(out[3:])


def own_kernel(plan, table, pool, token, refilled, store, window, in_sem, out_sem):
    moves = [
        (plan.kept(table, k), [plan.kept(table, k), plan.own_taker(table, k)]) for k in range(KEEP)
    ]
    for k, (source, _) in enumerate(moves):

        @pl.when(source >= 0)
        def _():
            @pl.loop(0, NPAGE, unroll=8)
            def _(p):
                pltpu.make_async_copy(
                    pool.at[plan.page(table, source, p)], window.at[k, p], in_sem.at[k]
                ).start()

    for k, (source, targets) in enumerate(moves):

        @pl.when(source >= 0)
        def _():
            pltpu.make_async_copy(window.at[k], window.at[k], in_sem.at[k]).wait()

        for lane, to in enumerate(targets):

            @pl.when((source >= 0) & (to >= 0))
            def _():
                @pl.loop(0, NPAGE, unroll=8)
                def _(p):
                    pltpu.make_async_copy(
                        window.at[k, p], refilled.at[plan.page(table, to, p)], out_sem.at[k, lane]
                    ).start()

    for k, (source, targets) in enumerate(moves):
        for lane, to in enumerate(targets):

            @pl.when((source >= 0) & (to >= 0))
            def _():
                pltpu.make_async_copy(window.at[k], window.at[k], out_sem.at[k, lane]).wait()


def own_windows(plan, table, pool, token):
    return pl.pallas_call(
        functools.partial(own_kernel, plan),
        out_shape=[
            jax.ShapeDtypeStruct(pool.shape, pool.dtype),
            jax.ShapeDtypeStruct((NZ * KEEP, NPAGE) + pool.shape[1:], pool.dtype),
        ],
        in_specs=[SMEM, HBM, ANY],
        out_specs=[HBM] * 2,
        scratch_shapes=[
            pltpu.VMEM((KEEP, NPAGE) + pool.shape[1:], pool.dtype),
            pltpu.SemaphoreType.DMA((KEEP,)),
            pltpu.SemaphoreType.DMA((KEEP, 2)),
        ],
        compiler_params=pltpu.CompilerParams(vmem_limit_bytes=ROOM),
        cost_estimate=pl.CostEstimate(flops=0, bytes_accessed=9_000_000, transcendentals=0),
        name="own_windows",
    )(table, pool, token)


def attend_to(branch, windows, row, result, row_sem, out, out_sem):
    count = len(branch)
    for i in range(count):

        @pl.when(branch[i] >= 0)
        def _():
            pltpu.make_async_copy(row.at[i], row.at[i], row_sem.at[i]).wait()

    @pl.when(functools.reduce(jnp.maximum, branch) >= 0)
    def _():
        kv = windows[0].shape[2]
        tokens = NPAGE * PAGE * kv
        flat = [
            window[:, :, 0, :].reshape(tokens, 2 * HD) if kv == 1 else window.reshape(tokens, 2 * HD)
            for window in windows
        ]
        query = [row[i, 0] for i in range(count)]
        scores = [
            lax.dot_general(
                query[i], flat[i][:, :HD], (((1,), (1,)), ((), ())), preferred_element_type=jnp.float32
            )
            for i in range(count)
        ]
        token = lax.broadcasted_iota(jnp.int32, scores[0].shape, 1)
        head = lax.broadcasted_iota(jnp.int32, scores[0].shape, 0)
        fits = (token & (kv - 1)) == lax.div(head, H // KVH)
        for i in range(count):
            masked = jnp.where(fits, scores[i], -jnp.inf)
            own = jnp.sum(
                query[i].astype(jnp.float32) * row[i, 1].astype(jnp.float32), -1, keepdims=True
            )
            peak = jnp.maximum(jnp.max(masked, -1, keepdims=True), own)
            terms = jnp.exp(masked - peak)
            own_term = jnp.exp(own - peak)
            total = jnp.sum(terms, -1, keepdims=True) + own_term
            weights = (terms / total).astype(jnp.bfloat16)
            own_weight = (own_term / total).astype(jnp.bfloat16).astype(jnp.float32)
            mixed = jnp.dot(weights, flat[i][:, HD:], preferred_element_type=jnp.float32)
            mixed = mixed + own_weight * row[i, 2].astype(jnp.float32)
            result[i] = mixed.astype(result.dtype)

    for i in range(count):

        @pl.when(branch[i] >= 0)
        def _():
            pltpu.make_async_copy(result.at[i], out.at[branch[i]], out_sem.at[i]).start()

    for i in range(count):

        @pl.when(branch[i] >= 0)
        def _():
            pltpu.make_async_copy(result.at[i], result.at[i], out_sem.at[i]).wait()


def attend_kernel(plan, whom, traced, *refs):
    if traced:
        at, refs = refs[0][0], refs[1:]
        whom = [(at, l) for _, l in whom]
    table, rows, refilled = refs[:3]
    out, window, row, result, sem, row_sem, out_sem = refs[-7:]
    own = [plan.own_taker(table, k) for k in range(KEEP)]
    takers = []
    for _ in range(CAP):
        taker = functools.reduce(jnp.maximum, own)
        own = [jnp.where(other == taker, -1, other) for other in own]
        takers.append(taker)
    branch = []
    for r, i in whom:
        if r is None:
            branch.append(plan.kept(table, i) if i < KEEP else takers[i - KEEP])
        else:
            branch.append(plan.taker(table, r, i))
    for i, who in enumerate(branch):

        @pl.when(who >= 0)
        def _():
            pltpu.make_async_copy(rows.at[who], row.at[i], row_sem.at[i]).start()

            @pl.loop(0, NPAGE, unroll=8)
            def _(p):
                pltpu.make_async_copy(
                    refilled.at[plan.page(table, who, p)], window.at[i, p], sem.at[i]
                ).start()

    for i, who in enumerate(branch):

        @pl.when(who >= 0)
        def _():
            pltpu.make_async_copy(window.at[i], window.at[i], sem.at[i]).wait()

    attend_to(
        branch, [window.at[i] for i in range(len(branch))], row, result, row_sem, out, out_sem
    )


def attend(plan, whom, at, table, rows, refilled, before):
    at = [] if at is None else [jnp.stack([at])]
    count = len(whom)
    heads = rows.shape[2]
    lead = len(at)
    return pl.pallas_call(
        functools.partial(attend_kernel, plan, whom, bool(at)),
        out_shape=jax.ShapeDtypeStruct((rows.shape[0], heads, HD), jnp.bfloat16),
        in_specs=[SMEM] * (lead + 1) + [ANY, HBM] + [ANY] * len(before),
        out_specs=ANY,
        scratch_shapes=[
            pltpu.VMEM((count, NPAGE) + refilled.shape[1:], refilled.dtype),
            pltpu.VMEM((count, 3, heads, HD), rows.dtype),
            pltpu.VMEM((count, heads, HD), jnp.bfloat16),
            pltpu.SemaphoreType.DMA((count,)),
            pltpu.SemaphoreType.DMA((count,)),
            pltpu.SemaphoreType.DMA((count,)),
        ],
        input_output_aliases={lead + 3: 0} if before else {},
        compiler_params=pltpu.CompilerParams(vmem_limit_bytes=ROOM),
        cost_estimate=pl.CostEstimate(
            flops=count * 2 * 2 * 16 * 1536 * 128, bytes_accessed=count * 800_000, transcendentals=0
        ),
        name="attend",
    )(*at, table, rows, refilled, *before)


def token_rows(hidden, w_query, w_key, w_value, query_gain, key_gain):
    features = lax.all_gather(hidden, "mp", axis=1, tiled=True)
    branch_count = features.shape[0]
    head_group = H // KVH
    heads = w_query.shape[1] // HD
    kv_local = w_key.shape[1] // HD
    query_full = jnp.dot(features, w_query, preferred_element_type=jnp.float32)
    query_full = query_full.reshape(branch_count, heads, HD)
    query_rows = (normalize(query_full, query_gain) / math.sqrt(HD)).astype(jnp.bfloat16)
    key_full = jnp.dot(features, w_key, preferred_element_type=jnp.float32)
    key_rows = normalize(key_full.reshape(branch_count, kv_local, HD), key_gain).astype(jnp.bfloat16)
    value_rows = jnp.dot(features, w_value, preferred_element_type=jnp.float32)
    value_rows = value_rows.reshape(branch_count, kv_local, HD).astype(jnp.bfloat16)
    return jnp.stack(
        [
            query_rows,
            jnp.repeat(key_rows, head_group, axis=1),
            jnp.repeat(value_rows, head_group, axis=1),
        ],
        axis=1,
    )


def shards(
    hidden, w_query, w_key, w_value, query_gain, key_gain, kv_pool, page_table, parent, surviving
):
    groups = lax.axis_size("dp")
    me = lax.axis_index("dp")
    ny = groups // NZ
    branch_count = hidden.shape[0]
    links = 2 + ny - 1
    facts = jnp.concatenate(
        [page_table.T, parent[None], surviving[None], jnp.zeros((6, parent.shape[0]), jnp.int32)]
    )
    packed = first_windows(groups, branch_count, facts, kv_pool)
    parent, surviving, page_table, packed = lax.optimization_barrier(
        (parent, surviving, page_table, packed)
    )
    sides = lax.axis_size("mp")

    def everywhere(move):
        return [
            (g * sides + m, to[0] * sides + to[1])
            for g in range(groups)
            for m in range(sides)
            for to in [move(g, m)]
        ]

    def outer(g, m):
        return g + ny if g // ny % 2 == 0 else g - ny, m

    def inner(g, m):
        if g // ny in (0, NZ - 1):
            return g, m ^ 1
        return g + ny if g // ny % 2 else g - ny, m

    def sideways(shift):
        return lambda g, m: (g // ny * ny + (g % ny + shift) % ny, m)

    pairs = [everywhere(outer), everywhere(inner)]
    pairs += [everywhere(sideways(shift)) for shift in range(1, ny)]
    along, beside, every = [0, 1], list(range(2, links)), list(range(links))

    def travel(packed, which):
        return [lax.ppermute(window, ("dp", "mp"), pairs[l]) for window, l in zip(packed, which)]

    arrived = travel(packed, every)
    plan = Plan(links, groups, branch_count)
    table = routing(parent, surviving, page_table, groups, branch_count, links)
    rounds = table[plan.rounds_at]
    refilled, store = own_windows(plan, table, kv_pool, packed[0])
    rows = token_rows(hidden, w_query, w_key, w_value, query_gain, key_gain)
    waiting = [[(None, i) for i in range(3)], [(None, i) for i in range(3, KEEP + CAP)]]
    waiting += [[(r, l) for l in every] for r in range(FIRST)]

    def attend_next(attention):
        return attend(plan, waiting.pop(0), None, table, rows, refilled, attention)

    attention = attend_next([])
    files = [(r, l, 0, NPAGE, l, r * NPAGE) for r in range(FIRST) for l in every]
    store, refilled, attention, packed = step(
        plan,
        [(FIRST, 0, NPAGE, every)],
        [file for file in files if file[1] in along],
        None,
        table,
        arrived[:2],
        kv_pool,
        rows,
        store,
        refilled,
        attention,
        filing=False,
    )
    moved = travel(packed, every)
    for r in range(FIRST, PREFIX):
        if r > FIRST:
            files = [(r - 1, l, 0, NPAGE, l, 0) for l in along]
            files += [(r - 2, l, 0, NPAGE, l, 0) for l in beside if r - 2 >= FIRST]
            arrived = came_along + came_beside
        packs = [(r, 0, NPAGE, beside)] if r > FIRST else []
        more_packs = [(r + 1, 0, NPAGE, along)] if r + 1 < PREFIX else []
        ahead = r == PREFIX - 1
        store, refilled, attention, packed = step(
            plan,
            packs if ahead else packs + more_packs,
            files,
            None,
            table,
            arrived,
            kv_pool,
            rows,
            store,
            refilled,
            attention,
            filing=not ahead,
        )
        if ahead:
            store, refilled, attention, more_packed = step(
                plan, more_packs, files, None, table, arrived, kv_pool, rows, store, refilled, attention
            )
            packed = packed + more_packed
        if r > FIRST:
            came_along, came_beside = moving_along, moving_beside
            moving_beside = travel(packed[: len(beside)], beside)
            packed = packed[len(beside) :]
            waiting.append([(at, l) for at, l, _, _, _, _ in files])
        else:
            came_along, came_beside, moving_beside = moved[:2], [], moved[2:]
        if packed:
            if came_beside:
                packed, came_beside = lax.optimization_barrier((packed, came_beside))
            moving_along = travel(packed, along)
        for _ in range(2 if len(waiting) > 1 else 1):
            attention = attend_next([attention])
    while waiting:
        attention = attend_next([attention])
    last = PREFIX - 1
    endings = [(last - 1, beside, came_beside), (last, along, came_along), (last, beside, moving_beside)]
    for r, which, arrived in endings:
        files = [(r, l, 0, NPAGE, i, 0) for i, l in enumerate(which)]
        store, refilled, attention, _ = step(
            plan, [], files, None, table, arrived, kv_pool, rows, store, refilled, attention, attending=True
        )

    def more(state):
        return state[0] < rounds

    def one_round(state):
        r, store, refilled, attention = state
        part = NPAGE // PIECES
        moving = []
        for piece in range(PIECES):
            store, refilled, attention, packed = step(
                plan, [(None, piece * part, part, every)], [], r, table, [], kv_pool, rows, store, refilled, attention
            )
            moving.append(travel(packed, every))
        for piece in range(PIECES):
            files = [(None, l, piece * part, part, l, 0) for l in every]
            store, refilled, attention, _ = step(
                plan, [], files, r, table, moving.pop(0), kv_pool, rows, store, refilled, attention
            )
        attention = attend(plan, [(r, l) for l in every], r, table, rows, refilled, [attention])
        return r + 1, store, refilled, attention

    _, store, refilled, attention = lax.while_loop(
        more, one_round, (jnp.int32(PREFIX), store, refilled, attention)
    )
    return (refilled, attention.reshape(branch_count, -1))


def solution(mesh):
    return jax.shard_map(
        shards,
        mesh=mesh,
        in_specs=(
            P("dp", "mp"),
            P(None, "mp"),
            P(None, "mp"),
            P(None, "mp"),
            P(),
            P(),
            P("dp", None, "mp", None),
            P(),
            P(),
            P(),
        ),
        out_specs=(P("dp", None, "mp", None), P("dp", "mp")),
        check_vma=False,
    )
```

```python
import functools
import math

import jax
import jax.numpy as jnp
from jax import lax
from jax.experimental import pallas as pl
from jax.experimental.pallas import tpu as pltpu
from jax.sharding import PartitionSpec as P

H = 64
KVH = 8
HD = 128
PAGE = 16
NPAGE = 48
CAP = 2
KEEP = 4
NZ = 4
ROUNDS = 40
LANES = 128
PREFIX = 8
FIRST = 2
REST = 2
PIECES = 2
LITTLE = 24 * 1024 * 1024
ROOM = 44 * 1024 * 1024
MUCH = 52 * 1024 * 1024
NEVER = 1 << 20


def normalize(values, gain):
    return values * lax.rsqrt(jnp.mean(values * values, -1, keepdims=True) + 1e-06) * gain


def plan_kernel(groups, branch_count, parent_row, alive_row, parent_column, alive_column, out, state):
    ny = groups // NZ
    branches = groups * branch_count
    shifts = list(range(1, ny))
    slots = NZ * KEEP
    me = lax.axis_index("dp")

    def iota(shape, axis):
        return lax.broadcasted_iota(jnp.int32, shape, axis)

    square = (branches, branches)
    down_ids, across_ids = iota(square, 0), iota(square, 1)
    same = lax.div(down_ids, branch_count) == lax.div(across_ids, branch_count)
    alive_r, alive_c = alive_row[...] > 0, alive_column[...] > 0
    before = jnp.where(same & (down_ids < across_ids) & alive_c, 1, 0)
    item_row = jnp.sum(before, axis=0, keepdims=True)
    item_row = item_row + lax.div(iota((1, branches), 1), branch_count) * KEEP
    before = jnp.where(same & (across_ids < down_ids) & alive_r, 1, 0)
    item_column = jnp.sum(before, axis=1, keepdims=True)
    item_column = item_column + lax.div(iota((branches, 1), 0), branch_count) * KEEP
    wanted = jnp.sum(
        jnp.where(parent_column[...] == across_ids, item_row, 0), axis=1, keepdims=True
    )
    wanted = jnp.where(alive_c, -1, wanted)
    wide = (branches, LANES)
    local = lax.rem(iota(wide, 0), branch_count)
    takes = jnp.where(wanted == iota(wide, 1), local, -1)
    child = jnp.max(takes.reshape(groups, branch_count, LANES), axis=1)
    holds = jnp.where((item_column == iota(wide, 1)) & alive_c, local, -1)
    branch = jnp.max(holds, axis=0, keepdims=True)

    shape = (groups, LANES)
    here, item = iota(shape, 0), iota(shape, 1)
    z, y = lax.div(here, ny), lax.rem(here, ny)
    source = lax.div(item, KEEP)
    item_z, item_y = lax.div(source, ny), lax.rem(source, ny)
    on_line = item_y == y
    need = child >= 0

    def across(mask):
        return jnp.max(jnp.where(mask, 1, 0), axis=0, keepdims=True)

    top = jnp.max(jnp.where(need, z, -1), axis=0, keepdims=True)
    bottom = jnp.min(jnp.where(need, z, NZ), axis=0, keepdims=True)
    top_crosses = across(need & (z == top) & (item_y != y))
    bottom_crosses = across(need & (z == bottom) & (item_y != y))
    tie = LANES - 1 - item
    up_hops, down_hops = jnp.maximum(top - z, 0), jnp.maximum(z - bottom, 0)
    up_key = (up_hops * 2 + top_crosses) * LANES + tie
    down_key = (down_hops * 2 + bottom_crosses) * LANES + tie
    go_up, go_down = on_line & (up_hops > 0), on_line & (down_hops > 0)

    def beside(x, shift):
        return jnp.where(
            y + shift < ny, pltpu.roll(x, groups - shift, 0), pltpu.roll(x, (ny - shift) % groups, 0)
        )

    crosses = [on_line & (beside(child, shift) >= 0) for shift in shifts]
    own = source == here
    start = [go_up & own, go_down & own] + [c & own for c in crosses]
    rows = len(start)
    for i, mask in enumerate(start):
        state[i] = jnp.where(mask, 0, NEVER)
        state[rows + i] = jnp.full(shape, -1, jnp.int32)

    def choose(i, r, key):
        ready = state[i]
        key = jnp.where(ready <= r, key(ready), -1)
        best = jnp.max(key, axis=1, keepdims=True)
        chosen = (key == best) & (best >= 0)
        state[i] = jnp.where(chosen, NEVER, ready)
        state[rows + i] = jnp.where(chosen, r, state[rows + i])
        return jnp.where(chosen, 1, 0)

    def one_round(r):
        ups = choose(0, r, lambda ready: up_key)
        downs = choose(1, r, lambda ready: down_key)
        for i in range(2, rows):
            choose(i, r, lambda ready: (ROUNDS - ready) * LANES + tie)
        ups = jnp.where(z > 0, pltpu.roll(ups, ny, 0), 0) > 0
        downs = jnp.where(z < NZ - 1, pltpu.roll(downs, groups - ny, 0), 0) > 0
        rested = jnp.where(r < FIRST, FIRST, r + REST)
        state[0] = jnp.where(ups & go_up, rested, state[0])
        state[1] = jnp.where(downs & go_down, rested, state[1])
        left = jnp.minimum(state[0], state[1])
        for i, cross in enumerate(crosses):
            there = jnp.where((ups | downs) & cross, jnp.maximum(r + 1, FIRST), state[2 + i])
            state[2 + i] = there
            left = jnp.minimum(left, there)
        return r + 1, jnp.min(left)

    rounds, _ = lax.while_loop(
        lambda carry: (carry[1] < NEVER) & (carry[0] < ROUNDS),
        lambda carry: one_round(carry[0]),
        (jnp.int32(0), jnp.int32(0)),
    )

    def row_of(x, group):
        return jnp.max(jnp.where(here == group, x, -1), axis=0, keepdims=True)

    my_z = lax.div(me, ny)
    my_y = me - my_z * ny
    even = lax.rem(my_z, 2) == 0
    item = iota((1, LANES), 1)
    group = lax.div(item, KEEP)
    slot = lax.div(group, ny) * KEEP + lax.rem(item, KEEP)
    value = jnp.where(group == me, slots + branch, slot)
    taker = row_of(child, me)
    up_out, down_out = row_of(state[rows], me), row_of(state[rows + 1], me)
    up_in, down_in = row_of(state[rows], me - ny), row_of(state[rows + 1], me + ny)
    outs = [jnp.where(even, up_out, down_out), jnp.where(even, down_out, up_out)]
    ins = [jnp.where(even, down_in, up_in), jnp.where(even, up_in, down_in)]
    for shift in shifts:
        outs.append(row_of(state[rows + 1 + shift], me))
        from_y = lax.rem(my_y + ny - shift, ny)
        ins.append(row_of(state[rows + 1 + shift], my_z * ny + from_y))
    table = [(times, value) for times in outs]
    table += [(times, slot) for times in ins[:2]]
    table += [(times, taker) for times in ins]
    at = iota((ROUNDS, LANES), 0)
    lane = iota((ROUNDS, LANES), 1)
    result = jnp.full((ROUNDS, LANES), -1, jnp.int32)
    for c, (times, values) in enumerate(table):
        column = jnp.max(jnp.where(times == at, values, -1), axis=1, keepdims=True)
        result = jnp.where(lane == c, column, result)
    out[pl.ds(0, ROUNDS), :] = result
    extra = iota((8, LANES), 0)
    out[pl.ds(ROUNDS, 8), :] = jnp.where(
        extra == 0, rounds, jnp.where(extra == 1, branch, jnp.where(extra == 2, taker, 0))
    )


class Plan:
    def __init__(self, links, groups, branch_count):
        self.links = links
        self.width = 2 * links + 2
        self.rounds_at = ROUNDS * self.width
        self.branch_at = self.rounds_at + 1
        self.taker_at = self.branch_at + groups * KEEP
        self.pages_at = self.taker_at + groups * KEEP

    def send(self, table, r, l):
        return table[r * self.width + l]

    def save(self, table, r, l):
        return table[r * self.width + self.links + l]

    def taker(self, table, r, l):
        return table[r * self.width + self.links + 2 + l]

    def page(self, table, branch, p):
        return table[self.pages_at + branch * NPAGE + p]

    def kept(self, table, k):
        return table[self.branch_at + lax.axis_index("dp") * KEEP + k]

    def own_taker(self, table, k):
        return table[self.taker_at + lax.axis_index("dp") * KEEP + k]


def routing(parent, surviving, page_table, groups, branch_count, links):
    ny = groups // NZ
    rows = 2 + ny - 1
    out = pl.pallas_call(
        functools.partial(plan_kernel, groups, branch_count),
        out_shape=jax.ShapeDtypeStruct((ROUNDS + 8, LANES), jnp.int32),
        in_specs=[VMEM] * 4,
        out_specs=VMEM,
        scratch_shapes=[pltpu.VMEM((2 * rows, groups, LANES), jnp.int32)],
        compiler_params=pltpu.CompilerParams(vmem_limit_bytes=LITTLE),
        cost_estimate=pl.CostEstimate(flops=0, bytes_accessed=6_000_000, transcendentals=0),
        name="plan",
    )(
        parent.reshape(1, -1),
        surviving.reshape(1, -1),
        parent.reshape(-1, 1),
        surviving.reshape(-1, 1),
    )
    pages = lax.dynamic_slice_in_dim(
        page_table, lax.axis_index("dp") * branch_count, branch_count, 0
    )
    items = groups * KEEP
    return jnp.concatenate(
        [
            out[:ROUNDS, : 2 * links + 2].reshape(-1),
            out[ROUNDS, :1],
            out[ROUNDS + 1, :items],
            out[ROUNDS + 2, :items],
            pages.reshape(-1),
        ]
    )


SMEM = pl.BlockSpec(memory_space=pltpu.SMEM)
VMEM = pl.BlockSpec(memory_space=pltpu.VMEM)
HBM = pl.BlockSpec(memory_space=pltpu.HBM)
ANY = pl.BlockSpec(memory_space=pl.ANY)


def first_kernel(groups, branch_count, facts, pool, *refs):
    ny = groups // NZ
    packed, (table, outbox, load_sem, sem, out_sem) = refs[:-5], refs[-5:]
    load = pltpu.make_async_copy(facts, table, load_sem)
    load.start()
    me = lax.axis_index("dp")
    z, y = me // ny, me % ny
    shape = (branch_count, groups * branch_count)
    child = lax.broadcasted_iota(jnp.int32, shape, 1)
    local = lax.broadcasted_iota(jnp.int32, shape, 0)
    column = lax.broadcasted_iota(jnp.int32, (branch_count, 1), 0)
    parent, surviving = facts[pl.ds(NPAGE, 1), :], facts[pl.ds(NPAGE + 1, 1), :]
    mine = (surviving == 0) & (parent == me * branch_count + local)
    target = lax.div(child, branch_count)
    target_z = lax.div(target, ny)
    target_y = target - target_z * ny

    def seen(mask):
        return jnp.max(mask.astype(jnp.int32), axis=1, keepdims=True)

    def leading(key):
        rows = []
        for _ in range(FIRST):
            best = jnp.max(key)
            rows.append(
                jnp.where(best >= 0, branch_count - 1 - lax.rem(best, branch_count), -1)
            )
            key = jnp.where(key == best, -1, key)
        return rows

    ways = []
    for steps in (target_z - z, z - target_z):
        hops = jnp.max(jnp.where(mine, steps, 0), axis=1, keepdims=True)
        far_across = seen(mine & (steps == hops) & (target_y != y))
        key = (hops * 2 + far_across) * branch_count + branch_count - 1 - column
        ways.append(leading(jnp.where(hops > 0, key, -1)))
    even = lax.rem(z, 2) == 0
    sends = [
        [jnp.where(even, u, d) for u, d in zip(*ways)],
        [jnp.where(even, d, u) for u, d in zip(*ways)],
    ]
    for shift in range(1, ny):
        to = lax.rem(y + shift, ny)
        crossing = seen(mine & (target_z == z) & (target_y == to))
        sends.append(leading(jnp.where(crossing > 0, branch_count - 1 - column, -1)))
    load.wait()
    wanted = [(l, r, row) for l, rows in enumerate(sends) for r, row in enumerate(rows)]
    boxes = []
    for i, (_, _, row) in enumerate(wanted):
        box = jnp.int32(i)
        for j in reversed(range(i)):
            box = jnp.where(wanted[j][2] == row, j, box)
        boxes.append(box)

    for i, (_, _, row) in enumerate(wanted):

        @pl.when((row >= 0) & (boxes[i] == i))
        def _():
            for p in range(NPAGE):
                page = table[p, me * branch_count + row]
                pltpu.make_async_copy(pool.at[page], outbox.at[i, p], sem.at[i]).start()

    for start in (True, False):
        for i, (l, r, row) in enumerate(wanted):
            target = packed[l].at[pl.ds(r * NPAGE, NPAGE)]
            copy = pltpu.make_async_copy(outbox.at[boxes[i]], target, out_sem.at[i])

            if start:

                @pl.when((row >= 0) & (boxes[i] == i))
                def _():
                    pltpu.make_async_copy(outbox.at[i], outbox.at[i], sem.at[i]).wait()

            @pl.when(row >= 0)
            def _():
                if start:
                    copy.start()
                else:
                    copy.wait()


def first_windows(groups, branch_count, facts, pool):
    links = 2 + groups // NZ - 1
    windows = jax.ShapeDtypeStruct((FIRST * NPAGE,) + pool.shape[1:], pool.dtype)
    return pl.pallas_call(
        functools.partial(first_kernel, groups, branch_count),
        out_shape=[windows] * links,
        in_specs=[VMEM, HBM],
        out_specs=[HBM] * links,
        scratch_shapes=[
            pltpu.SMEM(facts.shape, facts.dtype),
            pltpu.VMEM((links * FIRST, NPAGE) + pool.shape[1:], pool.dtype),
            pltpu.SemaphoreType.DMA,
            pltpu.SemaphoreType.DMA((links * FIRST,)),
            pltpu.SemaphoreType.DMA((links * FIRST,)),
        ],
        compiler_params=pltpu.CompilerParams(vmem_limit_bytes=LITTLE),
        cost_estimate=pl.CostEstimate(flops=0, bytes_accessed=6_000_000, transcendentals=0),
        name="first_windows",
    )(facts, pool)


def step_kernel(plan, packs, files, traced, count, filing, attending, *refs):
    if traced:
        at, refs = refs[0][0], refs[1:]
        packs = [(at,) + entry[1:] for entry in packs]
        files = [(at,) + entry[1:] for entry in files]
    links = plan.links
    table = refs[0]
    arrived = refs[1 : 1 + count]
    pool, rows = refs[1 + count : 3 + count]
    store, refilled, out = refs[6 + count : 9 + count]
    packed = refs[9 + count : -8]
    row, result, row_sem, out_sem, file_sem, save_sem, pack_sem, fresh_sem = refs[-8:]
    slots = NZ * KEEP

    comes = []
    for r, l, first, pages, array, offset in files:
        part = arrived[array].at[pl.ds(offset, pages)]
        save = plan.save(table, r, l) if l < 2 else None
        comes.append((save, plan.taker(table, r, l), part, first, pages))

    def is_fresh(source):
        fresh = [source == save for save, _, _, _, _ in comes if save is not None]
        return (source >= 0) & functools.reduce(jnp.logical_or, fresh) if fresh else False

    goes = []
    for r, first, pages, which in packs:
        for l in which:
            goes.append((plan.send(table, r, l), packed[len(goes)], first, pages))

    for i, (source, box, first, pages) in enumerate(goes):

        @pl.when(source >= slots)
        def _():
            @pl.loop(0, pages, unroll=8)
            def _(p):
                page = plan.page(table, source - slots, first + p)
                pltpu.make_async_copy(pool.at[page], box.at[p], pack_sem.at[i]).start()

        @pl.when((source >= 0) & (source < slots) & jnp.logical_not(is_fresh(source)))
        def _():
            pltpu.make_async_copy(
                store.at[jnp.clip(source, 0, slots - 1), pl.ds(first, pages)],
                box,
                pack_sem.at[i],
            ).start()

        for save, _, part, file_first, file_pages in comes:
            if save is not None and file_first <= first < file_first + file_pages:

                @pl.when((source >= 0) & (source == save))
                def _():
                    pltpu.make_async_copy(
                        part.at[pl.ds(first - file_first, pages)], box, fresh_sem.at[i]
                    ).start()

    for i, (save, taker, part, first, pages) in enumerate(comes if filing else []):
        if save is not None:

            @pl.when(save >= 0)
            def _():
                pltpu.make_async_copy(
                    part, store.at[jnp.maximum(save, 0), pl.ds(first, pages)], save_sem.at[i]
                ).start()

        @pl.when(taker >= 0)
        def _():
            if attending:
                pltpu.make_async_copy(rows.at[taker], row.at[i], row_sem.at[i]).start()

            @pl.loop(0, pages, unroll=8)
            def _(p):
                page = plan.page(table, taker, first + p)
                pltpu.make_async_copy(part.at[p], refilled.at[page], file_sem.at[i]).start()

    if attending:
        attend_to(
            [taker for _, taker, _, _, _ in comes],
            [part for _, _, part, _, _ in comes],
            row,
            result,
            row_sem,
            out,
            out_sem,
        )

    for i, (source, box, first, pages) in enumerate(goes):

        @pl.when((source >= 0) & jnp.logical_not(is_fresh(source)))
        def _():
            pltpu.make_async_copy(box, box, pack_sem.at[i]).wait()

        if comes:

            @pl.when(is_fresh(source))
            def _():
                pltpu.make_async_copy(box, box, fresh_sem.at[i]).wait()

    for i, (save, taker, part, first, pages) in enumerate(comes if filing else []):
        if save is not None:

            @pl.when(save >= 0)
            def _():
                pltpu.make_async_copy(part, part, save_sem.at[i]).wait()

        @pl.when(taker >= 0)
        def _():
            pltpu.make_async_copy(part, part, file_sem.at[i]).wait()


def step(plan, packs, files, at, table, arrived, pool, rows, store, refilled, attention, filing=True, attending=False):
    at = [] if at is None else [jnp.stack([at])]
    count = len(arrived)
    lead = len(at) + 1 + count
    heads = rows.shape[2]
    boxes = [
        jax.ShapeDtypeStruct((pages,) + pool.shape[1:], pool.dtype)
        for _, _, pages, which in packs
        for _ in which
    ]
    some = max(len(files), 1)
    out = pl.pallas_call(
        functools.partial(step_kernel, plan, packs, files, bool(at), count, filing, attending),
        out_shape=[
            jax.ShapeDtypeStruct(array.shape, array.dtype) for array in (store, refilled, attention)
        ]
        + boxes,
        in_specs=[SMEM] * (len(at) + 1) + [VMEM if filing else ANY] * count + [HBM, ANY, HBM, HBM, ANY],
        out_specs=[HBM] * 2 + [ANY] + [VMEM] * len(boxes),
        scratch_shapes=[
            pltpu.VMEM((some, 3, heads, HD), rows.dtype),
            pltpu.VMEM((some, heads, HD), attention.dtype),
        ]
        + [pltpu.SemaphoreType.DMA((some,))] * 4
        + [pltpu.SemaphoreType.DMA((max(len(boxes), 1),))] * 2,
        input_output_aliases={lead + 2: 0, lead + 3: 1, lead + 4: 2},
        compiler_params=pltpu.CompilerParams(vmem_limit_bytes=MUCH if attending or at else ROOM),
        cost_estimate=pl.CostEstimate(flops=0, bytes_accessed=6_000_000, transcendentals=0),
        name="step",
    )(*at, table, *arrived, pool, rows, store, refilled, attention)
    return out[0], out[1], out[2], list(out[3:])


def own_kernel(plan, table, pool, token, refilled, store, window, in_sem, out_sem):
    moves = [
        (plan.kept(table, k), [plan.kept(table, k), plan.own_taker(table, k)]) for k in range(KEEP)
    ]
    for k, (source, _) in enumerate(moves):

        @pl.when(source >= 0)
        def _():
            @pl.loop(0, NPAGE, unroll=8)
            def _(p):
                pltpu.make_async_copy(
                    pool.at[plan.page(table, source, p)], window.at[k, p], in_sem.at[k]
                ).start()

    for k, (source, targets) in enumerate(moves):

        @pl.when(source >= 0)
        def _():
            pltpu.make_async_copy(window.at[k], window.at[k], in_sem.at[k]).wait()

        for lane, to in enumerate(targets):

            @pl.when((source >= 0) & (to >= 0))
            def _():
                @pl.loop(0, NPAGE, unroll=8)
                def _(p):
                    pltpu.make_async_copy(
                        window.at[k, p], refilled.at[plan.page(table, to, p)], out_sem.at[k, lane]
                    ).start()

    for k, (source, targets) in enumerate(moves):
        for lane, to in enumerate(targets):

            @pl.when((source >= 0) & (to >= 0))
            def _():
                pltpu.make_async_copy(window.at[k], window.at[k], out_sem.at[k, lane]).wait()


def own_windows(plan, table, pool, token):
    return pl.pallas_call(
        functools.partial(own_kernel, plan),
        out_shape=[
            jax.ShapeDtypeStruct(pool.shape, pool.dtype),
            jax.ShapeDtypeStruct((NZ * KEEP, NPAGE) + pool.shape[1:], pool.dtype),
        ],
        in_specs=[SMEM, HBM, ANY],
        out_specs=[HBM] * 2,
        scratch_shapes=[
            pltpu.VMEM((KEEP, NPAGE) + pool.shape[1:], pool.dtype),
            pltpu.SemaphoreType.DMA((KEEP,)),
            pltpu.SemaphoreType.DMA((KEEP, 2)),
        ],
        compiler_params=pltpu.CompilerParams(vmem_limit_bytes=ROOM),
        cost_estimate=pl.CostEstimate(flops=0, bytes_accessed=9_000_000, transcendentals=0),
        name="own_windows",
    )(table, pool, token)


def attend_to(branch, windows, row, result, row_sem, out, out_sem):
    count = len(branch)
    for i in range(count):

        @pl.when(branch[i] >= 0)
        def _():
            pltpu.make_async_copy(row.at[i], row.at[i], row_sem.at[i]).wait()

    @pl.when(functools.reduce(jnp.maximum, branch) >= 0)
    def _():
        kv = windows[0].shape[2]
        tokens = NPAGE * PAGE * kv
        flat = [
            window[:, :, 0, :].reshape(tokens, 2 * HD) if kv == 1 else window.reshape(tokens, 2 * HD)
            for window in windows
        ]
        query = [row[i, 0] for i in range(count)]
        scores = [
            lax.dot_general(
                query[i], flat[i][:, :HD], (((1,), (1,)), ((), ())), preferred_element_type=jnp.float32
            )
            for i in range(count)
        ]
        token = lax.broadcasted_iota(jnp.int32, scores[0].shape, 1)
        head = lax.broadcasted_iota(jnp.int32, scores[0].shape, 0)
        fits = (token & (kv - 1)) == lax.div(head, H // KVH)
        for i in range(count):
            masked = jnp.where(fits, scores[i], -jnp.inf)
            own = jnp.sum(
                query[i].astype(jnp.float32) * row[i, 1].astype(jnp.float32), -1, keepdims=True
            )
            peak = jnp.maximum(jnp.max(masked, -1, keepdims=True), own)
            terms = jnp.exp(masked - peak)
            own_term = jnp.exp(own - peak)
            total = jnp.sum(terms, -1, keepdims=True) + own_term
            weights = (terms / total).astype(jnp.bfloat16)
            own_weight = (own_term / total).astype(jnp.bfloat16).astype(jnp.float32)
            mixed = jnp.dot(weights, flat[i][:, HD:], preferred_element_type=jnp.float32)
            mixed = mixed + own_weight * row[i, 2].astype(jnp.float32)
            result[i] = mixed.astype(result.dtype)

    for i in range(count):

        @pl.when(branch[i] >= 0)
        def _():
            pltpu.make_async_copy(result.at[i], out.at[branch[i]], out_sem.at[i]).start()

    for i in range(count):

        @pl.when(branch[i] >= 0)
        def _():
            pltpu.make_async_copy(result.at[i], result.at[i], out_sem.at[i]).wait()


def attend_kernel(plan, whom, traced, *refs):
    if traced:
        at, refs = refs[0][0], refs[1:]
        whom = [(at, l) for _, l in whom]
    table, rows, refilled = refs[:3]
    out, window, row, result, sem, row_sem, out_sem = refs[-7:]
    own = [plan.own_taker(table, k) for k in range(KEEP)]
    takers = []
    for _ in range(CAP):
        taker = functools.reduce(jnp.maximum, own)
        own = [jnp.where(other == taker, -1, other) for other in own]
        takers.append(taker)
    branch = []
    for r, i in whom:
        if r is None:
            branch.append(plan.kept(table, i) if i < KEEP else takers[i - KEEP])
        else:
            branch.append(plan.taker(table, r, i))
    for i, who in enumerate(branch):

        @pl.when(who >= 0)
        def _():
            pltpu.make_async_copy(rows.at[who], row.at[i], row_sem.at[i]).start()

            @pl.loop(0, NPAGE, unroll=8)
            def _(p):
                pltpu.make_async_copy(
                    refilled.at[plan.page(table, who, p)], window.at[i, p], sem.at[i]
                ).start()

    for i, who in enumerate(branch):

        @pl.when(who >= 0)
        def _():
            pltpu.make_async_copy(window.at[i], window.at[i], sem.at[i]).wait()

    attend_to(
        branch, [window.at[i] for i in range(len(branch))], row, result, row_sem, out, out_sem
    )


def attend(plan, whom, at, table, rows, refilled, before):
    at = [] if at is None else [jnp.stack([at])]
    count = len(whom)
    heads = rows.shape[2]
    lead = len(at)
    return pl.pallas_call(
        functools.partial(attend_kernel, plan, whom, bool(at)),
        out_shape=jax.ShapeDtypeStruct((rows.shape[0], heads, HD), jnp.bfloat16),
        in_specs=[SMEM] * (lead + 1) + [ANY, HBM] + [ANY] * len(before),
        out_specs=ANY,
        scratch_shapes=[
            pltpu.VMEM((count, NPAGE) + refilled.shape[1:], refilled.dtype),
            pltpu.VMEM((count, 3, heads, HD), rows.dtype),
            pltpu.VMEM((count, heads, HD), jnp.bfloat16),
            pltpu.SemaphoreType.DMA((count,)),
            pltpu.SemaphoreType.DMA((count,)),
            pltpu.SemaphoreType.DMA((count,)),
        ],
        input_output_aliases={lead + 3: 0} if before else {},
        compiler_params=pltpu.CompilerParams(vmem_limit_bytes=ROOM),
        cost_estimate=pl.CostEstimate(
            flops=count * 2 * 2 * 16 * 1536 * 128, bytes_accessed=count * 800_000, transcendentals=0
        ),
        name="attend",
    )(*at, table, rows, refilled, *before)


def token_rows(hidden, w_query, w_key, w_value, query_gain, key_gain):
    features = lax.all_gather(hidden, "mp", axis=1, tiled=True)
    branch_count = features.shape[0]
    head_group = H // KVH
    heads = w_query.shape[1] // HD
    kv_local = w_key.shape[1] // HD
    query_full = jnp.dot(features, w_query, preferred_element_type=jnp.float32)
    query_full = query_full.reshape(branch_count, heads, HD)
    query_rows = (normalize(query_full, query_gain) / math.sqrt(HD)).astype(jnp.bfloat16)
    key_full = jnp.dot(features, w_key, preferred_element_type=jnp.float32)
    key_rows = normalize(key_full.reshape(branch_count, kv_local, HD), key_gain).astype(jnp.bfloat16)
    value_rows = jnp.dot(features, w_value, preferred_element_type=jnp.float32)
    value_rows = value_rows.reshape(branch_count, kv_local, HD).astype(jnp.bfloat16)
    return jnp.stack(
        [
            query_rows,
            jnp.repeat(key_rows, head_group, axis=1),
            jnp.repeat(value_rows, head_group, axis=1),
        ],
        axis=1,
    )


def shards(
    hidden, w_query, w_key, w_value, query_gain, key_gain, kv_pool, page_table, parent, surviving
):
    groups = lax.axis_size("dp")
    me = lax.axis_index("dp")
    ny = groups // NZ
    branch_count = hidden.shape[0]
    links = 2 + ny - 1
    facts = jnp.concatenate(
        [page_table.T, parent[None], surviving[None], jnp.zeros((6, parent.shape[0]), jnp.int32)]
    )
    packed = first_windows(groups, branch_count, facts, kv_pool)
    parent, surviving, page_table, packed = lax.optimization_barrier(
        (parent, surviving, page_table, packed)
    )
    sides = lax.axis_size("mp")

    def everywhere(move):
        return [
            (g * sides + m, to[0] * sides + to[1])
            for g in range(groups)
            for m in range(sides)
            for to in [move(g, m)]
        ]

    def outer(g, m):
        return g + ny if g // ny % 2 == 0 else g - ny, m

    def inner(g, m):
        if g // ny in (0, NZ - 1):
            return g, m ^ 1
        return g + ny if g // ny % 2 else g - ny, m

    def sideways(shift):
        return lambda g, m: (g // ny * ny + (g % ny + shift) % ny, m)

    pairs = [everywhere(outer), everywhere(inner)]
    pairs += [everywhere(sideways(shift)) for shift in range(1, ny)]
    along, beside, every = [0, 1], list(range(2, links)), list(range(links))

    def travel(packed, which):
        return [lax.ppermute(window, ("dp", "mp"), pairs[l]) for window, l in zip(packed, which)]

    arrived = travel(packed, every)
    plan = Plan(links, groups, branch_count)
    table = routing(parent, surviving, page_table, groups, branch_count, links)
    rounds = table[plan.rounds_at]
    refilled, store = own_windows(plan, table, kv_pool, packed[0])
    rows = token_rows(hidden, w_query, w_key, w_value, query_gain, key_gain)
    waiting = [[(None, i) for i in range(3)], [(None, i) for i in range(3, KEEP + CAP)]]
    waiting += [[(r, l) for l in every] for r in range(FIRST)]

    def attend_next(attention):
        return attend(plan, waiting.pop(0), None, table, rows, refilled, attention)

    attention = attend_next([])
    files = [(r, l, 0, NPAGE, l, r * NPAGE) for r in range(FIRST) for l in every]
    store, refilled, attention, packed = step(
        plan,
        [(FIRST, 0, NPAGE, every)],
        [file for file in files if file[1] in along],
        None,
        table,
        arrived[:2],
        kv_pool,
        rows,
        store,
        refilled,
        attention,
        filing=False,
    )
    moved = travel(packed, every)
    for r in range(FIRST, PREFIX):
        if r > FIRST:
            files = [(r - 1, l, 0, NPAGE, l, 0) for l in along]
            files += [(r - 2, l, 0, NPAGE, l, 0) for l in beside if came_beside]
            arrived = came_along + came_beside
        packs = [(r, 0, NPAGE, beside)] if r > FIRST else []
        more_packs = [(r + 1, 0, NPAGE, along)] if r + 1 < PREFIX else []
        ahead = r in (FIRST + 1, PREFIX - 1)
        store, refilled, attention, packed = step(
            plan,
            packs if ahead else packs + more_packs,
            files,
            None,
            table,
            arrived,
            kv_pool,
            rows,
            store,
            refilled,
            attention,
            filing=not ahead,
        )
        if r == FIRST + 1:
            files = files + [(r - 1, l, 0, NPAGE, l, 0) for l in beside]
            arrived, moving_beside = arrived + moving_beside, []
        if ahead:
            store, refilled, attention, more_packed = step(
                plan, more_packs, files, None, table, arrived, kv_pool, rows, store, refilled, attention
            )
            packed = packed + more_packed
        if r > FIRST:
            came_along, came_beside = moving_along, moving_beside
            moving_beside = travel(packed[: len(beside)], beside)
            packed = packed[len(beside) :]
            waiting.append([(at, l) for at, l, _, _, _, _ in files])
        else:
            came_along, came_beside, moving_beside = moved[:2], [], moved[2:]
        if packed:
            if came_beside:
                packed, came_beside = lax.optimization_barrier((packed, came_beside))
            moving_along = travel(packed, along)
        for _ in range(2 if len(waiting) > 1 else 1):
            attention = attend_next([attention])
    while waiting:
        attention = attend_next([attention])
    last = PREFIX - 1
    endings = [(last - 1, beside, came_beside), (last, along, came_along), (last, beside, moving_beside)]
    for r, which, arrived in endings:
        files = [(r, l, 0, NPAGE, i, 0) for i, l in enumerate(which)]
        store, refilled, attention, _ = step(
            plan, [], files, None, table, arrived, kv_pool, rows, store, refilled, attention, attending=True
        )

    def more(state):
        return state[0] < rounds

    def one_round(state):
        r, store, refilled, attention = state
        part = NPAGE // PIECES
        moving = []
        for piece in range(PIECES):
            store, refilled, attention, packed = step(
                plan, [(None, piece * part, part, every)], [], r, table, [], kv_pool, rows, store, refilled, attention
            )
            moving.append(travel(packed, every))
        for piece in range(PIECES):
            files = [(None, l, piece * part, part, l, 0) for l in every]
            store, refilled, attention, _ = step(
                plan, [], files, r, table, moving.pop(0), kv_pool, rows, store, refilled, attention
            )
        attention = attend(plan, [(r, l) for l in every], r, table, rows, refilled, [attention])
        return r + 1, store, refilled, attention

    _, store, refilled, attention = lax.while_loop(
        more, one_round, (jnp.int32(PREFIX), store, refilled, attention)
    )
    return (refilled, attention.reshape(branch_count, -1))


def solution(mesh):
    return jax.shard_map(
        shards,
        mesh=mesh,
        in_specs=(
            P("dp", "mp"),
            P(None, "mp"),
            P(None, "mp"),
            P(None, "mp"),
            P(),
            P(),
            P("dp", None, "mp", None),
            P(),
            P(),
            P(),
        ),
        out_specs=(P("dp", None, "mp", None), P("dp", "mp")),
        check_vma=False,
    )
```
